32 devices in a mesh: ctx: 8 (over y, x, core), head: 4 (over z).
Axes of the slice: x: 2, y: 2, z: 4, core: 2. Of those that a mesh axis runs over, the one named last changes fastest.
Arguments:
- packets: float32 [2048, 1024], P('ctx', 'head')
- baseline: float32 [2048, 1024], P('ctx', 'head'), may hold values from -3 to 3
- w_query: float32 [1024, 1024], P('head'), may hold values from -0.1875 to 0.1875
- w_key: float32 [1024, 1024], P('head'), may hold values from -0.1875 to 0.1875
- w_value: float32 [1024, 1024], P('head'), may hold values from -0.1875 to 0.1875
- w_out: float32 [1024, 1024], P('head'), may hold values from -0.1875 to 0.1875
- gain: float32 [1024], P('head'), may hold values from 0.1 to 1.9
- probe: float32 [2048, 1024], P('ctx', 'head'), may hold values from -6 to 6
- sessions: int32 [2048], replicated, may hold values from 0 to 3, never falling along the last dimension, each value on 1 to 1024 neighbouring positions
- block_lists: int32 [16, 5], P('ctx'), may hold values from 0 to 15, as said below
Outputs:
- attributions: float32 [2048, 1024], P('ctx', 'head')
The draws below stay inside these ranges and needn't reach their ends.
Inputs may be any that keep to these rules, and one draw needn't show every extreme that they name: `block_lists`: row b lists 5 different blocks, b itself first, all within 4 blocks of b.
All inputs are finite; a program needn't handle non-finite values.
Results may differ from the reference program's by a relative error of at most 0.0003.
Values sent between devices are 32-bit elements; how exact they have to be, the bound alone decides.
No kernel may reach another device: no remote copies, remote signals or barrier semaphores. Data moves between devices by JAX's collectives and lax.ppermute only.
A program may use at most 128 MiB of HBM per device.

```python
import math
import jax
import jax.numpy as jnp
import numpy as np
from jax import lax

D = 1024
HEADS = 16
BLK = 128
KVB = 5
REACH = 2
TOK_CTX = 256
TOKENS = 2048
NB = 16


def draw_packets(key, part):
    base = jax.random.normal(key, (TOKENS, D), jnp.float32)
    return jnp.clip(base, -6.0, 6.0)


def draw_block_lists(key, part):
    span = REACH * (TOK_CTX // BLK)
    offsets = jnp.concatenate([jnp.arange(-span, 0), jnp.arange(1, span + 1)]).astype(jnp.int32)
    rows = jnp.arange(NB, dtype=jnp.int32)

    def pick(row_key, row):
        order = jax.random.permutation(row_key, 2 * span).astype(jnp.int32)
        target = row + offsets
        valid = (target >= 0) & (target < NB)
        score = order + jnp.where(valid, 4 * span, 0).astype(jnp.int32)
        chosen = lax.top_k(score, KVB - 1)[1]
        return jnp.concatenate([row[None], target[chosen]]).astype(jnp.int32)
    row_keys = jax.random.split(key, NB)
    return jax.vmap(pick)(row_keys, rows)


def shard_levels(key, shape, shards, smallest, high):
    loudness = 1.0
    for axis_at, shards_of in shards:
        heights = jax.random.uniform(jax.random.fold_in(jax.random.fold_in(key, 6), axis_at), (shards_of,), jnp.float32, smallest / len(shards), high / len(shards))
        loudness = loudness * jnp.repeat(jnp.exp(heights), shape[axis_at] // shards_of).reshape((-1,) + (1,) * (len(shape) - 1 - axis_at))
    return loudness


def length_profile(number_of, total, bound, lean):
    portions = [(1 << 20) // math.isqrt(standing ** lean) + 1 for standing in range(2, number_of + 1)]
    spare, given = total - bound - (number_of - 1), [1] * (number_of - 1)
    while spare > 0:
        candidates = [i for i in range(number_of - 1) if given[i] < bound]
        mass, left = sum([portions[i] for i in candidates]), spare
        for i in candidates:
            extra = min(bound - given[i], max(1, left * portions[i] // mass), spare)
            given[i] = given[i] + extra
            spare = spare - extra
    return np.array([bound] + given)


def ragged(own_key, number_of, total, most, lean):
    if number_of == 2:
        one = jax.random.randint(own_key, (), max(1, total - most), min(most, total - 1) + 1)
        return jnp.stack([one, total - one])
    tallies = jnp.asarray(length_profile(number_of, total, most, lean), jnp.int32)
    pairs = (number_of - 1) // 2
    source_of, receiver = tallies[1:1 + 2 * pairs:2], tallies[2:2 + 2 * pairs:2]
    margin = jnp.minimum(source_of - 1, most - receiver)
    shifted = jax.random.randint(jax.random.fold_in(own_key, 1), (pairs,), 0, 1 << 20) % (margin + 1)
    tallies = tallies.at[1:1 + 2 * pairs:2].set(source_of - shifted).at[2:2 + 2 * pairs:2].set(receiver + shifted)
    return tallies[jax.random.permutation(jax.random.fold_in(own_key, 2), number_of)]


def scatter_about(own_key, extent, spread, limit, cuts=(), kind=jnp.bfloat16):
    drawn = spread * jax.random.normal(own_key, extent, jnp.float32)
    if cuts:
        drawn = drawn * shard_levels(own_key, extent, cuts, -0.22, 0.18)
    return jnp.clip(drawn, -limit, limit).astype(kind)


def setup_inputs(seed: int = 0) -> dict:
    splits = jax.random.split(jax.random.key(seed), 11)
    packets = draw_packets(jax.random.fold_in(splits[10], 71), 0)
    baseline = scatter_about(splits[1], (TOKENS, D), 0.5, 3.0, ((0, 8), (1, 4)), jnp.float32)
    w_query = scatter_about(splits[2], (D, D), D ** -0.5, 0.1875, ((0, 4),), jnp.float32)
    w_key = scatter_about(splits[3], (D, D), D ** -0.5, 0.1875, ((0, 4),), jnp.float32)
    w_value = scatter_about(splits[4], (D, D), D ** -0.5, 0.1875, ((0, 4),), jnp.float32)
    w_out = scatter_about(splits[5], (D, D), D ** -0.5, 0.1875, ((0, 4),), jnp.float32)
    gain = jnp.clip(1.0 + 0.18 * jax.random.normal(splits[6], (D,), jnp.float32), 0.1, 1.9)
    probe = scatter_about(splits[7], (TOKENS, D), 1.0, 6.0, ((0, 8), (1, 4)), jnp.float32)
    sessions = jnp.searchsorted(jnp.cumsum(ragged(splits[8], TOKENS // (4 * BLK), TOKENS, 8 * BLK, 0)), jnp.arange(TOKENS), side="right").astype(jnp.int32)
    block_lists = draw_block_lists(jax.random.fold_in(splits[10], 71), 0)
    return dict(packets=packets, baseline=baseline, w_query=w_query, w_key=w_key, w_value=w_value, w_out=w_out, gain=gain, probe=probe, sessions=sessions, block_lists=block_lists)


ALPHAS = (0.25, 0.75)
EPS = 1e-05
HIGHEST = lax.Precision.HIGHEST

def layer_target(point, w_query, w_key, w_value, w_out, gain, probe, sessions, block_lists):
    head_dim = D // HEADS
    scale = 1.0 / math.sqrt(head_dim)
    query = jnp.dot(point, w_query.T, precision=HIGHEST)
    keys = jnp.dot(point, w_key.T, precision=HIGHEST)
    values = jnp.dot(point, w_value.T, precision=HIGHEST)
    query_blocks = query.reshape(NB, BLK, HEADS, head_dim)
    key_blocks = keys.reshape(NB, BLK, HEADS, head_dim)
    value_blocks = values.reshape(NB, BLK, HEADS, head_dim)
    session_blocks = sessions.reshape(NB, BLK)

    def one_block(args):
        query_block, query_sessions, listed = args
        picked_keys = key_blocks[listed].reshape(KVB * BLK, HEADS, head_dim)
        picked_values = value_blocks[listed].reshape(KVB * BLK, HEADS, head_dim)
        key_sessions = session_blocks[listed].reshape(KVB * BLK)
        scores = jnp.einsum('qhd,khd->hqk', query_block, picked_keys, precision=HIGHEST) * scale
        keep = query_sessions[:, None] == key_sessions[None, :]
        scores = jnp.where(keep[None], scores, -1e+30)
        top = lax.optimization_barrier(jnp.max(scores, axis=-1, keepdims=True))
        expo = jnp.exp(scores - top)
        probs = expo / lax.optimization_barrier(jnp.sum(expo, axis=-1, keepdims=True))
        return jnp.einsum('hqk,khd->qhd', probs, picked_values, precision=HIGHEST)
    mixed = lax.map(one_block, (query_blocks, session_blocks, block_lists)).reshape(TOKENS, D)
    summed = point + jnp.dot(mixed, w_out.T, precision=HIGHEST)
    mean = lax.optimization_barrier(jnp.mean(summed, axis=-1, keepdims=True))
    var = lax.optimization_barrier(jnp.mean(summed * summed, axis=-1, keepdims=True)) - mean * mean
    normed = (summed - mean) * lax.rsqrt(var + EPS)
    return jnp.sum(probe * gain * normed)

def reference(packets, baseline, w_query, w_key, w_value, w_out, gain, probe, sessions, block_lists):
    travel = packets - baseline
    total = jnp.zeros_like(packets)
    for alpha in ALPHAS:
        total = total + jax.grad(layer_target)(baseline + alpha * travel, w_query, w_key, w_value, w_out, gain, probe, sessions, block_lists)
    return travel * total / len(ALPHAS)
```

```python
import math

import jax
import jax.numpy as jnp
from jax import lax
from jax.experimental import pallas as pl
from jax.experimental.pallas import tpu as pltpu
from jax.sharding import PartitionSpec as P

HEADS = 16
BLK = 128
KVB = 5
REACH = 2


ALPHAS = (0.25, 0.75)
EPS = 1e-05
HIGHEST = lax.Precision.HIGHEST


def from_behind(x, axis, by):
    size = lax.axis_size(axis)
    pairs = [(i, i + by) for i in range(size) if 0 <= i + by < size]
    return lax.ppermute(x, axis, pairs)


def integrate(points, weights_qkv, w_out, gain, probe, sessions, block_lists):
    steps, rows, feats = points.shape
    width = weights_qkv.shape[1]
    head_dim = width // HEADS
    local_heads = feats // head_dim
    blocks = rows // BLK
    where = lax.axis_index("ctx")
    first = (where - REACH) * blocks
    slots = (2 * REACH + 1) * blocks
    scale = 1.0 / math.sqrt(head_dim)
    part_cols = weights_qkv
    qkv = jnp.einsum(
        "std,ed->ste",
        lax.all_gather(points, "head", axis=2, tiled=True),
        part_cols,
        precision=HIGHEST,
    )
    query = qkv[:, :, :feats]
    pairs = qkv[:, :, feats:]
    below = []
    above = []
    for dist in range(1, REACH + 1):
        below.append(from_behind(pairs, "ctx", dist))
        above.append(from_behind(pairs, "ctx", -dist))
    window = jnp.concatenate(below[::-1] + [pairs] + above, axis=1)
    local = (block_lists - first).reshape(-1)
    tiles = window.reshape(steps, slots, BLK, 2 * feats)
    picked = jnp.take(tiles, local, axis=1).reshape(
        steps, blocks, KVB * BLK, 2, local_heads, head_dim
    )
    keys = picked[:, :, :, 0]
    values = picked[:, :, :, 1]
    token_index = block_lists[:, :, None] * BLK + jnp.arange(BLK, dtype=jnp.int32)[None, None, :]
    key_sessions = jnp.take(sessions, token_index.reshape(blocks, KVB * BLK), axis=0)
    query_sessions = lax.dynamic_slice_in_dim(sessions, where * rows, rows, 0).reshape(blocks, BLK)
    keep = query_sessions[:, :, None] == key_sessions[:, None, :]
    query_heads = query.reshape(steps, blocks, BLK, local_heads, head_dim)
    scores = jnp.einsum("sbqhd,sbkhd->sbhqk", query_heads, keys, precision=HIGHEST) * scale
    scores = jnp.where(keep[None, :, None], scores, -1e30)
    top = jnp.max(scores, axis=-1, keepdims=True)
    expo = jnp.exp(scores - top)
    probs = expo / jnp.sum(expo, axis=-1, keepdims=True)
    mixed = jnp.einsum("sbhqk,sbkhd->sbqhd", probs, values, precision=HIGHEST)
    heads_out = mixed.reshape(steps, rows, feats)
    part_cols = w_out
    projected = jnp.einsum(
        "std,ed->ste",
        lax.all_gather(heads_out, "head", axis=2, tiled=True),
        part_cols,
        precision=HIGHEST,
    )
    summed = points + projected
    first_sum, second_sum = lax.psum(
        (jnp.sum(summed, axis=-1), jnp.sum(summed * summed, axis=-1)), "head"
    )
    mean = first_sum / width
    inverse = lax.rsqrt(second_sum / width - mean * mean + EPS)
    normed = (summed - mean[..., None]) * inverse[..., None]
    upstream = probe * gain
    upstream_sum, upstream_dot = lax.psum(
        (jnp.sum(upstream, axis=-1), jnp.sum(upstream * normed, axis=-1)), "head"
    )
    direct = inverse[..., None] * (
        upstream - upstream_sum[..., None] / width - normed * (upstream_dot / width)[..., None]
    )
    partial_heads = jnp.einsum("ste,ed->std", direct, w_out, precision=HIGHEST)
    grad_heads = lax.psum_scatter(partial_heads, "head", scatter_dimension=2, tiled=True)
    grad_mixed = grad_heads.reshape(steps, blocks, BLK, local_heads, head_dim)
    delta = jnp.einsum("sbqhd,sbqhd->sbhq", grad_mixed, mixed, precision=HIGHEST)
    grad_probs = jnp.einsum("sbqhd,sbkhd->sbhqk", grad_mixed, values, precision=HIGHEST)
    grad_scores = probs * (grad_probs - delta[..., None]) * scale
    grad_query = jnp.einsum("sbhqk,sbkhd->sbqhd", grad_scores, keys, precision=HIGHEST)
    grad_keys = jnp.einsum("sbhqk,sbqhd->sbkhd", grad_scores, query_heads, precision=HIGHEST)
    grad_values = jnp.einsum("sbhqk,sbqhd->sbkhd", probs, grad_mixed, precision=HIGHEST)
    grad_picked = jnp.stack([grad_keys, grad_values], axis=3).reshape(
        steps, blocks * KVB, BLK, 2 * feats
    )
    selector = (local[:, None] == jnp.arange(slots, dtype=jnp.int32)[None, :]).astype(jnp.float32)
    grad_window = jnp.einsum("snlc,nw->swlc", grad_picked, selector, precision=HIGHEST).reshape(
        steps, slots * BLK, 2 * feats
    )
    owned = grad_window[:, REACH * rows : (REACH + 1) * rows]
    for dist in range(1, REACH + 1):
        upper = grad_window[:, (REACH + dist) * rows : (REACH + dist + 1) * rows]
        lower = grad_window[:, (REACH - dist) * rows : (REACH - dist + 1) * rows]
        owned = owned + from_behind(upper, "ctx", dist)
        owned = owned + from_behind(lower, "ctx", -dist)
    grad_qkv = jnp.concatenate([grad_query.reshape(steps, rows, feats), owned], axis=-1)
    partial_input = jnp.einsum("ste,ed->std", grad_qkv, weights_qkv, precision=HIGHEST)
    return (direct, partial_input)


def collect_inputs(partial_input):
    return lax.psum_scatter(partial_input, "head", scatter_dimension=2, tiled=True)


def general_shards(packets, baseline, w_query, w_key, w_value, w_out, gain, probe, sessions, block_lists):
    weights_qkv = jnp.concatenate([w_query, w_key, w_value], axis=0)
    travel = packets - baseline
    points = jnp.stack([baseline + alpha * travel for alpha in ALPHAS])
    passes = [
        integrate(points[index : index + 1], weights_qkv, w_out, gain, probe, sessions, block_lists)
        for index in range(len(ALPHAS))
    ]
    grads = jnp.zeros_like(packets)
    for direct, partial_input in passes:
        grads = grads + direct.sum(axis=0) + collect_inputs(partial_input).sum(axis=0)
    return travel * grads / len(ALPHAS)


F32 = jnp.float32
BF16 = jnp.bfloat16
LIMIT = 48 * 1024 * 1024
VM = pl.BlockSpec(memory_space=pltpu.VMEM)
SM = pl.BlockSpec(memory_space=pltpu.SMEM)


def halves(x):
    high = x.astype(BF16)
    low = (x - high.astype(F32)).astype(BF16)
    return high, low


def halves_outside(x):
    rounded = lax.reduce_precision(x, 8, 7)
    return rounded.astype(BF16), (x - rounded).astype(BF16)


def mm(a, b):
    return lax.dot_general(a, b, (((1,), (0,)), ((), ())), preferred_element_type=F32)


def mm_nt(a, b):
    return lax.dot_general(a, b, (((1,), (1,)), ((), ())), preferred_element_type=F32)


def call(kernel, outs, scratch, n_smem, *args):
    return pl.pallas_call(
        kernel,
        out_shape=outs,
        in_specs=[SM] * n_smem + [VM] * (len(args) - n_smem),
        out_specs=jax.tree.map(lambda _: VM, outs),
        scratch_shapes=scratch,
        compiler_params=pltpu.CompilerParams(vmem_limit_bytes=LIMIT),
    )(*args)


def shift(x, by, low, high):
    return lax.ppermute(x, "head", [(i, i + by) for i in range(low, high + 1)])


def rotate(x, by):
    size = lax.axis_size("head")
    return lax.ppermute(x, "head", [(i, (i + by) % size) for i in range(size)])


def exchange(pieces):
    return [pieces[0]] + [rotate(pieces[k], k) for k in range(1, len(pieces))]


def project_kernel(z_ref, w3, own0, own1, *rest):
    ups = [rest[0:2], rest[2:4], rest[4:6]]
    downs = [rest[6:8], rest[8:10], rest[10:12]]
    out, rows, x3 = rest[12:]
    z = z_ref[0]
    n = 4
    quarter = rows.shape[1]
    width = rows.shape[2]
    for s, own in enumerate((own0, own1)):
        tokens, feats = own.shape
        for k in range(n):
            column = lax.rem(z - k + n, n) * feats
            at = pl.ds(pl.multiple_of(z * quarter, quarter), quarter)
            if k == 0:
                x = own[...]
                mine = own[at, :]
            else:
                up, down = ups[k - 1][s], downs[n - k - 1][s]
                x = up[...] + down[...]
                mine = up[at, :] + down[at, :]
            rows[s, :, pl.ds(pl.multiple_of(column, feats), feats)] = mine
            high, low = halves(x)
            span = pl.ds(s * tokens, tokens)
            x3[span, pl.ds(pl.multiple_of(column, feats), feats)] = high
            x3[span, pl.ds(pl.multiple_of(width + column, feats), feats)] = high
            x3[span, pl.ds(pl.multiple_of(2 * width + column, feats), feats)] = low
    part = out.shape[1]
    for s in range(2):
        for h in range(n):
            out[2 * h + s] = mm_nt(
                w3[h * part : (h + 1) * part, :], x3[s * tokens : (s + 1) * tokens, :]
            )


def attend_kernel(lists, session_col, session_row, qkv, mixed, p_high, p_low, q3, k3, v2):
    for b in range(NBLOCKS):
        t = qkv[b // 2, :, (b % 2) * BLK : (b % 2 + 1) * BLK]
        q_high, q_low = halves(t[:HD] * SCALE)
        q3[b] = jnp.concatenate([q_high, q_high, q_low], axis=0)
        k_high, k_low = halves(t[HD : 2 * HD].T)
        k3[b] = jnp.concatenate([k_high, k_low, k_high], axis=1)
        v_high, v_low = halves(t[2 * HD :])
        v2[b] = jnp.concatenate([v_high, v_low], axis=0)

    def body(c, carry):
        for e in range(2):
            b = 2 * c + e
            query = q3[b]
            mine = session_row[pl.ds(b, 1), :]
            scores = []
            for j in range(KVB):
                other = lists[b, j]
                s = mm(k3[other], query)
                scores.append(jnp.where(session_col[other] == mine, s, -1e30))
            s = jnp.concatenate(scores, axis=0)
            top = jnp.max(s, axis=0, keepdims=True)
            expo = jnp.exp(s - top)
            probs = expo * (1.0 / jnp.sum(expo, axis=0, keepdims=True))
            high, low = halves(probs)
            p_high[b] = high
            p_low[b] = low
            values = jnp.concatenate([v2[lists[b, j]] for j in range(KVB)], axis=1)
            both = mm(values, high)
            mixed[c, :, e * BLK : (e + 1) * BLK] = both[:HD] + both[HD:] + mm(values[:HD], low)
        return carry

    lax.fori_loop(0, NBLOCKS // 2, body, 0)


def attend_back_kernel(lists, qkv, p_high, p_low, grad, mixed, out, q2, k2, v3, acc):
    for b in range(NBLOCKS):
        t = qkv[b // 2, :, (b % 2) * BLK : (b % 2 + 1) * BLK]
        q_high, q_low = halves(t[:HD])
        q2[b] = jnp.concatenate([q_high, q_low], axis=0)
        k_high, k_low = halves(t[HD : 2 * HD])
        k2[b] = jnp.concatenate([k_high, k_low], axis=0)
        v_high, v_low = halves(t[2 * HD :].T)
        v3[b] = jnp.concatenate([v_high, v_low, v_high], axis=1)
    acc[...] = jnp.zeros_like(acc)

    def body(c, carry):
        for e in range(2):
            b = 2 * c + e
            lanes = slice(e * BLK, (e + 1) * BLK)
            g = grad[c, :, lanes]
            delta = jnp.sum(g * mixed[c, :, lanes], axis=0, keepdims=True)
            g_high, g_low = halves(g)
            g3 = jnp.concatenate([g_high, g_high, g_low], axis=0)
            g2 = jnp.concatenate([g_high, g_low], axis=0)
            grad_probs = jnp.concatenate([mm(v3[lists[b, j]], g3) for j in range(KVB)], axis=0)
            ph, pw = p_high[b], p_low[b]
            probs = ph.astype(F32) + pw.astype(F32)
            s_high, s_low = halves(probs * (grad_probs - delta) * SCALE)
            keys = jnp.concatenate([k2[lists[b, j]] for j in range(KVB)], axis=1)
            both = mm(keys, s_high)
            out[c, 0:HD, lanes] = both[:HD] + both[HD:] + mm(keys[:HD], s_low)
            query = q2[b]
            both = mm_nt(query, s_high)
            grad_keys = both[:HD] + both[HD:] + mm_nt(query[:HD], s_low)
            both = mm_nt(g2, ph)
            grad_values = both[:HD] + both[HD:] + mm_nt(g2[:HD], pw)
            for j in range(KVB):
                at = slice(j * BLK, (j + 1) * BLK)
                acc[lists[b, j]] += jnp.concatenate([grad_keys[:, at], grad_values[:, at]], axis=0)
        return carry

    lax.fori_loop(0, NBLOCKS // 2, body, 0)
    for b in range(NBLOCKS):
        out[b // 2, HD : 3 * HD, (b % 2) * BLK : (b % 2 + 1) * BLK] = acc[b]


def to_tokens_kernel(z_ref, mixed, o0, o1, o2, o3, turned):
    z = z_ref[0]
    n = 4
    quarter = o0.shape[1]
    for s in range(2):
        turned[s] = jnp.concatenate([mixed[2 * h + s] for h in range(n)], axis=0).T
    for k, o in enumerate((o0, o1, o2, o3)):
        start = pl.multiple_of(lax.rem(z + k, n) * quarter, quarter)
        o[...] = turned[:, pl.ds(start, quarter), :]


def to_heads_kernel(z_ref, g0, g1, g2, g3, out, turned):
    z = z_ref[0]
    n = 4
    quarter = g0.shape[1]
    for k, g in enumerate((g0, g1, g2, g3)):
        start = pl.multiple_of(lax.rem(z - k + n, n) * quarter, quarter)
        turned[:, pl.ds(start, quarter), :] = g[...]
    for s in range(2):
        t = turned[s].T
        for h in range(n):
            out[2 * h + s] = t[h * HD : (h + 1) * HD]


def norm_kernel(
    z_ref, w_high, w_low, rows, u0, u1, u2, u3, m0, m1, m2, m3,
    g0, g1, g2, g3, direct_sum, mixed, upstream, grad,
):
    z = z_ref[0]
    n = 4
    quarter, width = rows.shape[1:]
    feats = width // n
    for k, (u, m) in enumerate(((u0, m0), (u1, m1), (u2, m2), (u3, m3))):
        at = pl.ds(pl.multiple_of(lax.rem(z - k + n, n) * feats, feats), feats)
        upstream[:, at] = u[...]
        for s in range(2):
            mixed[s * quarter : (s + 1) * quarter, at] = m[s]
    m_high, m_low = halves(mixed[...])
    projected = mm_nt(m_high, w_high[...]) + mm_nt(m_low, w_high[...]) + mm_nt(m_high, w_low[...])
    summed = rows[...].reshape(2 * quarter, width) + projected
    mean = jnp.sum(summed, axis=-1, keepdims=True) / width
    second = jnp.sum(summed * summed, axis=-1, keepdims=True) / width
    inverse = lax.rsqrt(second - mean * mean + EPS)
    normed = (summed - mean) * inverse
    up = jnp.concatenate([upstream[...], upstream[...]], axis=0)
    up_mean = jnp.sum(up, axis=-1, keepdims=True) / width
    up_dot = jnp.sum(up * normed, axis=-1, keepdims=True) / width
    direct = inverse * (up - up_mean - normed * up_dot)
    direct_sum[...] = direct[:quarter] + direct[quarter:]
    d_high, d_low = halves(direct)
    grad[...] = mm(d_high, w_high[...]) + mm(d_low, w_high[...]) + mm(d_high, w_low[...])
    for k, g in enumerate((g0, g1, g2, g3)):
        at = pl.ds(pl.multiple_of(lax.rem(z + k, n) * feats, feats), feats)
        for s in range(2):
            g[s] = grad[s * quarter : (s + 1) * quarter, at]


def input_kernel(z_ref, w3, grads, direct_sum, f0, f1, f2, f3):
    z = z_ref[0]
    n = 4
    quarter, width = direct_sum.shape
    feats = width // n
    g = jnp.concatenate([grads[2 * h] + grads[2 * h + 1] for h in range(n)], axis=0).T
    g_high, g_low = halves(g)
    mine = pl.ds(pl.multiple_of(z * quarter, quarter), quarter)
    for k, f in enumerate((f0, f1, f2, f3)):
        column = lax.rem(z + k, n) * feats
        at = pl.ds(pl.multiple_of(column, feats), feats)
        w_high = w3[:, at]
        w_low = w3[:, pl.ds(pl.multiple_of(width + column, feats), feats)]
        f[...] = mm(g_high, w_high) + mm(g_low, w_high) + mm(g_high, w_low)
        f[mine, :] += direct_sum[:, at]


HD = 64
NBLOCKS = 16
SCALE = 1.0 / math.sqrt(HD)


def shape(dims, kind=F32):
    return jax.ShapeDtypeStruct(dims, kind)


def shards(packets, baseline, w_query, w_key, w_value, w_out, gain, probe, sessions, block_lists):
    tokens, feats = packets.shape
    width = w_query.shape[1]
    n = lax.axis_size("head")
    heads = feats // HD
    members = lax.axis_size("ctx")
    quarter = tokens // n
    z = lax.axis_index("head")
    z_ref = z.reshape(1)
    slab = feats // members
    part = 3 * HD

    travel = packets - baseline
    own = [baseline + alpha * travel for alpha in ALPHAS]
    ups, downs = [own], [own]
    for step in range(1, n):
        ups.append([shift(x, 1, step - 1, n - 2) for x in ups[-1]])
        downs.append([shift(x, -1, 1, n - step) for x in downs[-1]])

    lists = lax.all_gather(block_lists, "ctx", axis=0, tiled=True)
    slab_rows = lax.dynamic_slice_in_dim(w_out, lax.axis_index("ctx") * slab, slab, 0)
    whole_out = lax.all_gather(slab_rows, ("head", "ctx"), axis=0, tiled=True)
    out_high, out_low = halves_outside(whole_out)
    weights = jnp.concatenate(
        [w.reshape(heads, HD, width) for w in (w_query, w_key, w_value)], axis=1
    ).reshape(heads * part, width)
    high, low = halves_outside(weights)
    w3 = jnp.concatenate([high, low, high], axis=1)

    upstream = probe * gain
    up_pieces = exchange(
        [
            lax.dynamic_slice_in_dim(upstream, lax.rem(z + k, n) * quarter, quarter, 0)
            for k in range(n)
        ]
    )

    received = [x for group in (ups[1:], downs[1:]) for pair in group for x in pair]
    qkv, rows = call(
        project_kernel,
        (shape((members, part, tokens)), shape((2, quarter, width))),
        [pltpu.VMEM((2 * tokens, 3 * width), BF16)],
        1, z_ref, w3, own[0], own[1], *received,
    )
    qkv = lax.all_to_all(qkv, "ctx", 0, 0, tiled=True)

    blocks = members * tokens // BLK
    session_row = sessions.reshape(blocks, BLK)
    session_col = sessions.reshape(blocks, BLK, 1)
    mixed, p_high, p_low = call(
        attend_kernel,
        (
            shape((members, HD, tokens)),
            shape((blocks, KVB * BLK, BLK), BF16),
            shape((blocks, KVB * BLK, BLK), BF16),
        ),
        [
            pltpu.VMEM((blocks, part, BLK), BF16),
            pltpu.VMEM((blocks, BLK, part), BF16),
            pltpu.VMEM((blocks, 2 * HD, BLK), BF16),
        ],
        1, lists, session_col, session_row, qkv,
    )
    arrived = lax.all_to_all(mixed, "ctx", 0, 0, tiled=True)
    pieces = call(
        to_tokens_kernel,
        (shape((2, quarter, feats)),) * n,
        [pltpu.VMEM((2, tokens, feats), F32)],
        1, z_ref, arrived,
    )
    pieces = exchange(pieces)
    *grads, direct_sum = call(
        norm_kernel,
        (shape((2, quarter, feats)),) * n + (shape((quarter, width)),),
        [
            pltpu.VMEM((2 * quarter, width), F32),
            pltpu.VMEM((quarter, width), F32),
            pltpu.VMEM((2 * quarter, width), F32),
        ],
        1, z_ref, out_high, out_low, rows, *up_pieces, *pieces,
    )
    grads = exchange(grads)
    grad = call(
        to_heads_kernel,
        shape((members, HD, tokens)),
        [pltpu.VMEM((2, tokens, feats), F32)],
        1, z_ref, *grads,
    )
    grad = lax.all_to_all(grad, "ctx", 0, 0, tiled=True)
    grad_qkv = call(
        attend_back_kernel,
        shape((members, part, tokens)),
        [
            pltpu.VMEM((blocks, 2 * HD, BLK), BF16),
            pltpu.VMEM((blocks, 2 * HD, BLK), BF16),
            pltpu.VMEM((blocks, BLK, part), BF16),
            pltpu.VMEM((blocks, 2 * HD, BLK), F32),
        ],
        1, lists, qkv, p_high, p_low, grad, mixed,
    )
    grad_qkv = lax.all_to_all(grad_qkv, "ctx", 0, 0, tiled=True)
    totals = exchange(
        call(
            input_kernel,
            (shape((tokens, feats)),) * n,
            [],
            1, z_ref, w3, grad_qkv, direct_sum,
        )
    )
    return travel * (totals[0] + totals[1] + totals[2] + totals[3]) / len(ALPHAS)


def pick_shards(mesh):
    members, n = mesh.shape["ctx"], mesh.shape["head"]
    return shards if n == 4 and members == 2 * HEADS // n else general_shards


def solution(mesh):
    return jax.shard_map(
        pick_shards(mesh),
        mesh=mesh,
        in_specs=(
            P("ctx", "head"),
            P("ctx", "head"),
            P("head", None),
            P("head", None),
            P("head", None),
            P("head", None),
            P("head"),
            P("ctx", "head"),
            P(),
            P("ctx", None),
        ),
        out_specs=P("ctx", "head"),
        check_vma=False,
    )
```

```python
import functools
import math

import jax
import jax.numpy as jnp
from jax import lax
from jax.experimental import pallas as pl
from jax.experimental.pallas import tpu as pltpu
from jax.sharding import PartitionSpec as P

HEADS = 16
BLK = 128
KVB = 5
REACH = 2


ALPHAS = (0.25, 0.75)
EPS = 1e-05
HIGHEST = lax.Precision.HIGHEST


def from_behind(x, axis, by):
    size = lax.axis_size(axis)
    pairs = [(i, i + by) for i in range(size) if 0 <= i + by < size]
    return lax.ppermute(x, axis, pairs)


def integrate(points, weights_qkv, w_out, gain, probe, sessions, block_lists):
    steps, rows, feats = points.shape
    width = weights_qkv.shape[1]
    head_dim = width // HEADS
    local_heads = feats // head_dim
    blocks = rows // BLK
    where = lax.axis_index("ctx")
    first = (where - REACH) * blocks
    slots = (2 * REACH + 1) * blocks
    scale = 1.0 / math.sqrt(head_dim)
    part_cols = weights_qkv
    qkv = jnp.einsum(
        "std,ed->ste",
        lax.all_gather(points, "head", axis=2, tiled=True),
        part_cols,
        precision=HIGHEST,
    )
    query = qkv[:, :, :feats]
    pairs = qkv[:, :, feats:]
    below = []
    above = []
    for dist in range(1, REACH + 1):
        below.append(from_behind(pairs, "ctx", dist))
        above.append(from_behind(pairs, "ctx", -dist))
    window = jnp.concatenate(below[::-1] + [pairs] + above, axis=1)
    local = (block_lists - first).reshape(-1)
    tiles = window.reshape(steps, slots, BLK, 2 * feats)
    picked = jnp.take(tiles, local, axis=1).reshape(
        steps, blocks, KVB * BLK, 2, local_heads, head_dim
    )
    keys = picked[:, :, :, 0]
    values = picked[:, :, :, 1]
    token_index = block_lists[:, :, None] * BLK + jnp.arange(BLK, dtype=jnp.int32)[None, None, :]
    key_sessions = jnp.take(sessions, token_index.reshape(blocks, KVB * BLK), axis=0)
    query_sessions = lax.dynamic_slice_in_dim(sessions, where * rows, rows, 0).reshape(blocks, BLK)
    keep = query_sessions[:, :, None] == key_sessions[:, None, :]
    query_heads = query.reshape(steps, blocks, BLK, local_heads, head_dim)
    scores = jnp.einsum("sbqhd,sbkhd->sbhqk", query_heads, keys, precision=HIGHEST) * scale
    scores = jnp.where(keep[None, :, None], scores, -1e30)
    top = jnp.max(scores, axis=-1, keepdims=True)
    expo = jnp.exp(scores - top)
    probs = expo / jnp.sum(expo, axis=-1, keepdims=True)
    mixed = jnp.einsum("sbhqk,sbkhd->sbqhd", probs, values, precision=HIGHEST)
    heads_out = mixed.reshape(steps, rows, feats)
    part_cols = w_out
    projected = jnp.einsum(
        "std,ed->ste",
        lax.all_gather(heads_out, "head", axis=2, tiled=True),
        part_cols,
        precision=HIGHEST,
    )
    summed = points + projected
    first_sum, second_sum = lax.psum(
        (jnp.sum(summed, axis=-1), jnp.sum(summed * summed, axis=-1)), "head"
    )
    mean = first_sum / width
    inverse = lax.rsqrt(second_sum / width - mean * mean + EPS)
    normed = (summed - mean[..., None]) * inverse[..., None]
    upstream = probe * gain
    upstream_sum, upstream_dot = lax.psum(
        (jnp.sum(upstream, axis=-1), jnp.sum(upstream * normed, axis=-1)), "head"
    )
    direct = inverse[..., None] * (
        upstream - upstream_sum[..., None] / width - normed * (upstream_dot / width)[..., None]
    )
    partial_heads = jnp.einsum("ste,ed->std", direct, w_out, precision=HIGHEST)
    grad_heads = lax.psum_scatter(partial_heads, "head", scatter_dimension=2, tiled=True)
    grad_mixed = grad_heads.reshape(steps, blocks, BLK, local_heads, head_dim)
    delta = jnp.einsum("sbqhd,sbqhd->sbhq", grad_mixed, mixed, precision=HIGHEST)
    grad_probs = jnp.einsum("sbqhd,sbkhd->sbhqk", grad_mixed, values, precision=HIGHEST)
    grad_scores = probs * (grad_probs - delta[..., None]) * scale
    grad_query = jnp.einsum("sbhqk,sbkhd->sbqhd", grad_scores, keys, precision=HIGHEST)
    grad_keys = jnp.einsum("sbhqk,sbqhd->sbkhd", grad_scores, query_heads, precision=HIGHEST)
    grad_values = jnp.einsum("sbhqk,sbqhd->sbkhd", probs, grad_mixed, precision=HIGHEST)
    grad_picked = jnp.stack([grad_keys, grad_values], axis=3).reshape(
        steps, blocks * KVB, BLK, 2 * feats
    )
    selector = (local[:, None] == jnp.arange(slots, dtype=jnp.int32)[None, :]).astype(jnp.float32)
    grad_window = jnp.einsum("snlc,nw->swlc", grad_picked, selector, precision=HIGHEST).reshape(
        steps, slots * BLK, 2 * feats
    )
    owned = grad_window[:, REACH * rows : (REACH + 1) * rows]
    for dist in range(1, REACH + 1):
        upper = grad_window[:, (REACH + dist) * rows : (REACH + dist + 1) * rows]
        lower = grad_window[:, (REACH - dist) * rows : (REACH - dist + 1) * rows]
        owned = owned + from_behind(upper, "ctx", dist)
        owned = owned + from_behind(lower, "ctx", -dist)
    grad_qkv = jnp.concatenate([grad_query.reshape(steps, rows, feats), owned], axis=-1)
    partial_input = jnp.einsum("ste,ed->std", grad_qkv, weights_qkv, precision=HIGHEST)
    return (direct, partial_input)


def collect_inputs(partial_input):
    return lax.psum_scatter(partial_input, "head", scatter_dimension=2, tiled=True)


def general_shards(packets, baseline, w_query, w_key, w_value, w_out, gain, probe, sessions, block_lists):
    weights_qkv = jnp.concatenate([w_query, w_key, w_value], axis=0)
    travel = packets - baseline
    points = jnp.stack([baseline + alpha * travel for alpha in ALPHAS])
    passes = [
        integrate(points[index : index + 1], weights_qkv, w_out, gain, probe, sessions, block_lists)
        for index in range(len(ALPHAS))
    ]
    grads = jnp.zeros_like(packets)
    for direct, partial_input in passes:
        grads = grads + direct.sum(axis=0) + collect_inputs(partial_input).sum(axis=0)
    return travel * grads / len(ALPHAS)


F32 = jnp.float32
BF16 = jnp.bfloat16
LIMIT = 48 * 1024 * 1024
VM = pl.BlockSpec(memory_space=pltpu.VMEM)
SM = pl.BlockSpec(memory_space=pltpu.SMEM)


def halves(x):
    high = x.astype(BF16)
    low = (x - high.astype(F32)).astype(BF16)
    return high, low


def halves_outside(x):
    rounded = lax.reduce_precision(x, 8, 7)
    return rounded.astype(BF16), (x - rounded).astype(BF16)


def mm(a, b):
    return lax.dot_general(a, b, (((1,), (0,)), ((), ())), preferred_element_type=F32)


def mm_nt(a, b):
    return lax.dot_general(a, b, (((1,), (1,)), ((), ())), preferred_element_type=F32)


def call(kernel, outs, scratch, n_smem, *args):
    return pl.pallas_call(
        kernel,
        out_shape=outs,
        in_specs=[SM] * n_smem + [VM] * (len(args) - n_smem),
        out_specs=jax.tree.map(lambda _: VM, outs),
        scratch_shapes=scratch,
        compiler_params=pltpu.CompilerParams(vmem_limit_bytes=LIMIT),
    )(*args)


def shift(x, by, low, high):
    return lax.ppermute(x, "head", [(i, i + by) for i in range(low, high + 1)])


def rotate(x, by):
    size = lax.axis_size("head")
    return lax.ppermute(x, "head", [(i, (i + by) % size) for i in range(size)])


def exchange(pieces):
    return [pieces[0]] + [rotate(pieces[k], k) for k in range(1, len(pieces))]


def project_kernel(z_ref, w3, own, u1, u2, u3, d1, d2, d3, out, rows, x3):
    ups, downs = (u1, u2, u3), (d1, d2, d3)
    z = z_ref[0]
    n = 4
    quarter, width = rows.shape[1:]
    both, feats = own.shape
    tokens = both // 2
    for k in range(n):
        column = pl.multiple_of(lax.rem(z - k + n, n) * feats, feats)
        x = own[...] if k == 0 else ups[k - 1][...] + downs[n - k - 1][...]
        for s in range(2):
            t = x[s * tokens : (s + 1) * tokens]
            rows[s, :, pl.ds(column, feats)] = jnp.where(
                lax.rem(z, 2) == 0, t[:quarter], t[quarter:]
            )
        high, low = halves(x)
        x3[:, pl.ds(column, feats)] = high
        x3[:, pl.ds(pl.multiple_of(width + column, feats), feats)] = high
        x3[:, pl.ds(pl.multiple_of(2 * width + column, feats), feats)] = low
    part = out.shape[1]
    for h in range(n):
        r = mm_nt(w3[h * part : (h + 1) * part, :], x3[...])
        for s in range(2):
            out[2 * h + s] = r[:, s * tokens : (s + 1) * tokens]


def fold(x):
    top, bottom = x[: HD // 2], x[HD // 2 :]
    left = lax.broadcasted_iota(jnp.int32, top.shape, 1) < HD
    return jnp.where(left, top, pltpu.roll(bottom, HD, 1)), jnp.where(
        left, pltpu.roll(top, HD, 1), bottom
    )


def unfold(first, second):
    left = lax.broadcasted_iota(jnp.int32, first.shape, 1) < HD
    top = jnp.where(left, first, pltpu.roll(second, HD, 1))
    bottom = jnp.where(left, pltpu.roll(first, HD, 1), second)
    return jnp.concatenate([top, bottom], axis=0)


def attend_kernel(
    lists, session_col, session_row, qkv0, qkv1, mixed, folded, p_high, p_low, q3, k3, v2
):
    qkv = (qkv0, qkv1)
    for b in range(NBLOCKS):
        t = qkv[b % 2][b // 2]
        q_high, q_low = halves(t[:HD] * SCALE)
        q3[b] = jnp.concatenate([q_high, q_high, q_low], axis=0)
        k_high, k_low = halves(t[HD : 2 * HD].T)
        k3[b] = jnp.concatenate([k_high, k_low, k_high], axis=1)
        v_high, v_low = halves(t[2 * HD :])
        v2[b] = jnp.concatenate([v_high, v_low], axis=0)

    def body(c, carry):
        for e in range(2):
            b = 2 * c + e
            query = q3[b]
            mine = session_row[pl.ds(b, 1), :]
            scores = []
            for j in range(KVB):
                other = lists[b, j]
                s = mm(k3[other], query)
                scores.append(jnp.where(session_col[other] == mine, s, -1e30))
            s = jnp.concatenate(scores, axis=0)
            top = jnp.max(s, axis=0, keepdims=True)
            expo = jnp.exp(s - top)
            probs = expo * (1.0 / jnp.sum(expo, axis=0, keepdims=True))
            high, low = halves(probs)
            p_high[b] = high
            p_low[b] = low
            values = jnp.concatenate([v2[lists[b, j]] for j in range(KVB)], axis=1)
            both = mm(values, high)
            block = both[:HD] + both[HD:] + mm(values[:HD], low)
            mixed[b] = block
            folded[4 * c + 2 * e], folded[4 * c + 2 * e + 1] = fold(block)
        return carry

    lax.fori_loop(0, NBLOCKS // 2, body, 0)


def attend_back_kernel(
    lists, qkv0, qkv1, p_high, p_low, grad, mixed, out0, out1, q2, k2, v3, acc
):
    qkv, out = (qkv0, qkv1), (out0, out1)
    for b in range(NBLOCKS):
        t = qkv[b % 2][b // 2]
        q_high, q_low = halves(t[:HD])
        q2[b] = jnp.concatenate([q_high, q_low], axis=0)
        k_high, k_low = halves(t[HD : 2 * HD])
        k2[b] = jnp.concatenate([k_high, k_low], axis=0)
        v_high, v_low = halves(t[2 * HD :].T)
        v3[b] = jnp.concatenate([v_high, v_low, v_high], axis=1)
    acc[...] = jnp.zeros_like(acc)

    def body(c, carry):
        for e in range(2):
            b = 2 * c + e
            g = unfold(grad[4 * c + 2 * e], grad[4 * c + 2 * e + 1])
            delta = jnp.sum(g * mixed[b], axis=0, keepdims=True)
            g_high, g_low = halves(g)
            g3 = jnp.concatenate([g_high, g_high, g_low], axis=0)
            g2 = jnp.concatenate([g_high, g_low], axis=0)
            grad_probs = jnp.concatenate([mm(v3[lists[b, j]], g3) for j in range(KVB)], axis=0)
            ph, pw = p_high[b], p_low[b]
            probs = ph.astype(F32) + pw.astype(F32)
            s_high, s_low = halves(probs * (grad_probs - delta) * SCALE)
            keys = jnp.concatenate([k2[lists[b, j]] for j in range(KVB)], axis=1)
            both = mm(keys, s_high)
            out[e][c, 0:HD] = both[:HD] + both[HD:] + mm(keys[:HD], s_low)
            query = q2[b]
            both = mm_nt(query, s_high)
            grad_keys = both[:HD] + both[HD:] + mm_nt(query[:HD], s_low)
            both = mm_nt(g2, ph)
            grad_values = both[:HD] + both[HD:] + mm_nt(g2[:HD], pw)
            for j in range(KVB):
                at = slice(j * BLK, (j + 1) * BLK)
                acc[lists[b, j]] += jnp.concatenate([grad_keys[:, at], grad_values[:, at]], axis=0)
        return carry

    lax.fori_loop(0, NBLOCKS // 2, body, 0)
    for b in range(NBLOCKS):
        out[b % 2][b // 2, HD : 3 * HD] = acc[b]


def norm_kernel(
    z_ref, w_high, w_low, rows0, rows1, u0, u1, u2, u3, pieces, out, direct_sum, upstream, mixed
):
    z = z_ref[0]
    n = 4
    quarter, width = direct_sum.shape
    feats = width // n
    for k, u in enumerate((u0, u1, u2, u3)):
        at = pl.ds(pl.multiple_of(lax.rem(z - k + n, n) * feats, feats), feats)
        upstream[:, at] = u[...]
    for group in range(n):
        for h in range(n):
            at = group * feats + h * HD
            mixed[at : at + HD, :] = unfold(pieces[2 * h * n + group], pieces[(2 * h + 1) * n + group])
    m_high, m_low = halves(mixed[...].T)
    projected = mm_nt(m_high, w_high[...]) + mm_nt(m_low, w_high[...]) + mm_nt(m_high, w_low[...])
    rows = jnp.where(z < 2, rows0[...], rows1[...])
    summed = rows.reshape(2 * quarter, width) + projected
    mean = jnp.sum(summed, axis=-1, keepdims=True) / width
    second = jnp.sum(summed * summed, axis=-1, keepdims=True) / width
    inverse = lax.rsqrt(second - mean * mean + EPS)
    normed = (summed - mean) * inverse
    up = jnp.concatenate([upstream[...], upstream[...]], axis=0)
    up_mean = jnp.sum(up, axis=-1, keepdims=True) / width
    up_dot = jnp.sum(up * normed, axis=-1, keepdims=True) / width
    direct = inverse * (up - up_mean - normed * up_dot)
    direct_sum[...] = direct[:quarter] + direct[quarter:]
    d_high, d_low = halves(direct)
    grad = mm(d_high, w_high[...]) + mm(d_low, w_high[...]) + mm(d_high, w_low[...])
    grad = grad.T
    for group in range(n):
        for h in range(n):
            at = group * feats + h * HD
            out[2 * h * n + group], out[(2 * h + 1) * n + group] = fold(grad[at : at + HD])


def input_kernel(half, z_ref, w3, grads, direct_sum, f0, f1, f2, f3):
    z = z_ref[0]
    n = 4
    quarter, width = direct_sum.shape
    feats = width // n
    g = jnp.concatenate([grads[2 * h] + grads[2 * h + 1] for h in range(n)], axis=0).T
    g_high, g_low = halves(g)
    mine = pl.ds(pl.multiple_of(lax.rem(z, 2) * quarter, quarter), quarter)
    here = z // 2 == half
    for k, f in enumerate((f0, f1, f2, f3)):
        column = lax.rem(z + k, n) * feats
        at = pl.ds(pl.multiple_of(column, feats), feats)
        w_high = w3[:, at]
        w_low = w3[:, pl.ds(pl.multiple_of(width + column, feats), feats)]
        f[...] = mm(g_high, w_high) + mm(g_low, w_high) + mm(g_high, w_low)
        f[mine, :] += jnp.where(here, direct_sum[:, at], 0.0)


HD = 64
NBLOCKS = 16
SCALE = 1.0 / math.sqrt(HD)


def shape(dims, kind=F32):
    return jax.ShapeDtypeStruct(dims, kind)


def shards(packets, baseline, w_query, w_key, w_value, w_out, gain, probe, sessions, block_lists):
    tokens, feats = packets.shape
    width = w_query.shape[1]
    n = lax.axis_size("head")
    heads = feats // HD
    members = lax.axis_size("ctx")
    quarter = tokens // n
    z = lax.axis_index("head")
    z_ref = z.reshape(1)
    slab = feats // members
    part = 3 * HD

    travel = packets - baseline
    half = tokens // 2
    gathered = []
    for e in range(2):
        span = slice(e * half, (e + 1) * half)
        own = jnp.concatenate([baseline[span] + alpha * travel[span] for alpha in ALPHAS])
        ups, downs = [own], [own]
        for step in range(1, n):
            ups.append(shift(ups[-1], 1, step - 1, n - 2))
            downs.append(shift(downs[-1], -1, 1, n - step))
        gathered.append([own] + ups[1:] + downs[1:])

    lists = lax.all_to_all(
        jnp.broadcast_to(block_lists[None], (members,) + block_lists.shape), "ctx", 0, 0, tiled=True
    ).reshape(-1, KVB)
    weights = jnp.concatenate(
        [w.reshape(heads, HD, width) for w in (w_query, w_key, w_value)], axis=1
    ).reshape(heads * part, width)
    high, low = halves_outside(weights)
    w3 = jnp.concatenate([high, low, high], axis=1)
    upstream = probe * gain
    up_pieces = exchange(
        [
            lax.dynamic_slice_in_dim(upstream, lax.rem(z + k, n) * quarter, quarter, 0)
            for k in range(n)
        ]
    )
    slab_rows = lax.dynamic_slice_in_dim(w_out, lax.axis_index("ctx") * slab, slab, 0)

    gathered[0], w3, lists, slab_rows = lax.optimization_barrier(
        (gathered[0], w3, lists, slab_rows)
    )
    gathered[1], up_pieces = lax.optimization_barrier((gathered[1], up_pieces))
    whole_out = lax.all_gather(slab_rows, ("head", "ctx"), axis=0, tiled=True)
    out_high, out_low = halves_outside(whole_out)

    qkv, rows = [], []
    for e in range(2):
        projected, own_rows = call(
            project_kernel,
            (shape((members, part, half)), shape((2, quarter, width))),
            [pltpu.VMEM((tokens, 3 * width), BF16)],
            1, z_ref, w3, *gathered[e],
        )
        qkv.append(lax.all_to_all(projected, "ctx", 0, 0, tiled=True))
        rows.append(own_rows)

    blocks = members * tokens // BLK
    everyone = members * n
    session_row = sessions.reshape(blocks, BLK)
    session_col = sessions.reshape(blocks, BLK, 1)
    mixed, folded, p_high, p_low = call(
        attend_kernel,
        (
            shape((blocks, HD, BLK)),
            shape((everyone, HD // 2, BLK)),
            shape((blocks, KVB * BLK, BLK), BF16),
            shape((blocks, KVB * BLK, BLK), BF16),
        ),
        [
            pltpu.VMEM((blocks, part, BLK), BF16),
            pltpu.VMEM((blocks, BLK, part), BF16),
            pltpu.VMEM((blocks, 2 * HD, BLK), BF16),
        ],
        1, lists, session_col, session_row, *qkv,
    )
    folded = lax.all_to_all(folded, ("ctx", "head"), 0, 0, tiled=True)
    grad, direct_sum = call(
        norm_kernel,
        (shape((everyone, HD // 2, BLK)), shape((quarter, width))),
        [pltpu.VMEM((quarter, width), F32), pltpu.VMEM((width, 2 * quarter), F32)],
        1, z_ref, out_high, out_low, *rows, *up_pieces, folded,
    )
    grad = lax.all_to_all(grad, ("ctx", "head"), 0, 0, tiled=True)
    grad_qkv = call(
        attend_back_kernel,
        (shape((members, part, half)),) * 2,
        [
            pltpu.VMEM((blocks, 2 * HD, BLK), BF16),
            pltpu.VMEM((blocks, 2 * HD, BLK), BF16),
            pltpu.VMEM((blocks, BLK, part), BF16),
            pltpu.VMEM((blocks, 2 * HD, BLK), F32),
        ],
        1, lists, *qkv, p_high, p_low, grad, mixed,
    )
    grad_qkv = [lax.all_to_all(g, "ctx", 0, 0, tiled=True) for g in grad_qkv]
    totals = []
    for e in range(2):
        parts = exchange(
            call(
                functools.partial(input_kernel, e),
                (shape((half, feats)),) * n,
                [],
                1, z_ref, w3, grad_qkv[e], direct_sum,
            )
        )
        totals.append(parts[0] + parts[1] + parts[2] + parts[3])
    return travel * jnp.concatenate(totals) / len(ALPHAS)


def pick_shards(mesh):
    members, n = mesh.shape["ctx"], mesh.shape["head"]
    return shards if n == 4 and members == 2 * HEADS // n else general_shards


def solution(mesh):
    return jax.shard_map(
        pick_shards(mesh),
        mesh=mesh,
        in_specs=(
            P("ctx", "head"),
            P("ctx", "head"),
            P("head", None),
            P("head", None),
            P("head", None),
            P("head", None),
            P("head"),
            P("ctx", "head"),
            P(),
            P("ctx", None),
        ),
        out_specs=P("ctx", "head"),
        check_vma=False,
    )
```

```python
import functools
import math

import jax
import jax.numpy as jnp
from jax import lax
from jax.experimental import pallas as pl
from jax.experimental.pallas import tpu as pltpu
from jax.sharding import PartitionSpec as P

HEADS = 16
BLK = 128
KVB = 5
REACH = 2


ALPHAS = (0.25, 0.75)
EPS = 1e-05
HIGHEST = lax.Precision.HIGHEST


def from_behind(x, axis, by):
    size = lax.axis_size(axis)
    pairs = [(i, i + by) for i in range(size) if 0 <= i + by < size]
    return lax.ppermute(x, axis, pairs)


def integrate(points, weights_qkv, w_out, gain, probe, sessions, block_lists):
    steps, rows, feats = points.shape
    width = weights_qkv.shape[1]
    head_dim = width // HEADS
    local_heads = feats // head_dim
    blocks = rows // BLK
    where = lax.axis_index("ctx")
    first = (where - REACH) * blocks
    slots = (2 * REACH + 1) * blocks
    scale = 1.0 / math.sqrt(head_dim)
    part_cols = weights_qkv
    qkv = jnp.einsum(
        "std,ed->ste",
        lax.all_gather(points, "head", axis=2, tiled=True),
        part_cols,
        precision=HIGHEST,
    )
    query = qkv[:, :, :feats]
    pairs = qkv[:, :, feats:]
    below = []
    above = []
    for dist in range(1, REACH + 1):
        below.append(from_behind(pairs, "ctx", dist))
        above.append(from_behind(pairs, "ctx", -dist))
    window = jnp.concatenate(below[::-1] + [pairs] + above, axis=1)
    local = (block_lists - first).reshape(-1)
    tiles = window.reshape(steps, slots, BLK, 2 * feats)
    picked = jnp.take(tiles, local, axis=1).reshape(
        steps, blocks, KVB * BLK, 2, local_heads, head_dim
    )
    keys = picked[:, :, :, 0]
    values = picked[:, :, :, 1]
    token_index = block_lists[:, :, None] * BLK + jnp.arange(BLK, dtype=jnp.int32)[None, None, :]
    key_sessions = jnp.take(sessions, token_index.reshape(blocks, KVB * BLK), axis=0)
    query_sessions = lax.dynamic_slice_in_dim(sessions, where * rows, rows, 0).reshape(blocks, BLK)
    keep = query_sessions[:, :, None] == key_sessions[:, None, :]
    query_heads = query.reshape(steps, blocks, BLK, local_heads, head_dim)
    scores = jnp.einsum("sbqhd,sbkhd->sbhqk", query_heads, keys, precision=HIGHEST) * scale
    scores = jnp.where(keep[None, :, None], scores, -1e30)
    top = jnp.max(scores, axis=-1, keepdims=True)
    expo = jnp.exp(scores - top)
    probs = expo / jnp.sum(expo, axis=-1, keepdims=True)
    mixed = jnp.einsum("sbhqk,sbkhd->sbqhd", probs, values, precision=HIGHEST)
    heads_out = mixed.reshape(steps, rows, feats)
    part_cols = w_out
    projected = jnp.einsum(
        "std,ed->ste",
        lax.all_gather(heads_out, "head", axis=2, tiled=True),
        part_cols,
        precision=HIGHEST,
    )
    summed = points + projected
    first_sum, second_sum = lax.psum(
        (jnp.sum(summed, axis=-1), jnp.sum(summed * summed, axis=-1)), "head"
    )
    mean = first_sum / width
    inverse = lax.rsqrt(second_sum / width - mean * mean + EPS)
    normed = (summed - mean[..., None]) * inverse[..., None]
    upstream = probe * gain
    upstream_sum, upstream_dot = lax.psum(
        (jnp.sum(upstream, axis=-1), jnp.sum(upstream * normed, axis=-1)), "head"
    )
    direct = inverse[..., None] * (
        upstream - upstream_sum[..., None] / width - normed * (upstream_dot / width)[..., None]
    )
    partial_heads = jnp.einsum("ste,ed->std", direct, w_out, precision=HIGHEST)
    grad_heads = lax.psum_scatter(partial_heads, "head", scatter_dimension=2, tiled=True)
    grad_mixed = grad_heads.reshape(steps, blocks, BLK, local_heads, head_dim)
    delta = jnp.einsum("sbqhd,sbqhd->sbhq", grad_mixed, mixed, precision=HIGHEST)
    grad_probs = jnp.einsum("sbqhd,sbkhd->sbhqk", grad_mixed, values, precision=HIGHEST)
    grad_scores = probs * (grad_probs - delta[..., None]) * scale
    grad_query = jnp.einsum("sbhqk,sbkhd->sbqhd", grad_scores, keys, precision=HIGHEST)
    grad_keys = jnp.einsum("sbhqk,sbqhd->sbkhd", grad_scores, query_heads, precision=HIGHEST)
    grad_values = jnp.einsum("sbhqk,sbqhd->sbkhd", probs, grad_mixed, precision=HIGHEST)
    grad_picked = jnp.stack([grad_keys, grad_values], axis=3).reshape(
        steps, blocks * KVB, BLK, 2 * feats
    )
    selector = (local[:, None] == jnp.arange(slots, dtype=jnp.int32)[None, :]).astype(jnp.float32)
    grad_window = jnp.einsum("snlc,nw->swlc", grad_picked, selector, precision=HIGHEST).reshape(
        steps, slots * BLK, 2 * feats
    )
    owned = grad_window[:, REACH * rows : (REACH + 1) * rows]
    for dist in range(1, REACH + 1):
        upper = grad_window[:, (REACH + dist) * rows : (REACH + dist + 1) * rows]
        lower = grad_window[:, (REACH - dist) * rows : (REACH - dist + 1) * rows]
        owned = owned + from_behind(upper, "ctx", dist)
        owned = owned + from_behind(lower, "ctx", -dist)
    grad_qkv = jnp.concatenate([grad_query.reshape(steps, rows, feats), owned], axis=-1)
    partial_input = jnp.einsum("ste,ed->std", grad_qkv, weights_qkv, precision=HIGHEST)
    return (direct, partial_input)


def collect_inputs(partial_input):
    return lax.psum_scatter(partial_input, "head", scatter_dimension=2, tiled=True)


def general_shards(packets, baseline, w_query, w_key, w_value, w_out, gain, probe, sessions, block_lists):
    weights_qkv = jnp.concatenate([w_query, w_key, w_value], axis=0)
    travel = packets - baseline
    points = jnp.stack([baseline + alpha * travel for alpha in ALPHAS])
    passes = [
        integrate(points[index : index + 1], weights_qkv, w_out, gain, probe, sessions, block_lists)
        for index in range(len(ALPHAS))
    ]
    grads = jnp.zeros_like(packets)
    for direct, partial_input in passes:
        grads = grads + direct.sum(axis=0) + collect_inputs(partial_input).sum(axis=0)
    return travel * grads / len(ALPHAS)


F32 = jnp.float32
BF16 = jnp.bfloat16
MIB = 1 << 20
VM = pl.BlockSpec(memory_space=pltpu.VMEM)
SM = pl.BlockSpec(memory_space=pltpu.SMEM)


def halves(x):
    high = x.astype(BF16)
    low = (x - high.astype(F32)).astype(BF16)
    return high, low


def halves_outside(x):
    rounded = lax.reduce_precision(x, 8, 7)
    return rounded.astype(BF16), (x - rounded).astype(BF16)


def mm(a, b):
    return lax.dot_general(a, b, (((1,), (0,)), ((), ())), preferred_element_type=F32)


def mm_nt(a, b):
    return lax.dot_general(a, b, (((1,), (1,)), ((), ())), preferred_element_type=F32)


def call(kernel, mib, outs, scratch, n_smem, *args):
    return pl.pallas_call(
        kernel,
        out_shape=outs,
        in_specs=[SM] * n_smem + [VM] * (len(args) - n_smem),
        out_specs=jax.tree.map(lambda _: VM, outs),
        scratch_shapes=scratch,
        compiler_params=pltpu.CompilerParams(vmem_limit_bytes=mib * MIB),
    )(*args)


def shift(x, by, low, high):
    return lax.ppermute(x, "head", [(i, i + by) for i in range(low, high + 1)])


def rotate(x, by):
    size = lax.axis_size("head")
    return lax.ppermute(x, "head", [(i, (i + by) % size) for i in range(size)])


def exchange(pieces):
    return [pieces[0]] + [rotate(pieces[k], k) for k in range(1, len(pieces))]


def project_kernel(z_ref, w3, own, u1, u2, u3, d1, d2, d3, out, rows, x3):
    ups, downs = (u1, u2, u3), (d1, d2, d3)
    z = z_ref[0]
    n = 4
    quarter, width = rows.shape[1:]
    both, feats = own.shape
    tokens = both // 2
    for k in range(n):
        column = pl.multiple_of(lax.rem(z - k + n, n) * feats, feats)
        for s in range(2):
            span = pl.ds(s * tokens, tokens)
            if k == 0:
                x = own[span]
            else:
                x = ups[k - 1][span] + downs[n - k - 1][span]
            for q in range(n):
                @pl.when(z == q)
                def _(x=x, q=q, s=s):
                    rows[s, :, pl.ds(column, feats)] = x[q * quarter : (q + 1) * quarter]
            high, low = halves(x)
            x3[span, pl.ds(column, feats)] = high
            x3[span, pl.ds(pl.multiple_of(width + column, feats), feats)] = high
            x3[span, pl.ds(pl.multiple_of(2 * width + column, feats), feats)] = low
    part = out.shape[1]
    for h in range(n):
        r = mm_nt(w3[h * part : (h + 1) * part, :], x3[...])
        for s in range(2):
            out[2 * h + s] = r[:, s * tokens : (s + 1) * tokens]


def fold(x):
    top, bottom = x[: HD // 2], x[HD // 2 :]
    left = lax.broadcasted_iota(jnp.int32, top.shape, 1) < HD
    return jnp.where(left, top, pltpu.roll(bottom, HD, 1)), jnp.where(
        left, pltpu.roll(top, HD, 1), bottom
    )


def unfold(first, second):
    left = lax.broadcasted_iota(jnp.int32, first.shape, 1) < HD
    top = jnp.where(left, first, pltpu.roll(second, HD, 1))
    bottom = jnp.where(left, pltpu.roll(first, HD, 1), second)
    return jnp.concatenate([top, bottom], axis=0)


def attend_kernel(
    lists, session_col, session_row, qkv, mixed, folded, p_high, p_low, q3, k3, v2
):
    for b in range(NBLOCKS):
        t = qkv[b // 2, :, (b % 2) * BLK : (b % 2 + 1) * BLK]
        q_high, q_low = halves(t[:HD] * SCALE)
        q3[b] = jnp.concatenate([q_high, q_high, q_low], axis=0)
        k_high, k_low = halves(t[HD : 2 * HD].T)
        k3[b] = jnp.concatenate([k_high, k_low, k_high], axis=1)
        v_high, v_low = halves(t[2 * HD :])
        v2[b] = jnp.concatenate([v_high, v_low], axis=0)

    def body(c, carry):
        blocks = [GROUP * c + e for e in range(GROUP)]
        scores = []
        for b in blocks:
            mine = session_row[pl.ds(b, 1), :]
            tiles = []
            for j in range(KVB):
                other = lists[b, j]
                s = mm(k3[other], q3[b])
                tiles.append(jnp.where(session_col[other] == mine, s, -1e30))
            scores.append(jnp.concatenate(tiles, axis=0))
        tops = [jnp.max(s, axis=0, keepdims=True) for s in scores]
        expos = [jnp.exp(s - top) for s, top in zip(scores, tops)]
        scales = [1.0 / jnp.sum(expo, axis=0, keepdims=True) for expo in expos]
        for b, e, expo, each in zip(blocks, range(GROUP), expos, scales):
            high, low = halves(expo * each)
            p_high[b] = high
            p_low[b] = low
            values = jnp.concatenate([v2[lists[b, j]] for j in range(KVB)], axis=1)
            both = mm(values, high)
            block = both[:HD] + both[HD:] + mm(values[:HD], low)
            mixed[b] = block
            folded[2 * b], folded[2 * b + 1] = fold(block)
        return carry

    lax.fori_loop(0, NBLOCKS // GROUP, body, 0)


def attend_back_kernel(
    lists, qkv, p_high, p_low, grad, mixed, out0, out1, q2, k2, v3, acc
):
    out = (out0, out1)
    for b in range(NBLOCKS):
        t = qkv[b // 2, :, (b % 2) * BLK : (b % 2 + 1) * BLK]
        q_high, q_low = halves(t[:HD])
        q2[b] = jnp.concatenate([q_high, q_low], axis=0)
        k_high, k_low = halves(t[HD : 2 * HD])
        k2[b] = jnp.concatenate([k_high, k_low], axis=0)
        v_high, v_low = halves(t[2 * HD :].T)
        v3[b] = jnp.concatenate([v_high, v_low, v_high], axis=1)
    acc[...] = jnp.zeros_like(acc)

    def body(c, carry):
        blocks = [GROUP * c + e for e in range(GROUP)]
        grads = [unfold(grad[2 * b], grad[2 * b + 1]) for b in blocks]
        parts = [halves(g) for g in grads]
        probs_grads = []
        for b, (g_high, g_low) in zip(blocks, parts):
            g3 = jnp.concatenate([g_high, g_high, g_low], axis=0)
            probs_grads.append(
                jnp.concatenate([mm(v3[lists[b, j]], g3) for j in range(KVB)], axis=0)
            )
        added = []
        for e, b in enumerate(blocks):
            delta = jnp.sum(grads[e] * mixed[b], axis=0, keepdims=True)
            g2 = jnp.concatenate(parts[e], axis=0)
            ph, pw = p_high[b], p_low[b]
            probs = ph.astype(F32) + pw.astype(F32)
            s_high, s_low = halves(probs * (probs_grads[e] - delta) * SCALE)
            keys = jnp.concatenate([k2[lists[b, j]] for j in range(KVB)], axis=1)
            both = mm(keys, s_high)
            out[e % 2][(GROUP // 2) * c + e // 2, 0:HD] = (
                both[:HD] + both[HD:] + mm(keys[:HD], s_low)
            )
            query = q2[b]
            both = mm_nt(query, s_high)
            grad_keys = both[:HD] + both[HD:] + mm_nt(query[:HD], s_low)
            both = mm_nt(g2, ph)
            grad_values = both[:HD] + both[HD:] + mm_nt(g2[:HD], pw)
            added.append(jnp.concatenate([grad_keys, grad_values], axis=0))
        for b, both in zip(blocks, added):
            for j in range(KVB):
                acc[lists[b, j]] += both[:, j * BLK : (j + 1) * BLK]
        return carry

    lax.fori_loop(0, NBLOCKS // GROUP, body, 0)
    for b in range(NBLOCKS):
        out[b % 2][b // 2, HD : 3 * HD] = acc[b]


def norm_kernel(
    w_high, w_low, rows, ups, pieces, out, direct_sum, upstream, mixed
):
    n = 4
    quarter, width = direct_sum.shape
    feats = width // n
    for k in range(n):
        upstream[:, k * feats : (k + 1) * feats] = ups[k]
    for group in range(n):
        for h in range(n):
            at = group * feats + h * HD
            mixed[at : at + HD, :] = unfold(pieces[2 * h * n + group], pieces[(2 * h + 1) * n + group])
    m_high, m_low = halves(mixed[...].T)
    projected = mm_nt(m_high, w_high[...]) + mm_nt(m_low, w_high[...]) + mm_nt(m_high, w_low[...])
    summed = rows[...].reshape(2 * quarter, width) + projected
    mean = jnp.sum(summed, axis=-1, keepdims=True) / width
    second = jnp.sum(summed * summed, axis=-1, keepdims=True) / width
    inverse = lax.rsqrt(second - mean * mean + EPS)
    normed = (summed - mean) * inverse
    up = jnp.concatenate([upstream[...], upstream[...]], axis=0)
    up_mean = jnp.sum(up, axis=-1, keepdims=True) / width
    up_dot = jnp.sum(up * normed, axis=-1, keepdims=True) / width
    direct = inverse * (up - up_mean - normed * up_dot)
    direct_sum[...] = direct[:quarter] + direct[quarter:]
    d_high, d_low = halves(direct)
    grad = mm(d_high, w_high[...]) + mm(d_low, w_high[...]) + mm(d_high, w_low[...])
    grad = grad.T
    for group in range(n):
        for h in range(n):
            at = group * feats + h * HD
            out[2 * h * n + group], out[(2 * h + 1) * n + group] = fold(grad[at : at + HD])


def input_kernel(half, z_ref, w3, grads, direct_sum, f0, f1, f2, f3):
    z = z_ref[0]
    n = 4
    quarter, width = direct_sum.shape
    feats = width // n
    g = jnp.concatenate([grads[2 * h] + grads[2 * h + 1] for h in range(n)], axis=0).T
    g_high, g_low = halves(g)
    mine = pl.ds(pl.multiple_of(lax.rem(z, 2) * quarter, quarter), quarter)
    here = z // 2 == half
    for k, f in enumerate((f0, f1, f2, f3)):
        column = lax.rem(z + k, n) * feats
        at = pl.ds(pl.multiple_of(column, feats), feats)
        w_high = w3[:, at]
        w_low = w3[:, pl.ds(pl.multiple_of(width + column, feats), feats)]
        f[...] = mm(g_high, w_high) + mm(g_low, w_high) + mm(g_high, w_low)
        f[mine, :] += jnp.where(here, direct_sum[:, at], 0.0)


HD = 64
NBLOCKS = 16
GROUP = 4
SCALE = 1.0 / math.sqrt(HD)


def shape(dims, kind=F32):
    return jax.ShapeDtypeStruct(dims, kind)


def shards(packets, baseline, w_query, w_key, w_value, w_out, gain, probe, sessions, block_lists):
    tokens, feats = packets.shape
    width = w_query.shape[1]
    n = lax.axis_size("head")
    heads = feats // HD
    members = lax.axis_size("ctx")
    quarter = tokens // n
    z = lax.axis_index("head")
    z_ref = z.reshape(1)
    slab = feats // members
    part = 3 * HD

    travel = packets - baseline
    half = tokens // 2
    own = jnp.concatenate([baseline + alpha * travel for alpha in ALPHAS])
    ups, downs = [own], [own]
    for step in range(1, n):
        ups.append(shift(ups[-1], 1, step - 1, n - 2))
        downs.append(shift(downs[-1], -1, 1, n - step))
    gathered = [own] + ups[1:] + downs[1:]

    lists = lax.all_to_all(
        jnp.broadcast_to(block_lists[None], (members,) + block_lists.shape), "ctx", 0, 0, tiled=True
    ).reshape(-1, KVB)
    weights = jnp.concatenate(
        [w.reshape(heads, HD, width) for w in (w_query, w_key, w_value)], axis=1
    ).reshape(heads * part, width)
    high, low = halves_outside(weights)
    w3 = jnp.concatenate([high, low, high], axis=1)
    slab_rows = lax.dynamic_slice_in_dim(w_out, lax.axis_index("ctx") * slab, slab, 0)
    upstream = (probe * gain).reshape(n, quarter, feats)
    gathered, w3, lists, slab_rows, upstream = lax.optimization_barrier(
        (gathered, w3, lists, slab_rows, upstream)
    )
    whole_out = lax.all_gather(slab_rows, ("head", "ctx"), axis=0, tiled=True)
    out_high, out_low = halves_outside(whole_out)

    qkv, rows = call(
        project_kernel, 20,
        (shape((members, part, tokens)), shape((2, quarter, width))),
        [pltpu.VMEM((2 * tokens, 3 * width), BF16)],
        1, z_ref, w3, *gathered,
    )
    qkv = lax.all_to_all(qkv, "ctx", 0, 0, tiled=True)
    upstream = lax.all_to_all(upstream, "head", 0, 0, tiled=True)
    qkv, upstream = lax.optimization_barrier((qkv, upstream))

    blocks = members * tokens // BLK
    everyone = members * n
    session_row = sessions.reshape(blocks, BLK)
    session_col = sessions.reshape(blocks, BLK, 1)
    mixed, folded, p_high, p_low = call(
        attend_kernel, 20,
        (
            shape((blocks, HD, BLK)),
            shape((everyone, HD // 2, BLK)),
            shape((blocks, KVB * BLK, BLK), BF16),
            shape((blocks, KVB * BLK, BLK), BF16),
        ),
        [
            pltpu.VMEM((blocks, part, BLK), BF16),
            pltpu.VMEM((blocks, BLK, part), BF16),
            pltpu.VMEM((blocks, 2 * HD, BLK), BF16),
        ],
        1, lists, session_col, session_row, qkv,
    )
    folded = lax.all_to_all(folded, ("ctx", "head"), 0, 0, tiled=True)
    grad, direct_sum = call(
        norm_kernel, 20,
        (shape((everyone, HD // 2, BLK)), shape((quarter, width))),
        [pltpu.VMEM((quarter, width), F32), pltpu.VMEM((width, 2 * quarter), F32)],
        0, out_high, out_low, rows, upstream, folded,
    )
    grad = lax.all_to_all(grad, ("ctx", "head"), 0, 0, tiled=True)
    grad_qkv = call(
        attend_back_kernel, 20,
        (shape((members, part, half)),) * 2,
        [
            pltpu.VMEM((blocks, 2 * HD, BLK), BF16),
            pltpu.VMEM((blocks, 2 * HD, BLK), BF16),
            pltpu.VMEM((blocks, BLK, part), BF16),
            pltpu.VMEM((blocks, 2 * HD, BLK), F32),
        ],
        1, lists, qkv, p_high, p_low, grad, mixed,
    )
    grad_qkv = [lax.all_to_all(g, "ctx", 0, 0, tiled=True) for g in grad_qkv]
    totals = []
    for e in range(2):
        parts = exchange(
            call(
                functools.partial(input_kernel, e), 16,
                (shape((half, feats)),) * n,
                [],
                1, z_ref, w3, grad_qkv[e], direct_sum,
            )
        )
        totals.append(parts[0] + parts[1] + parts[2] + parts[3])
    return travel * jnp.concatenate(totals) / len(ALPHAS)


def pick_shards(mesh):
    members, n = mesh.shape["ctx"], mesh.shape["head"]
    return shards if n == 4 and members == 2 * HEADS // n else general_shards


def solution(mesh):
    return jax.shard_map(
        pick_shards(mesh),
        mesh=mesh,
        in_specs=(
            P("ctx", "head"),
            P("ctx", "head"),
            P("head", None),
            P("head", None),
            P("head", None),
            P("head", None),
            P("head"),
            P("ctx", "head"),
            P(),
            P("ctx", None),
        ),
        out_specs=P("ctx", "head"),
        check_vma=False,
    )
```

```python
import functools
import math

import jax
import jax.numpy as jnp
from jax import lax
from jax.experimental import pallas as pl
from jax.experimental.pallas import tpu as pltpu
from jax.sharding import PartitionSpec as P

HEADS = 16
BLK = 128
KVB = 5
REACH = 2


ALPHAS = (0.25, 0.75)
EPS = 1e-05
HIGHEST = lax.Precision.HIGHEST


def from_behind(x, axis, by):
    size = lax.axis_size(axis)
    pairs = [(i, i + by) for i in range(size) if 0 <= i + by < size]
    return lax.ppermute(x, axis, pairs)


def integrate(points, weights_qkv, w_out, gain, probe, sessions, block_lists):
    steps, rows, feats = points.shape
    width = weights_qkv.shape[1]
    head_dim = width // HEADS
    local_heads = feats // head_dim
    blocks = rows // BLK
    where = lax.axis_index("ctx")
    first = (where - REACH) * blocks
    slots = (2 * REACH + 1) * blocks
    scale = 1.0 / math.sqrt(head_dim)
    part_cols = weights_qkv
    qkv = jnp.einsum(
        "std,ed->ste",
        lax.all_gather(points, "head", axis=2, tiled=True),
        part_cols,
        precision=HIGHEST,
    )
    query = qkv[:, :, :feats]
    pairs = qkv[:, :, feats:]
    below = []
    above = []
    for dist in range(1, REACH + 1):
        below.append(from_behind(pairs, "ctx", dist))
        above.append(from_behind(pairs, "ctx", -dist))
    window = jnp.concatenate(below[::-1] + [pairs] + above, axis=1)
    local = (block_lists - first).reshape(-1)
    tiles = window.reshape(steps, slots, BLK, 2 * feats)
    picked = jnp.take(tiles, local, axis=1).reshape(
        steps, blocks, KVB * BLK, 2, local_heads, head_dim
    )
    keys = picked[:, :, :, 0]
    values = picked[:, :, :, 1]
    token_index = block_lists[:, :, None] * BLK + jnp.arange(BLK, dtype=jnp.int32)[None, None, :]
    key_sessions = jnp.take(sessions, token_index.reshape(blocks, KVB * BLK), axis=0)
    query_sessions = lax.dynamic_slice_in_dim(sessions, where * rows, rows, 0).reshape(blocks, BLK)
    keep = query_sessions[:, :, None] == key_sessions[:, None, :]
    query_heads = query.reshape(steps, blocks, BLK, local_heads, head_dim)
    scores = jnp.einsum("sbqhd,sbkhd->sbhqk", query_heads, keys, precision=HIGHEST) * scale
    scores = jnp.where(keep[None, :, None], scores, -1e30)
    top = jnp.max(scores, axis=-1, keepdims=True)
    expo = jnp.exp(scores - top)
    probs = expo / jnp.sum(expo, axis=-1, keepdims=True)
    mixed = jnp.einsum("sbhqk,sbkhd->sbqhd", probs, values, precision=HIGHEST)
    heads_out = mixed.reshape(steps, rows, feats)
    part_cols = w_out
    projected = jnp.einsum(
        "std,ed->ste",
        lax.all_gather(heads_out, "head", axis=2, tiled=True),
        part_cols,
        precision=HIGHEST,
    )
    summed = points + projected
    first_sum, second_sum = lax.psum(
        (jnp.sum(summed, axis=-1), jnp.sum(summed * summed, axis=-1)), "head"
    )
    mean = first_sum / width
    inverse = lax.rsqrt(second_sum / width - mean * mean + EPS)
    normed = (summed - mean[..., None]) * inverse[..., None]
    upstream = probe * gain
    upstream_sum, upstream_dot = lax.psum(
        (jnp.sum(upstream, axis=-1), jnp.sum(upstream * normed, axis=-1)), "head"
    )
    direct = inverse[..., None] * (
        upstream - upstream_sum[..., None] / width - normed * (upstream_dot / width)[..., None]
    )
    partial_heads = jnp.einsum("ste,ed->std", direct, w_out, precision=HIGHEST)
    grad_heads = lax.psum_scatter(partial_heads, "head", scatter_dimension=2, tiled=True)
    grad_mixed = grad_heads.reshape(steps, blocks, BLK, local_heads, head_dim)
    delta = jnp.einsum("sbqhd,sbqhd->sbhq", grad_mixed, mixed, precision=HIGHEST)
    grad_probs = jnp.einsum("sbqhd,sbkhd->sbhqk", grad_mixed, values, precision=HIGHEST)
    grad_scores = probs * (grad_probs - delta[..., None]) * scale
    grad_query = jnp.einsum("sbhqk,sbkhd->sbqhd", grad_scores, keys, precision=HIGHEST)
    grad_keys = jnp.einsum("sbhqk,sbqhd->sbkhd", grad_scores, query_heads, precision=HIGHEST)
    grad_values = jnp.einsum("sbhqk,sbqhd->sbkhd", probs, grad_mixed, precision=HIGHEST)
    grad_picked = jnp.stack([grad_keys, grad_values], axis=3).reshape(
        steps, blocks * KVB, BLK, 2 * feats
    )
    selector = (local[:, None] == jnp.arange(slots, dtype=jnp.int32)[None, :]).astype(jnp.float32)
    grad_window = jnp.einsum("snlc,nw->swlc", grad_picked, selector, precision=HIGHEST).reshape(
        steps, slots * BLK, 2 * feats
    )
    owned = grad_window[:, REACH * rows : (REACH + 1) * rows]
    for dist in range(1, REACH + 1):
        upper = grad_window[:, (REACH + dist) * rows : (REACH + dist + 1) * rows]
        lower = grad_window[:, (REACH - dist) * rows : (REACH - dist + 1) * rows]
        owned = owned + from_behind(upper, "ctx", dist)
        owned = owned + from_behind(lower, "ctx", -dist)
    grad_qkv = jnp.concatenate([grad_query.reshape(steps, rows, feats), owned], axis=-1)
    partial_input = jnp.einsum("ste,ed->std", grad_qkv, weights_qkv, precision=HIGHEST)
    return (direct, partial_input)


def collect_inputs(partial_input):
    return lax.psum_scatter(partial_input, "head", scatter_dimension=2, tiled=True)


def general_shards(packets, baseline, w_query, w_key, w_value, w_out, gain, probe, sessions, block_lists):
    weights_qkv = jnp.concatenate([w_query, w_key, w_value], axis=0)
    travel = packets - baseline
    points = jnp.stack([baseline + alpha * travel for alpha in ALPHAS])
    passes = [
        integrate(points[index : index + 1], weights_qkv, w_out, gain, probe, sessions, block_lists)
        for index in range(len(ALPHAS))
    ]
    grads = jnp.zeros_like(packets)
    for direct, partial_input in passes:
        grads = grads + direct.sum(axis=0) + collect_inputs(partial_input).sum(axis=0)
    return travel * grads / len(ALPHAS)


F32 = jnp.float32
BF16 = jnp.bfloat16
MIB = 1 << 20
VM = pl.BlockSpec(memory_space=pltpu.VMEM)
SM = pl.BlockSpec(memory_space=pltpu.SMEM)


def halves(x):
    high = x.astype(BF16)
    low = (x - high.astype(F32)).astype(BF16)
    return high, low


def halves_outside(x):
    rounded = lax.reduce_precision(x, 8, 7)
    return rounded.astype(BF16), (x - rounded).astype(BF16)


def mm(a, b):
    return lax.dot_general(a, b, (((1,), (0,)), ((), ())), preferred_element_type=F32)


def mm_nt(a, b):
    return lax.dot_general(a, b, (((1,), (1,)), ((), ())), preferred_element_type=F32)


def call(kernel, mib, outs, scratch, n_smem, *args, streamed_in=(), streamed_out=()):
    grid = (NBLOCKS // GROUP,) if streamed_in or streamed_out else ()
    one_in = pl.BlockSpec((GROUP, KVB * BLK, BLK), lambda c: (c, 0, 0))
    in_specs = [SM] * n_smem + [VM] * (len(args) - n_smem)
    for i in streamed_in:
        in_specs[i] = one_in
    out_specs = jax.tree.map(lambda _: VM, outs)
    if streamed_out:
        out_specs = tuple(one_in if i in streamed_out else VM for i in range(len(outs)))
    return pl.pallas_call(
        kernel,
        out_shape=outs,
        grid=grid,
        in_specs=in_specs,
        out_specs=out_specs,
        scratch_shapes=scratch,
        compiler_params=pltpu.CompilerParams(vmem_limit_bytes=mib * MIB),
    )(*args)


def shift(x, by, low, high):
    return lax.ppermute(x, "head", [(i, i + by) for i in range(low, high + 1)])


def rotate(x, by):
    size = lax.axis_size("head")
    return lax.ppermute(x, "head", [(i, (i + by) % size) for i in range(size)])


def exchange(pieces):
    return [pieces[0]] + [rotate(pieces[k], k) for k in range(1, len(pieces))]


def project_kernel(z_ref, w3, own, u1, u2, u3, d1, d2, d3, out, rows, x3):
    ups, downs = (u1, u2, u3), (d1, d2, d3)
    z = z_ref[0]
    n = 4
    quarter, width = rows.shape[1:]
    both, feats = own.shape
    tokens = both // 2
    for k in range(n):
        column = pl.multiple_of(lax.rem(z - k + n, n) * feats, feats)
        for s in range(2):
            span = pl.ds(s * tokens, tokens)
            if k == 0:
                x = own[span]
            else:
                x = ups[k - 1][span] + downs[n - k - 1][span]
            for q in range(n):
                @pl.when(z == q)
                def _(x=x, q=q, s=s):
                    rows[s, :, pl.ds(column, feats)] = x[q * quarter : (q + 1) * quarter]
            high, low = halves(x)
            x3[span, pl.ds(column, feats)] = high
            x3[span, pl.ds(pl.multiple_of(width + column, feats), feats)] = high
            x3[span, pl.ds(pl.multiple_of(2 * width + column, feats), feats)] = low
    part = out.shape[1]
    for h in range(n):
        r = mm_nt(w3[h * part : (h + 1) * part, :], x3[...])
        for s in range(2):
            out[2 * h + s] = r[:, s * tokens : (s + 1) * tokens]


def fold(x):
    top, bottom = x[: HD // 2], x[HD // 2 :]
    left = lax.broadcasted_iota(jnp.int32, top.shape, 1) < HD
    return jnp.where(left, top, pltpu.roll(bottom, HD, 1)), jnp.where(
        left, pltpu.roll(top, HD, 1), bottom
    )


def unfold(first, second):
    left = lax.broadcasted_iota(jnp.int32, first.shape, 1) < HD
    top = jnp.where(left, first, pltpu.roll(second, HD, 1))
    bottom = jnp.where(left, pltpu.roll(first, HD, 1), second)
    return jnp.concatenate([top, bottom], axis=0)


def attend_kernel(
    lists, session_col, session_row, qkv, mixed, folded, p_high, p_low, q3, k3, v2
):
    c = pl.program_id(0)

    @pl.when(c == 0)
    def _():
        for b in range(NBLOCKS):
            t = qkv[b // 2, :, (b % 2) * BLK : (b % 2 + 1) * BLK]
            q_high, q_low = halves(t[:HD] * SCALE)
            q3[b] = jnp.concatenate([q_high, q_high, q_low], axis=0)
            k_high, k_low = halves(t[HD : 2 * HD].T)
            k3[b] = jnp.concatenate([k_high, k_low, k_high], axis=1)
            v_high, v_low = halves(t[2 * HD :])
            v2[b] = jnp.concatenate([v_high, v_low], axis=0)

    blocks = [GROUP * c + e for e in range(GROUP)]
    scores = []
    for b in blocks:
        mine = session_row[pl.ds(b, 1), :]
        tiles = []
        for j in range(KVB):
            other = lists[b, j]
            s = mm(k3[other], q3[b])
            tiles.append(jnp.where(session_col[other] == mine, s, -1e30))
        scores.append(jnp.concatenate(tiles, axis=0))
    tops = [jnp.max(s, axis=0, keepdims=True) for s in scores]
    expos = [jnp.exp(s - top) for s, top in zip(scores, tops)]
    scales = [1.0 / jnp.sum(expo, axis=0, keepdims=True) for expo in expos]
    for b, e, expo, each in zip(blocks, range(GROUP), expos, scales):
        high, low = halves(expo * each)
        p_high[e] = high
        p_low[e] = low
        values = jnp.concatenate([v2[lists[b, j]] for j in range(KVB)], axis=1)
        both = mm(values, high)
        block = both[:HD] + both[HD:] + mm(values[:HD], low)
        mixed[b] = block
        folded[2 * b], folded[2 * b + 1] = fold(block)


def attend_back_kernel(
    lists, qkv, p_high, p_low, grad, mixed, out0, out1, q2, k2, v3, acc
):
    out = (out0, out1)
    c = pl.program_id(0)

    @pl.when(c == 0)
    def _():
        for b in range(NBLOCKS):
            t = qkv[b // 2, :, (b % 2) * BLK : (b % 2 + 1) * BLK]
            q_high, q_low = halves(t[:HD])
            q2[b] = jnp.concatenate([q_high, q_low], axis=0)
            k_high, k_low = halves(t[HD : 2 * HD])
            k2[b] = jnp.concatenate([k_high, k_low], axis=0)
            v_high, v_low = halves(t[2 * HD :].T)
            v3[b] = jnp.concatenate([v_high, v_low, v_high], axis=1)
        acc[...] = jnp.zeros_like(acc)

    blocks = [GROUP * c + e for e in range(GROUP)]
    grads = [unfold(grad[2 * b], grad[2 * b + 1]) for b in blocks]
    parts = [halves(g) for g in grads]
    probs_grads = []
    for b, (g_high, g_low) in zip(blocks, parts):
        g3 = jnp.concatenate([g_high, g_high, g_low], axis=0)
        probs_grads.append(
            jnp.concatenate([mm(v3[lists[b, j]], g3) for j in range(KVB)], axis=0)
        )
    added = []
    for e, b in enumerate(blocks):
        delta = jnp.sum(grads[e] * mixed[b], axis=0, keepdims=True)
        g2 = jnp.concatenate(parts[e], axis=0)
        ph, pw = p_high[e], p_low[e]
        probs = ph.astype(F32) + pw.astype(F32)
        s_high, s_low = halves(probs * (probs_grads[e] - delta) * SCALE)
        keys = jnp.concatenate([k2[lists[b, j]] for j in range(KVB)], axis=1)
        both = mm(keys, s_high)
        out[e % 2][(GROUP // 2) * c + e // 2, 0:HD] = (
            both[:HD] + both[HD:] + mm(keys[:HD], s_low)
        )
        query = q2[b]
        both = mm_nt(query, s_high)
        grad_keys = both[:HD] + both[HD:] + mm_nt(query[:HD], s_low)
        both = mm_nt(g2, ph)
        grad_values = both[:HD] + both[HD:] + mm_nt(g2[:HD], pw)
        added.append(jnp.concatenate([grad_keys, grad_values], axis=0))
    for b, both in zip(blocks, added):
        for j in range(KVB):
            acc[lists[b, j]] += both[:, j * BLK : (j + 1) * BLK]

    @pl.when(c == NBLOCKS // GROUP - 1)
    def _():
        for b in range(NBLOCKS):
            out[b % 2][b // 2, HD : 3 * HD] = acc[b]


def split_kernel(slabs, high, low):
    members, n = slabs.shape[:2]
    slab = high.shape[0] // (members * n)
    for i in range(members):
        for j in range(n):
            at = slice((j * members + i) * slab, (j * members + i + 1) * slab)
            high[at], low[at] = halves(slabs[i, j, :slab])


def norm_kernel(
    z_ref, w_high, w_low, rows, ups, pieces, out, direct_sum, upstream, mixed
):
    n = 4
    quarter, width = direct_sum.shape
    feats = width // n
    for k in range(n):
        start = pl.multiple_of(z_ref[0] * quarter, quarter)
        upstream[:, k * feats : (k + 1) * feats] = ups[k, pl.ds(start, quarter)]
    for group in range(n):
        for h in range(n):
            at = group * feats + h * HD
            mixed[at : at + HD, :] = unfold(pieces[2 * h * n + group], pieces[(2 * h + 1) * n + group])
    m_high, m_low = halves(mixed[...].T)
    projected = mm_nt(m_high, w_high[...]) + mm_nt(m_low, w_high[...]) + mm_nt(m_high, w_low[...])
    summed = rows[...].reshape(2 * quarter, width) + projected
    mean = jnp.sum(summed, axis=-1, keepdims=True) / width
    second = jnp.sum(summed * summed, axis=-1, keepdims=True) / width
    inverse = lax.rsqrt(second - mean * mean + EPS)
    normed = (summed - mean) * inverse
    up = jnp.concatenate([upstream[...], upstream[...]], axis=0)
    up_mean = jnp.sum(up, axis=-1, keepdims=True) / width
    up_dot = jnp.sum(up * normed, axis=-1, keepdims=True) / width
    direct = inverse * (up - up_mean - normed * up_dot)
    direct_sum[...] = direct[:quarter] + direct[quarter:]
    d_high, d_low = halves(direct)
    grad = mm(d_high, w_high[...]) + mm(d_low, w_high[...]) + mm(d_high, w_low[...])
    grad = grad.T
    for group in range(n):
        for h in range(n):
            at = group * feats + h * HD
            out[2 * h * n + group], out[(2 * h + 1) * n + group] = fold(grad[at : at + HD])


def input_kernel(half, z_ref, w3, grads, direct_sum, f0, f1, f2, f3):
    z = z_ref[0]
    n = 4
    quarter, width = direct_sum.shape
    feats = width // n
    g = jnp.concatenate([grads[2 * h] + grads[2 * h + 1] for h in range(n)], axis=0).T
    g_high, g_low = halves(g)
    mine = pl.ds(pl.multiple_of(lax.rem(z, 2) * quarter, quarter), quarter)
    here = z // 2 == half
    for k, f in enumerate((f0, f1, f2, f3)):
        column = lax.rem(z + k, n) * feats
        at = pl.ds(pl.multiple_of(column, feats), feats)
        w_high = w3[:, at]
        w_low = w3[:, pl.ds(pl.multiple_of(width + column, feats), feats)]
        f[...] = mm(g_high, w_high) + mm(g_low, w_high) + mm(g_high, w_low)
        f[mine, :] += jnp.where(here, direct_sum[:, at], 0.0)


HD = 64
NBLOCKS = 16
GROUP = 4
SCALE = 1.0 / math.sqrt(HD)


def shape(dims, kind=F32):
    return jax.ShapeDtypeStruct(dims, kind)


def shards(packets, baseline, w_query, w_key, w_value, w_out, gain, probe, sessions, block_lists):
    tokens, feats = packets.shape
    width = w_query.shape[1]
    n = lax.axis_size("head")
    heads = feats // HD
    members = lax.axis_size("ctx")
    quarter = tokens // n
    z = lax.axis_index("head")
    z_ref = z.reshape(1)
    slab = feats // members
    part = 3 * HD

    travel = packets - baseline
    half = tokens // 2
    own = jnp.concatenate([baseline + alpha * travel for alpha in ALPHAS])
    ups, downs = [own], [own]
    for step in range(1, n):
        ups.append(shift(ups[-1], 1, step - 1, n - 2))
        downs.append(shift(downs[-1], -1, 1, n - step))
    gathered = [own] + ups[1:] + downs[1:]

    slab_rows = lax.dynamic_slice_in_dim(w_out, lax.axis_index("ctx") * slab, slab, 0)
    listed = block_lists.reshape(1, -1).astype(F32)
    listed = jnp.pad(listed, ((0, 7), (0, width - listed.shape[1])))
    slabs = lax.all_gather(jnp.concatenate([slab_rows, listed]), "head", axis=0)
    slabs = lax.all_gather(slabs, "ctx", axis=0)
    lists = slabs[:, 0, slab, : block_lists.size].astype(jnp.int32).reshape(-1, KVB)
    out_high, out_low = call(
        split_kernel, 24, (shape((width, width), BF16),) * 2, [], 0, slabs
    )
    weights = jnp.concatenate(
        [w.reshape(heads, HD, width) for w in (w_query, w_key, w_value)], axis=1
    ).reshape(heads * part, width)
    high, low = halves_outside(weights)
    w3 = jnp.concatenate([high, low, high], axis=1)
    qkv, rows = call(
        project_kernel, 20,
        (shape((members, part, tokens)), shape((2, quarter, width))),
        [pltpu.VMEM((2 * tokens, 3 * width), BF16)],
        1, z_ref, w3, *gathered,
    )
    qkv, upstream = lax.optimization_barrier((qkv, probe * gain))
    qkv = lax.all_to_all(qkv, "ctx", 0, 0, tiled=True)
    upstream = lax.all_gather(upstream, "head", axis=0)

    blocks = members * tokens // BLK
    everyone = members * n
    session_row = sessions.reshape(blocks, BLK)
    session_col = sessions.reshape(blocks, BLK, 1)
    mixed, folded, p_high, p_low = call(
        attend_kernel, 20,
        (
            shape((blocks, HD, BLK)),
            shape((everyone, HD // 2, BLK)),
            shape((blocks, KVB * BLK, BLK), BF16),
            shape((blocks, KVB * BLK, BLK), BF16),
        ),
        [
            pltpu.VMEM((blocks, part, BLK), BF16),
            pltpu.VMEM((blocks, BLK, part), BF16),
            pltpu.VMEM((blocks, 2 * HD, BLK), BF16),
        ],
        1, lists, session_col, session_row, qkv, streamed_out=(2, 3),
    )
    folded = lax.all_to_all(folded, ("ctx", "head"), 0, 0, tiled=True)
    grad, direct_sum = call(
        norm_kernel, 20,
        (shape((everyone, HD // 2, BLK)), shape((quarter, width))),
        [pltpu.VMEM((quarter, width), F32), pltpu.VMEM((width, 2 * quarter), F32)],
        1, z_ref, out_high, out_low, rows, upstream, folded,
    )
    grad = lax.all_to_all(grad, ("ctx", "head"), 0, 0, tiled=True)
    grad_qkv = call(
        attend_back_kernel, 20,
        (shape((members, part, half)),) * 2,
        [
            pltpu.VMEM((blocks, 2 * HD, BLK), BF16),
            pltpu.VMEM((blocks, 2 * HD, BLK), BF16),
            pltpu.VMEM((blocks, BLK, part), BF16),
            pltpu.VMEM((blocks, 2 * HD, BLK), F32),
        ],
        1, lists, qkv, p_high, p_low, grad, mixed, streamed_in=(2, 3),
    )
    grad_qkv = [lax.all_to_all(g, "ctx", 0, 0, tiled=True) for g in grad_qkv]
    totals = []
    for e in range(2):
        parts = exchange(
            call(
                functools.partial(input_kernel, e), 16,
                (shape((half, feats)),) * n,
                [],
                1, z_ref, w3, grad_qkv[e], direct_sum,
            )
        )
        totals.append(parts[0] + parts[1] + parts[2] + parts[3])
    return travel * jnp.concatenate(totals) / len(ALPHAS)


def pick_shards(mesh):
    members, n = mesh.shape["ctx"], mesh.shape["head"]
    return shards if n == 4 and members == 2 * HEADS // n else general_shards


def solution(mesh):
    return jax.shard_map(
        pick_shards(mesh),
        mesh=mesh,
        in_specs=(
            P("ctx", "head"),
            P("ctx", "head"),
            P("head", None),
            P("head", None),
            P("head", None),
            P("head", None),
            P("head"),
            P("ctx", "head"),
            P(),
            P("ctx", None),
        ),
        out_specs=P("ctx", "head"),
        check_vma=False,
    )
```

```python
import functools
import math

import jax
import jax.numpy as jnp
from jax import lax
from jax.experimental import pallas as pl
from jax.experimental.pallas import tpu as pltpu
from jax.sharding import PartitionSpec as P

HEADS = 16
BLK = 128
KVB = 5
REACH = 2


ALPHAS = (0.25, 0.75)
EPS = 1e-05
HIGHEST = lax.Precision.HIGHEST


def from_behind(x, axis, by):
    size = lax.axis_size(axis)
    pairs = [(i, i + by) for i in range(size) if 0 <= i + by < size]
    return lax.ppermute(x, axis, pairs)


def integrate(points, weights_qkv, w_out, gain, probe, sessions, block_lists):
    steps, rows, feats = points.shape
    width = weights_qkv.shape[1]
    head_dim = width // HEADS
    local_heads = feats // head_dim
    blocks = rows // BLK
    where = lax.axis_index("ctx")
    first = (where - REACH) * blocks
    slots = (2 * REACH + 1) * blocks
    scale = 1.0 / math.sqrt(head_dim)
    part_cols = weights_qkv
    qkv = jnp.einsum(
        "std,ed->ste",
        lax.all_gather(points, "head", axis=2, tiled=True),
        part_cols,
        precision=HIGHEST,
    )
    query = qkv[:, :, :feats]
    pairs = qkv[:, :, feats:]
    below = []
    above = []
    for dist in range(1, REACH + 1):
        below.append(from_behind(pairs, "ctx", dist))
        above.append(from_behind(pairs, "ctx", -dist))
    window = jnp.concatenate(below[::-1] + [pairs] + above, axis=1)
    local = (block_lists - first).reshape(-1)
    tiles = window.reshape(steps, slots, BLK, 2 * feats)
    picked = jnp.take(tiles, local, axis=1).reshape(
        steps, blocks, KVB * BLK, 2, local_heads, head_dim
    )
    keys = picked[:, :, :, 0]
    values = picked[:, :, :, 1]
    token_index = block_lists[:, :, None] * BLK + jnp.arange(BLK, dtype=jnp.int32)[None, None, :]
    key_sessions = jnp.take(sessions, token_index.reshape(blocks, KVB * BLK), axis=0)
    query_sessions = lax.dynamic_slice_in_dim(sessions, where * rows, rows, 0).reshape(blocks, BLK)
    keep = query_sessions[:, :, None] == key_sessions[:, None, :]
    query_heads = query.reshape(steps, blocks, BLK, local_heads, head_dim)
    scores = jnp.einsum("sbqhd,sbkhd->sbhqk", query_heads, keys, precision=HIGHEST) * scale
    scores = jnp.where(keep[None, :, None], scores, -1e30)
    top = jnp.max(scores, axis=-1, keepdims=True)
    expo = jnp.exp(scores - top)
    probs = expo / jnp.sum(expo, axis=-1, keepdims=True)
    mixed = jnp.einsum("sbhqk,sbkhd->sbqhd", probs, values, precision=HIGHEST)
    heads_out = mixed.reshape(steps, rows, feats)
    part_cols = w_out
    projected = jnp.einsum(
        "std,ed->ste",
        lax.all_gather(heads_out, "head", axis=2, tiled=True),
        part_cols,
        precision=HIGHEST,
    )
    summed = points + projected
    first_sum, second_sum = lax.psum(
        (jnp.sum(summed, axis=-1), jnp.sum(summed * summed, axis=-1)), "head"
    )
    mean = first_sum / width
    inverse = lax.rsqrt(second_sum / width - mean * mean + EPS)
    normed = (summed - mean[..., None]) * inverse[..., None]
    upstream = probe * gain
    upstream_sum, upstream_dot = lax.psum(
        (jnp.sum(upstream, axis=-1), jnp.sum(upstream * normed, axis=-1)), "head"
    )
    direct = inverse[..., None] * (
        upstream - upstream_sum[..., None] / width - normed * (upstream_dot / width)[..., None]
    )
    partial_heads = jnp.einsum("ste,ed->std", direct, w_out, precision=HIGHEST)
    grad_heads = lax.psum_scatter(partial_heads, "head", scatter_dimension=2, tiled=True)
    grad_mixed = grad_heads.reshape(steps, blocks, BLK, local_heads, head_dim)
    delta = jnp.einsum("sbqhd,sbqhd->sbhq", grad_mixed, mixed, precision=HIGHEST)
    grad_probs = jnp.einsum("sbqhd,sbkhd->sbhqk", grad_mixed, values, precision=HIGHEST)
    grad_scores = probs * (grad_probs - delta[..., None]) * scale
    grad_query = jnp.einsum("sbhqk,sbkhd->sbqhd", grad_scores, keys, precision=HIGHEST)
    grad_keys = jnp.einsum("sbhqk,sbqhd->sbkhd", grad_scores, query_heads, precision=HIGHEST)
    grad_values = jnp.einsum("sbhqk,sbqhd->sbkhd", probs, grad_mixed, precision=HIGHEST)
    grad_picked = jnp.stack([grad_keys, grad_values], axis=3).reshape(
        steps, blocks * KVB, BLK, 2 * feats
    )
    selector = (local[:, None] == jnp.arange(slots, dtype=jnp.int32)[None, :]).astype(jnp.float32)
    grad_window = jnp.einsum("snlc,nw->swlc", grad_picked, selector, precision=HIGHEST).reshape(
        steps, slots * BLK, 2 * feats
    )
    owned = grad_window[:, REACH * rows : (REACH + 1) * rows]
    for dist in range(1, REACH + 1):
        upper = grad_window[:, (REACH + dist) * rows : (REACH + dist + 1) * rows]
        lower = grad_window[:, (REACH - dist) * rows : (REACH - dist + 1) * rows]
        owned = owned + from_behind(upper, "ctx", dist)
        owned = owned + from_behind(lower, "ctx", -dist)
    grad_qkv = jnp.concatenate([grad_query.reshape(steps, rows, feats), owned], axis=-1)
    partial_input = jnp.einsum("ste,ed->std", grad_qkv, weights_qkv, precision=HIGHEST)
    return (direct, partial_input)


def collect_inputs(partial_input):
    return lax.psum_scatter(partial_input, "head", scatter_dimension=2, tiled=True)


def general_shards(packets, baseline, w_query, w_key, w_value, w_out, gain, probe, sessions, block_lists):
    weights_qkv = jnp.concatenate([w_query, w_key, w_value], axis=0)
    travel = packets - baseline
    points = jnp.stack([baseline + alpha * travel for alpha in ALPHAS])
    passes = [
        integrate(points[index : index + 1], weights_qkv, w_out, gain, probe, sessions, block_lists)
        for index in range(len(ALPHAS))
    ]
    grads = jnp.zeros_like(packets)
    for direct, partial_input in passes:
        grads = grads + direct.sum(axis=0) + collect_inputs(partial_input).sum(axis=0)
    return travel * grads / len(ALPHAS)


F32 = jnp.float32
BF16 = jnp.bfloat16
MIB = 1 << 20
VM = pl.BlockSpec(memory_space=pltpu.VMEM)
SM = pl.BlockSpec(memory_space=pltpu.SMEM)


def halves(x):
    high = x.astype(BF16)
    low = (x - high.astype(F32)).astype(BF16)
    return high, low


def halves_outside(x):
    rounded = lax.reduce_precision(x, 8, 7)
    return rounded.astype(BF16), (x - rounded).astype(BF16)


def mm(a, b):
    return lax.dot_general(a, b, (((1,), (0,)), ((), ())), preferred_element_type=F32)


def mm_nt(a, b):
    return lax.dot_general(a, b, (((1,), (1,)), ((), ())), preferred_element_type=F32)


def call(kernel, mib, outs, scratch, n_smem, *args, streamed_in=(), streamed_out=()):
    grid = (NBLOCKS // GROUP,) if streamed_in or streamed_out else ()
    one_in = pl.BlockSpec((GROUP, KVB * BLK, BLK), lambda c: (c, 0, 0))
    in_specs = [SM] * n_smem + [VM] * (len(args) - n_smem)
    for i in streamed_in:
        in_specs[i] = one_in
    out_specs = jax.tree.map(lambda _: VM, outs)
    if streamed_out:
        out_specs = tuple(one_in if i in streamed_out else VM for i in range(len(outs)))
    return pl.pallas_call(
        kernel,
        out_shape=outs,
        grid=grid,
        in_specs=in_specs,
        out_specs=out_specs,
        scratch_shapes=scratch,
        compiler_params=pltpu.CompilerParams(vmem_limit_bytes=mib * MIB),
    )(*args)


def shift(x, by, low, high):
    return lax.ppermute(x, "head", [(i, i + by) for i in range(low, high + 1)])


def rotate(x, by):
    size = lax.axis_size("head")
    return lax.ppermute(x, "head", [(i, (i + by) % size) for i in range(size)])


def exchange(pieces):
    return [pieces[0]] + [rotate(pieces[k], k) for k in range(1, len(pieces))]


def weights_kernel(w_query, w_key, w_value, high, low):
    for h in range(w_query.shape[0] // HD):
        for i, w in enumerate((w_query, w_key, w_value)):
            at = slice((3 * h + i) * HD, (3 * h + i + 1) * HD)
            high[at], low[at] = halves(w[h * HD : (h + 1) * HD])


def project_kernel(
    z_ref, w_high, w_low, listed, own, u1, u2, u3, d1, d2, d3, out, rows, x_high, x_low
):
    ups, downs = (u1, u2, u3), (d1, d2, d3)
    z = z_ref[0]
    n = 4
    quarter, width = rows.shape[1:]
    both, feats = own.shape
    tokens = both // 2
    for k in range(n):
        column = pl.multiple_of(lax.rem(z - k + n, n) * feats, feats)
        for s in range(2):
            span = pl.ds(s * tokens, tokens)
            if k == 0:
                x = own[span]
            else:
                x = ups[k - 1][span] + downs[n - k - 1][span]
            for q in range(n):
                @pl.when(z == q)
                def _(x=x, q=q, s=s):
                    rows[s, :, pl.ds(column, feats)] = x[q * quarter : (q + 1) * quarter]
            high, low = halves(x)
            x_high[span, pl.ds(column, feats)] = high
            x_low[span, pl.ds(column, feats)] = low
    part = w_high.shape[0] // n
    for h in range(n):
        at = slice(h * part, (h + 1) * part)
        r = mm_nt(w_high[at], x_high[...]) + mm_nt(w_low[at], x_high[...])
        r = r + mm_nt(w_high[at], x_low[...])
        for s in range(2):
            out[2 * h + s, :part] = r[:, s * tokens : (s + 1) * tokens]
            out[2 * h + s, part:] = listed[...]


def fold(x):
    top, bottom = x[: HD // 2], x[HD // 2 :]
    left = lax.broadcasted_iota(jnp.int32, top.shape, 1) < HD
    return jnp.where(left, top, pltpu.roll(bottom, HD, 1)), jnp.where(
        left, pltpu.roll(top, HD, 1), bottom
    )


def unfold(first, second):
    left = lax.broadcasted_iota(jnp.int32, first.shape, 1) < HD
    top = jnp.where(left, first, pltpu.roll(second, HD, 1))
    bottom = jnp.where(left, pltpu.roll(first, HD, 1), second)
    return jnp.concatenate([top, bottom], axis=0)


def attend_kernel(
    lists, session_row, qkv, mixed, folded, p_high, p_low, q3, k3, v2, session_col
):
    c = pl.program_id(0)

    @pl.when(c == 0)
    def _():
        columns = session_row[...].T
        for b in range(NBLOCKS):
            t = qkv[b // 2, : 3 * HD, (b % 2) * BLK : (b % 2 + 1) * BLK]
            q_high, q_low = halves(t[:HD] * SCALE)
            session_col[b] = columns[:, b : b + 1]
            q3[b] = jnp.concatenate([q_high, q_high, q_low], axis=0)
            k_high, k_low = halves(t[HD : 2 * HD].T)
            k3[b] = jnp.concatenate([k_high, k_low, k_high], axis=1)
            v_high, v_low = halves(t[2 * HD :])
            v2[b] = jnp.concatenate([v_high, v_low], axis=0)

    blocks = [GROUP * c + e for e in range(GROUP)]
    scores = []
    for b in blocks:
        mine = session_row[pl.ds(b, 1), :]
        tiles = []
        for j in range(KVB):
            other = lists[b, j]
            s = mm(k3[other], q3[b])
            tiles.append(jnp.where(session_col[other] == mine, s, -1e30))
        scores.append(jnp.concatenate(tiles, axis=0))
    tops = [jnp.max(s, axis=0, keepdims=True) for s in scores]
    expos = [jnp.exp(s - top) for s, top in zip(scores, tops)]
    scales = [1.0 / jnp.sum(expo, axis=0, keepdims=True) for expo in expos]
    for b, e, expo, each in zip(blocks, range(GROUP), expos, scales):
        high, low = halves(expo * each)
        p_high[e] = high
        p_low[e] = low
        values = jnp.concatenate([v2[lists[b, j]] for j in range(KVB)], axis=1)
        both = mm(values, high)
        block = both[:HD] + both[HD:] + mm(values[:HD], low)
        mixed[b] = block
        folded[2 * b], folded[2 * b + 1] = fold(block)


def attend_back_kernel(
    lists, qkv, p_high, p_low, grad, mixed, out0, out1, q2, k2, v3, acc
):
    out = (out0, out1)
    c = pl.program_id(0)

    @pl.when(c == 0)
    def _():
        for b in range(NBLOCKS):
            t = qkv[b // 2, : 3 * HD, (b % 2) * BLK : (b % 2 + 1) * BLK]
            q_high, q_low = halves(t[:HD])
            q2[b] = jnp.concatenate([q_high, q_low], axis=0)
            k_high, k_low = halves(t[HD : 2 * HD])
            k2[b] = jnp.concatenate([k_high, k_low], axis=0)
            v_high, v_low = halves(t[2 * HD :].T)
            v3[b] = jnp.concatenate([v_high, v_low, v_high], axis=1)
        acc[...] = jnp.zeros_like(acc)

    blocks = [GROUP * c + e for e in range(GROUP)]
    grads = [unfold(grad[2 * b], grad[2 * b + 1]) for b in blocks]
    parts = [halves(g) for g in grads]
    probs_grads = []
    for b, (g_high, g_low) in zip(blocks, parts):
        g3 = jnp.concatenate([g_high, g_high, g_low], axis=0)
        probs_grads.append(
            jnp.concatenate([mm(v3[lists[b, j]], g3) for j in range(KVB)], axis=0)
        )
    added = []
    for e, b in enumerate(blocks):
        delta = jnp.sum(grads[e] * mixed[b], axis=0, keepdims=True)
        g2 = jnp.concatenate(parts[e], axis=0)
        ph, pw = p_high[e], p_low[e]
        probs = ph.astype(F32) + pw.astype(F32)
        s_high, s_low = halves(probs * (probs_grads[e] - delta) * SCALE)
        keys = jnp.concatenate([k2[lists[b, j]] for j in range(KVB)], axis=1)
        both = mm(keys, s_high)
        out[e % 2][(GROUP // 2) * c + e // 2, 0:HD] = (
            both[:HD] + both[HD:] + mm(keys[:HD], s_low)
        )
        query = q2[b]
        both = mm_nt(query, s_high)
        grad_keys = both[:HD] + both[HD:] + mm_nt(query[:HD], s_low)
        both = mm_nt(g2, ph)
        grad_values = both[:HD] + both[HD:] + mm_nt(g2[:HD], pw)
        added.append(jnp.concatenate([grad_keys, grad_values], axis=0))
    for b, both in zip(blocks, added):
        for j in range(KVB):
            acc[lists[b, j]] += both[:, j * BLK : (j + 1) * BLK]

    @pl.when(c == NBLOCKS // GROUP - 1)
    def _():
        for b in range(NBLOCKS):
            out[b % 2][b // 2, HD : 3 * HD] = acc[b]


def split_kernel(whole, high, low):
    high[...], low[...] = halves(whole[...])


def norm_kernel(
    w_high, w_low, rows, ups, pieces, out, direct_sum, upstream, mixed
):
    n = 4
    quarter, width = direct_sum.shape
    feats = width // n
    for k in range(n):
        upstream[:, k * feats : (k + 1) * feats] = ups[k]
    for group in range(n):
        for h in range(n):
            at = group * feats + h * HD
            mixed[at : at + HD, :] = unfold(pieces[2 * h * n + group], pieces[(2 * h + 1) * n + group])
    m_high, m_low = halves(mixed[...].T)
    projected = mm_nt(m_high, w_high[...]) + mm_nt(m_low, w_high[...]) + mm_nt(m_high, w_low[...])
    summed = rows[...].reshape(2 * quarter, width) + projected
    mean = jnp.sum(summed, axis=-1, keepdims=True) / width
    second = jnp.sum(summed * summed, axis=-1, keepdims=True) / width
    inverse = lax.rsqrt(second - mean * mean + EPS)
    normed = (summed - mean) * inverse
    up = jnp.concatenate([upstream[...], upstream[...]], axis=0)
    up_mean = jnp.sum(up, axis=-1, keepdims=True) / width
    up_dot = jnp.sum(up * normed, axis=-1, keepdims=True) / width
    direct = inverse * (up - up_mean - normed * up_dot)
    direct_sum[...] = direct[:quarter] + direct[quarter:]
    d_high, d_low = halves(direct)
    grad = mm(d_high, w_high[...]) + mm(d_low, w_high[...]) + mm(d_high, w_low[...])
    grad = grad.T
    for group in range(n):
        for h in range(n):
            at = group * feats + h * HD
            out[2 * h * n + group], out[(2 * h + 1) * n + group] = fold(grad[at : at + HD])


def input_kernel(half, z_ref, weight_high, weight_low, grads, direct_sum, f0, f1, f2, f3):
    z = z_ref[0]
    n = 4
    quarter, width = direct_sum.shape
    feats = width // n
    g = jnp.concatenate([grads[2 * h] + grads[2 * h + 1] for h in range(n)], axis=0).T
    g_high, g_low = halves(g)
    mine = pl.ds(pl.multiple_of(lax.rem(z, 2) * quarter, quarter), quarter)
    here = z // 2 == half
    for k, f in enumerate((f0, f1, f2, f3)):
        column = lax.rem(z + k, n) * feats
        at = pl.ds(pl.multiple_of(column, feats), feats)
        w_high, w_low = weight_high[:, at], weight_low[:, at]
        f[...] = mm(g_high, w_high) + mm(g_low, w_high) + mm(g_high, w_low)
        f[mine, :] += jnp.where(here, direct_sum[:, at], 0.0)


HD = 64
NBLOCKS = 16
GROUP = 4
SCALE = 1.0 / math.sqrt(HD)


def shape(dims, kind=F32):
    return jax.ShapeDtypeStruct(dims, kind)


def in_hbm(dims, kind=F32):
    return pltpu.HBM(dims, kind)


def shards(packets, baseline, w_query, w_key, w_value, w_out, gain, probe, sessions, block_lists):
    tokens, feats = packets.shape
    width = w_query.shape[1]
    n = lax.axis_size("head")
    heads = feats // HD
    members = lax.axis_size("ctx")
    quarter = tokens // n
    z = lax.axis_index("head")
    z_ref = z.reshape(1)
    slab = feats // members
    part = 3 * HD

    travel = packets - baseline
    half = tokens // 2
    own = jnp.concatenate([baseline + alpha * travel for alpha in ALPHAS])
    ups, downs = [own], [own]
    for step in range(1, n):
        ups.append(shift(ups[-1], 1, step - 1, n - 2))
        downs.append(shift(downs[-1], -1, 1, n - step))
    gathered = [own] + ups[1:] + downs[1:]

    slab_rows = lax.dynamic_slice_in_dim(w_out, lax.axis_index("ctx") * slab, slab, 0)
    whole_out = lax.all_gather(slab_rows, ("head", "ctx"), axis=0, tiled=True)
    listed = block_lists.reshape(1, -1).astype(F32)
    listed = jnp.pad(listed, ((0, 7), (0, tokens - listed.shape[1])))
    high, low = call(
        weights_kernel, 16, (in_hbm((heads * part, width), BF16),) * 2, [], 0,
        w_query, w_key, w_value,
    )
    qkv, rows = call(
        project_kernel, 20,
        (in_hbm((members, part + 8, tokens)), in_hbm((2, quarter, width))),
        [pltpu.VMEM((2 * tokens, width), BF16)] * 2,
        1, z_ref, high, low, listed, *gathered,
    )
    qkv, upstream = lax.optimization_barrier((qkv, probe * gain))
    upstream, whole_out = lax.optimization_barrier((upstream, whole_out))
    qkv = lax.all_to_all(qkv, "ctx", 0, 0, tiled=True)
    lists = qkv[:, part, : block_lists.size].astype(jnp.int32).reshape(-1, KVB)
    upstream = lax.all_gather(upstream, "head", axis=0)
    upstream = lax.dynamic_slice_in_dim(upstream, z * quarter, quarter, 1)

    out_high, out_low = call(
        split_kernel, 24, (in_hbm((width, width), BF16),) * 2, [], 0, whole_out
    )
    blocks = members * tokens // BLK
    everyone = members * n
    session_row = sessions.astype(F32).reshape(blocks, BLK)
    mixed, folded, p_high, p_low = call(
        attend_kernel, 20,
        (
            in_hbm((blocks, HD, BLK)),
            in_hbm((everyone, HD // 2, BLK)),
            in_hbm((blocks, KVB * BLK, BLK), BF16),
            in_hbm((blocks, KVB * BLK, BLK), BF16),
        ),
        [
            pltpu.VMEM((blocks, part, BLK), BF16),
            pltpu.VMEM((blocks, BLK, part), BF16),
            pltpu.VMEM((blocks, 2 * HD, BLK), BF16),
            pltpu.VMEM((blocks, BLK, 1), F32),
        ],
        1, lists, session_row, qkv, streamed_out=(2, 3),
    )
    folded = lax.all_to_all(folded, ("ctx", "head"), 0, 0, tiled=True)
    grad, direct_sum = call(
        norm_kernel, 20,
        (shape((everyone, HD // 2, BLK)), shape((quarter, width))),
        [pltpu.VMEM((quarter, width), F32), pltpu.VMEM((width, 2 * quarter), F32)],
        0, out_high, out_low, rows, upstream, folded,
    )
    grad = lax.all_to_all(grad, ("ctx", "head"), 0, 0, tiled=True)
    grad_qkv = call(
        attend_back_kernel, 20,
        (shape((members, part, half)),) * 2,
        [
            pltpu.VMEM((blocks, 2 * HD, BLK), BF16),
            pltpu.VMEM((blocks, 2 * HD, BLK), BF16),
            pltpu.VMEM((blocks, BLK, part), BF16),
            pltpu.VMEM((blocks, 2 * HD, BLK), F32),
        ],
        1, lists, qkv, p_high, p_low, grad, mixed, streamed_in=(2, 3),
    )
    grad_qkv = [lax.all_to_all(g, "ctx", 0, 0, tiled=True) for g in grad_qkv]
    totals = []
    for e in range(2):
        parts = exchange(
            call(
                functools.partial(input_kernel, e), 16,
                (shape((half, feats)),) * n,
                [],
                1, z_ref, high, low, grad_qkv[e], direct_sum,
            )
        )
        totals.append(parts[0] + parts[1] + parts[2] + parts[3])
    return travel * jnp.concatenate(totals) / len(ALPHAS)


def pick_shards(mesh):
    members, n = mesh.shape["ctx"], mesh.shape["head"]
    return shards if n == 4 and members == 2 * HEADS // n else general_shards


def solution(mesh):
    return jax.shard_map(
        pick_shards(mesh),
        mesh=mesh,
        in_specs=(
            P("ctx", "head"),
            P("ctx", "head"),
            P("head", None),
            P("head", None),
            P("head", None),
            P("head", None),
            P("head"),
            P("ctx", "head"),
            P(),
            P("ctx", None),
        ),
        out_specs=P("ctx", "head"),
        check_vma=False,
    )
```

```python
import functools
import math

import jax
import jax.numpy as jnp
from jax import lax
from jax.experimental import pallas as pl
from jax.experimental.pallas import tpu as pltpu
from jax.sharding import PartitionSpec as P

HEADS = 16
BLK = 128
KVB = 5
REACH = 2


ALPHAS = (0.25, 0.75)
EPS = 1e-05
HIGHEST = lax.Precision.HIGHEST


def from_behind(x, axis, by):
    size = lax.axis_size(axis)
    pairs = [(i, i + by) for i in range(size) if 0 <= i + by < size]
    return lax.ppermute(x, axis, pairs)


def integrate(points, weights_qkv, w_out, gain, probe, sessions, block_lists):
    steps, rows, feats = points.shape
    width = weights_qkv.shape[1]
    head_dim = width // HEADS
    local_heads = feats // head_dim
    blocks = rows // BLK
    where = lax.axis_index("ctx")
    first = (where - REACH) * blocks
    slots = (2 * REACH + 1) * blocks
    scale = 1.0 / math.sqrt(head_dim)
    part_cols = weights_qkv
    qkv = jnp.einsum(
        "std,ed->ste",
        lax.all_gather(points, "head", axis=2, tiled=True),
        part_cols,
        precision=HIGHEST,
    )
    query = qkv[:, :, :feats]
    pairs = qkv[:, :, feats:]
    below = []
    above = []
    for dist in range(1, REACH + 1):
        below.append(from_behind(pairs, "ctx", dist))
        above.append(from_behind(pairs, "ctx", -dist))
    window = jnp.concatenate(below[::-1] + [pairs] + above, axis=1)
    local = (block_lists - first).reshape(-1)
    tiles = window.reshape(steps, slots, BLK, 2 * feats)
    picked = jnp.take(tiles, local, axis=1).reshape(
        steps, blocks, KVB * BLK, 2, local_heads, head_dim
    )
    keys = picked[:, :, :, 0]
    values = picked[:, :, :, 1]
    token_index = block_lists[:, :, None] * BLK + jnp.arange(BLK, dtype=jnp.int32)[None, None, :]
    key_sessions = jnp.take(sessions, token_index.reshape(blocks, KVB * BLK), axis=0)
    query_sessions = lax.dynamic_slice_in_dim(sessions, where * rows, rows, 0).reshape(blocks, BLK)
    keep = query_sessions[:, :, None] == key_sessions[:, None, :]
    query_heads = query.reshape(steps, blocks, BLK, local_heads, head_dim)
    scores = jnp.einsum("sbqhd,sbkhd->sbhqk", query_heads, keys, precision=HIGHEST) * scale
    scores = jnp.where(keep[None, :, None], scores, -1e30)
    top = jnp.max(scores, axis=-1, keepdims=True)
    expo = jnp.exp(scores - top)
    probs = expo / jnp.sum(expo, axis=-1, keepdims=True)
    mixed = jnp.einsum("sbhqk,sbkhd->sbqhd", probs, values, precision=HIGHEST)
    heads_out = mixed.reshape(steps, rows, feats)
    part_cols = w_out
    projected = jnp.einsum(
        "std,ed->ste",
        lax.all_gather(heads_out, "head", axis=2, tiled=True),
        part_cols,
        precision=HIGHEST,
    )
    summed = points + projected
    first_sum, second_sum = lax.psum(
        (jnp.sum(summed, axis=-1), jnp.sum(summed * summed, axis=-1)), "head"
    )
    mean = first_sum / width
    inverse = lax.rsqrt(second_sum / width - mean * mean + EPS)
    normed = (summed - mean[..., None]) * inverse[..., None]
    upstream = probe * gain
    upstream_sum, upstream_dot = lax.psum(
        (jnp.sum(upstream, axis=-1), jnp.sum(upstream * normed, axis=-1)), "head"
    )
    direct = inverse[..., None] * (
        upstream - upstream_sum[..., None] / width - normed * (upstream_dot / width)[..., None]
    )
    partial_heads = jnp.einsum("ste,ed->std", direct, w_out, precision=HIGHEST)
    grad_heads = lax.psum_scatter(partial_heads, "head", scatter_dimension=2, tiled=True)
    grad_mixed = grad_heads.reshape(steps, blocks, BLK, local_heads, head_dim)
    delta = jnp.einsum("sbqhd,sbqhd->sbhq", grad_mixed, mixed, precision=HIGHEST)
    grad_probs = jnp.einsum("sbqhd,sbkhd->sbhqk", grad_mixed, values, precision=HIGHEST)
    grad_scores = probs * (grad_probs - delta[..., None]) * scale
    grad_query = jnp.einsum("sbhqk,sbkhd->sbqhd", grad_scores, keys, precision=HIGHEST)
    grad_keys = jnp.einsum("sbhqk,sbqhd->sbkhd", grad_scores, query_heads, precision=HIGHEST)
    grad_values = jnp.einsum("sbhqk,sbqhd->sbkhd", probs, grad_mixed, precision=HIGHEST)
    grad_picked = jnp.stack([grad_keys, grad_values], axis=3).reshape(
        steps, blocks * KVB, BLK, 2 * feats
    )
    selector = (local[:, None] == jnp.arange(slots, dtype=jnp.int32)[None, :]).astype(jnp.float32)
    grad_window = jnp.einsum("snlc,nw->swlc", grad_picked, selector, precision=HIGHEST).reshape(
        steps, slots * BLK, 2 * feats
    )
    owned = grad_window[:, REACH * rows : (REACH + 1) * rows]
    for dist in range(1, REACH + 1):
        upper = grad_window[:, (REACH + dist) * rows : (REACH + dist + 1) * rows]
        lower = grad_window[:, (REACH - dist) * rows : (REACH - dist + 1) * rows]
        owned = owned + from_behind(upper, "ctx", dist)
        owned = owned + from_behind(lower, "ctx", -dist)
    grad_qkv = jnp.concatenate([grad_query.reshape(steps, rows, feats), owned], axis=-1)
    partial_input = jnp.einsum("ste,ed->std", grad_qkv, weights_qkv, precision=HIGHEST)
    return (direct, partial_input)


def collect_inputs(partial_input):
    return lax.psum_scatter(partial_input, "head", scatter_dimension=2, tiled=True)


def general_shards(packets, baseline, w_query, w_key, w_value, w_out, gain, probe, sessions, block_lists):
    weights_qkv = jnp.concatenate([w_query, w_key, w_value], axis=0)
    travel = packets - baseline
    points = jnp.stack([baseline + alpha * travel for alpha in ALPHAS])
    passes = [
        integrate(points[index : index + 1], weights_qkv, w_out, gain, probe, sessions, block_lists)
        for index in range(len(ALPHAS))
    ]
    grads = jnp.zeros_like(packets)
    for direct, partial_input in passes:
        grads = grads + direct.sum(axis=0) + collect_inputs(partial_input).sum(axis=0)
    return travel * grads / len(ALPHAS)


F32 = jnp.float32
BF16 = jnp.bfloat16
MIB = 1 << 20
VM = pl.BlockSpec(memory_space=pltpu.VMEM)
SM = pl.BlockSpec(memory_space=pltpu.SMEM)


def halves(x):
    high = x.astype(BF16)
    low = (x - high.astype(F32)).astype(BF16)
    return high, low


def halves_outside(x):
    rounded = lax.reduce_precision(x, 8, 7)
    return rounded.astype(BF16), (x - rounded).astype(BF16)


def mm(a, b):
    return lax.dot_general(a, b, (((1,), (0,)), ((), ())), preferred_element_type=F32)


def mm_nt(a, b):
    return lax.dot_general(a, b, (((1,), (1,)), ((), ())), preferred_element_type=F32)


def call(kernel, mib, outs, scratch, n_smem, *args, streamed_in=(), streamed_out=(), parked=()):
    grid = (NBLOCKS // GROUP,) if streamed_in or streamed_out else ()
    one_in = pl.BlockSpec((GROUP, KVB * BLK, BLK), lambda c: (c, 0, 0))
    in_specs = [SM] * n_smem + [VM] * (len(args) - n_smem)
    for i in streamed_in:
        in_specs[i] = one_in
    for i in parked:
        in_specs[i] = pl.BlockSpec(memory_space=pl.ANY)
    args = [
        pltpu.with_memory_space_constraint(x, pltpu.HBM) if i in parked + streamed_in else x
        for i, x in enumerate(args)
    ]
    out_specs = jax.tree.map(lambda _: VM, outs)
    if streamed_out:
        out_specs = tuple(one_in if i in streamed_out else VM for i in range(len(outs)))
    return pl.pallas_call(
        kernel,
        out_shape=outs,
        grid=grid,
        in_specs=in_specs,
        out_specs=out_specs,
        scratch_shapes=scratch,
        compiler_params=pltpu.CompilerParams(vmem_limit_bytes=mib * MIB),
    )(*args)


def fetch(sources, places, arrived):
    copies = [
        pltpu.make_async_copy(source, place, arrived.at[i])
        for i, (source, place) in enumerate(zip(sources, places))
    ]
    for copy in copies:
        copy.start()
    return copies


def shift(x, by, low, high):
    return lax.ppermute(x, "head", [(i, i + by) for i in range(low, high + 1)])


def rotate(x, by):
    size = lax.axis_size("head")
    return lax.ppermute(x, "head", [(i, (i + by) % size) for i in range(size)])


def exchange(pieces):
    return [pieces[0]] + [rotate(pieces[k], k) for k in range(1, len(pieces))]


def weights_kernel(w_query, w_key, w_value, high, low):
    for h in range(w_query.shape[0] // HD):
        for i, w in enumerate((w_query, w_key, w_value)):
            at = slice((3 * h + i) * HD, (3 * h + i + 1) * HD)
            high[at], low[at] = halves(w[h * HD : (h + 1) * HD])


def project_kernel(
    z_ref, parked_high, parked_low, listed, own, u1, u2, u3, d1, d2, d3,
    out, rows, x_high, x_low, w_high, w_low, arrived,
):
    copies = fetch((parked_high, parked_low), (w_high, w_low), arrived)
    ups, downs = (u1, u2, u3), (d1, d2, d3)
    z = z_ref[0]
    n = 4
    quarter, width = rows.shape[1:]
    both, feats = own.shape
    tokens = both // 2
    for k in range(n):
        column = pl.multiple_of(lax.rem(z - k + n, n) * feats, feats)
        for s in range(2):
            span = pl.ds(s * tokens, tokens)
            if k == 0:
                x = own[span]
            else:
                x = ups[k - 1][span] + downs[n - k - 1][span]
            for q in range(n):
                @pl.when(z == q)
                def _(x=x, q=q, s=s):
                    rows[s, :, pl.ds(column, feats)] = x[q * quarter : (q + 1) * quarter]
            high, low = halves(x)
            x_high[span, pl.ds(column, feats)] = high
            x_low[span, pl.ds(column, feats)] = low
    part = w_high.shape[0] // n
    for copy in copies:
        copy.wait()
    for h in range(n):
        at = slice(h * part, (h + 1) * part)
        r = mm_nt(w_high[at], x_high[...]) + mm_nt(w_low[at], x_high[...])
        r = r + mm_nt(w_high[at], x_low[...])
        for s in range(2):
            out[2 * h + s, :part] = r[:, s * tokens : (s + 1) * tokens]
            out[2 * h + s, part:] = listed[...]


def fold(x):
    top, bottom = x[: HD // 2], x[HD // 2 :]
    left = lax.broadcasted_iota(jnp.int32, top.shape, 1) < HD
    return jnp.where(left, top, pltpu.roll(bottom, HD, 1)), jnp.where(
        left, pltpu.roll(top, HD, 1), bottom
    )


def unfold(first, second):
    left = lax.broadcasted_iota(jnp.int32, first.shape, 1) < HD
    top = jnp.where(left, first, pltpu.roll(second, HD, 1))
    bottom = jnp.where(left, pltpu.roll(first, HD, 1), second)
    return jnp.concatenate([top, bottom], axis=0)


def attend_kernel(
    lists, session_row, qkv, mixed, folded, p_high, p_low, q3, k3, v2, session_col
):
    c = pl.program_id(0)

    @pl.when(c == 0)
    def _():
        columns = session_row[...].T
        for b in range(NBLOCKS):
            t = qkv[b // 2, : 3 * HD, (b % 2) * BLK : (b % 2 + 1) * BLK]
            q_high, q_low = halves(t[:HD] * SCALE)
            session_col[b] = columns[:, b : b + 1]
            q3[b] = jnp.concatenate([q_high, q_high, q_low], axis=0)
            k_high, k_low = halves(t[HD : 2 * HD].T)
            k3[b] = jnp.concatenate([k_high, k_low, k_high], axis=1)
            v_high, v_low = halves(t[2 * HD :])
            v2[b] = jnp.concatenate([v_high, v_low], axis=0)

    blocks = [GROUP * c + e for e in range(GROUP)]
    scores = []
    for b in blocks:
        mine = session_row[pl.ds(b, 1), :]
        tiles = []
        for j in range(KVB):
            other = lists[b, j]
            s = mm(k3[other], q3[b])
            tiles.append(jnp.where(session_col[other] == mine, s, -1e30))
        scores.append(jnp.concatenate(tiles, axis=0))
    tops = [jnp.max(s, axis=0, keepdims=True) for s in scores]
    expos = [jnp.exp(s - top) for s, top in zip(scores, tops)]
    scales = [1.0 / jnp.sum(expo, axis=0, keepdims=True) for expo in expos]
    for b, e, expo, each in zip(blocks, range(GROUP), expos, scales):
        high, low = halves(expo * each)
        p_high[e] = high
        p_low[e] = low
        values = jnp.concatenate([v2[lists[b, j]] for j in range(KVB)], axis=1)
        both = mm(values, high)
        block = both[:HD] + both[HD:] + mm(values[:HD], low)
        mixed[b] = block
        folded[2 * b], folded[2 * b + 1] = fold(block)


def attend_back_kernel(
    lists, qkv, p_high, p_low, grad, mixed, out0, out1, q2, k2, v3, acc
):
    out = (out0, out1)
    c = pl.program_id(0)

    @pl.when(c == 0)
    def _():
        for b in range(NBLOCKS):
            t = qkv[b // 2, : 3 * HD, (b % 2) * BLK : (b % 2 + 1) * BLK]
            q_high, q_low = halves(t[:HD])
            q2[b] = jnp.concatenate([q_high, q_low], axis=0)
            k_high, k_low = halves(t[HD : 2 * HD])
            k2[b] = jnp.concatenate([k_high, k_low], axis=0)
            v_high, v_low = halves(t[2 * HD :].T)
            v3[b] = jnp.concatenate([v_high, v_low, v_high], axis=1)
        acc[...] = jnp.zeros_like(acc)

    blocks = [GROUP * c + e for e in range(GROUP)]
    grads = [unfold(grad[2 * b], grad[2 * b + 1]) for b in blocks]
    parts = [halves(g) for g in grads]
    probs_grads = []
    for b, (g_high, g_low) in zip(blocks, parts):
        g3 = jnp.concatenate([g_high, g_high, g_low], axis=0)
        probs_grads.append(
            jnp.concatenate([mm(v3[lists[b, j]], g3) for j in range(KVB)], axis=0)
        )
    added = []
    for e, b in enumerate(blocks):
        delta = jnp.sum(grads[e] * mixed[b], axis=0, keepdims=True)
        g2 = jnp.concatenate(parts[e], axis=0)
        ph, pw = p_high[e], p_low[e]
        probs = ph.astype(F32) + pw.astype(F32)
        s_high, s_low = halves(probs * (probs_grads[e] - delta) * SCALE)
        keys = jnp.concatenate([k2[lists[b, j]] for j in range(KVB)], axis=1)
        both = mm(keys, s_high)
        out[e % 2][(GROUP // 2) * c + e // 2, 0:HD] = (
            both[:HD] + both[HD:] + mm(keys[:HD], s_low)
        )
        query = q2[b]
        both = mm_nt(query, s_high)
        grad_keys = both[:HD] + both[HD:] + mm_nt(query[:HD], s_low)
        both = mm_nt(g2, ph)
        grad_values = both[:HD] + both[HD:] + mm_nt(g2[:HD], pw)
        added.append(jnp.concatenate([grad_keys, grad_values], axis=0))
    for b, both in zip(blocks, added):
        for j in range(KVB):
            acc[lists[b, j]] += both[:, j * BLK : (j + 1) * BLK]

    @pl.when(c == NBLOCKS // GROUP - 1)
    def _():
        for b in range(NBLOCKS):
            out[b % 2][b // 2, HD : 3 * HD] = acc[b]


def split_kernel(whole, high, low):
    high[...], low[...] = halves(whole[...])


def norm_kernel(
    parked_high, parked_low, parked_rows, ups, pieces, out, direct_sum,
    upstream, mixed, w_high, w_low, rows, arrived,
):
    copies = fetch((parked_high, parked_low, parked_rows), (w_high, w_low, rows), arrived)
    n = 4
    quarter, width = direct_sum.shape
    feats = width // n
    for k in range(n):
        upstream[:, k * feats : (k + 1) * feats] = ups[k]
    for group in range(n):
        for h in range(n):
            at = group * feats + h * HD
            mixed[at : at + HD, :] = unfold(pieces[2 * h * n + group], pieces[(2 * h + 1) * n + group])
    m_high, m_low = halves(mixed[...].T)
    for copy in copies:
        copy.wait()
    projected = mm_nt(m_high, w_high[...]) + mm_nt(m_low, w_high[...]) + mm_nt(m_high, w_low[...])
    summed = rows[...].reshape(2 * quarter, width) + projected
    mean = jnp.sum(summed, axis=-1, keepdims=True) / width
    second = jnp.sum(summed * summed, axis=-1, keepdims=True) / width
    inverse = lax.rsqrt(second - mean * mean + EPS)
    normed = (summed - mean) * inverse
    up = jnp.concatenate([upstream[...], upstream[...]], axis=0)
    up_mean = jnp.sum(up, axis=-1, keepdims=True) / width
    up_dot = jnp.sum(up * normed, axis=-1, keepdims=True) / width
    direct = inverse * (up - up_mean - normed * up_dot)
    direct_sum[...] = direct[:quarter] + direct[quarter:]
    d_high, d_low = halves(direct)
    grad = mm(d_high, w_high[...]) + mm(d_low, w_high[...]) + mm(d_high, w_low[...])
    grad = grad.T
    for group in range(n):
        for h in range(n):
            at = group * feats + h * HD
            out[2 * h * n + group], out[(2 * h + 1) * n + group] = fold(grad[at : at + HD])


def input_kernel(
    half, z_ref, parked_high, parked_low, parked_sum, grads, f0, f1, f2, f3,
    weight_high, weight_low, direct_sum, arrived,
):
    copies = fetch(
        (parked_high, parked_low, parked_sum), (weight_high, weight_low, direct_sum), arrived
    )
    z = z_ref[0]
    n = 4
    quarter, width = direct_sum.shape
    feats = width // n
    g = jnp.concatenate([grads[2 * h] + grads[2 * h + 1] for h in range(n)], axis=0).T
    g_high, g_low = halves(g)
    mine = pl.ds(pl.multiple_of(lax.rem(z, 2) * quarter, quarter), quarter)
    here = z // 2 == half
    for copy in copies:
        copy.wait()
    for k, f in enumerate((f0, f1, f2, f3)):
        column = lax.rem(z + k, n) * feats
        at = pl.ds(pl.multiple_of(column, feats), feats)
        w_high, w_low = weight_high[:, at], weight_low[:, at]
        f[...] = mm(g_high, w_high) + mm(g_low, w_high) + mm(g_high, w_low)
        f[mine, :] += jnp.where(here, direct_sum[:, at], 0.0)


HD = 64
NBLOCKS = 16
GROUP = 4
SCALE = 1.0 / math.sqrt(HD)


def shape(dims, kind=F32):
    return jax.ShapeDtypeStruct(dims, kind)


def in_hbm(dims, kind=F32):
    return pltpu.HBM(dims, kind)


def shards(packets, baseline, w_query, w_key, w_value, w_out, gain, probe, sessions, block_lists):
    tokens, feats = packets.shape
    width = w_query.shape[1]
    n = lax.axis_size("head")
    heads = feats // HD
    members = lax.axis_size("ctx")
    quarter = tokens // n
    z = lax.axis_index("head")
    z_ref = z.reshape(1)
    slab = feats // members
    part = 3 * HD

    travel = packets - baseline
    half = tokens // 2
    own = jnp.concatenate([baseline + alpha * travel for alpha in ALPHAS])
    ups, downs = [own], [own]
    for step in range(1, n):
        ups.append(shift(ups[-1], 1, step - 1, n - 2))
        downs.append(shift(downs[-1], -1, 1, n - step))
    gathered = [own] + ups[1:] + downs[1:]

    slab_rows = lax.dynamic_slice_in_dim(w_out, lax.axis_index("ctx") * slab, slab, 0)
    gathered, slab_rows = lax.optimization_barrier((gathered, slab_rows))
    whole_out = lax.all_gather(slab_rows, ("head", "ctx"), axis=0, tiled=True)
    listed = block_lists.reshape(1, -1).astype(F32)
    listed = jnp.pad(listed, ((0, 7), (0, tokens - listed.shape[1])))
    high, low = call(
        weights_kernel, 16, (in_hbm((heads * part, width), BF16),) * 2, [], 0,
        w_query, w_key, w_value,
    )
    qkv, rows = call(
        project_kernel, 20,
        (in_hbm((members, part + 8, tokens)), in_hbm((2, quarter, width))),
        [pltpu.VMEM((2 * tokens, width), BF16)] * 2
        + [pltpu.VMEM((heads * part, width), BF16)] * 2
        + [pltpu.SemaphoreType.DMA((2,))],
        1, z_ref, high, low, listed, *gathered, parked=(1, 2),
    )
    qkv, probe = lax.optimization_barrier((qkv, probe))
    qkv = lax.all_to_all(qkv, "ctx", 0, 0, tiled=True)
    lists = qkv[:, part, : block_lists.size].astype(jnp.int32).reshape(-1, KVB)
    upstream = (probe * gain).reshape(n, quarter, feats)
    upstream = lax.all_to_all(upstream, "head", 0, 0, tiled=True)
    qkv, upstream = lax.optimization_barrier((qkv, upstream))

    out_high, out_low = call(
        split_kernel, 24, (in_hbm((width, width), BF16),) * 2, [], 0, whole_out
    )
    blocks = members * tokens // BLK
    everyone = members * n
    session_row = sessions.astype(F32).reshape(blocks, BLK)
    mixed, folded, p_high, p_low = call(
        attend_kernel, 20,
        (
            in_hbm((blocks, HD, BLK)),
            in_hbm((everyone, HD // 2, BLK)),
            in_hbm((blocks, KVB * BLK, BLK), BF16),
            in_hbm((blocks, KVB * BLK, BLK), BF16),
        ),
        [
            pltpu.VMEM((blocks, part, BLK), BF16),
            pltpu.VMEM((blocks, BLK, part), BF16),
            pltpu.VMEM((blocks, 2 * HD, BLK), BF16),
            pltpu.VMEM((blocks, BLK, 1), F32),
        ],
        1, lists, session_row, qkv, streamed_out=(2, 3),
    )
    folded = lax.all_to_all(folded, ("ctx", "head"), 0, 0, tiled=True)
    grad, direct_sum = call(
        norm_kernel, 20,
        (shape((everyone, HD // 2, BLK)), in_hbm((quarter, width))),
        [
            pltpu.VMEM((quarter, width), F32),
            pltpu.VMEM((width, 2 * quarter), F32),
            pltpu.VMEM((width, width), BF16),
            pltpu.VMEM((width, width), BF16),
            pltpu.VMEM((2, quarter, width), F32),
            pltpu.SemaphoreType.DMA((3,)),
        ],
        0, out_high, out_low, rows, upstream, folded, parked=(0, 1, 2),
    )
    grad = lax.all_to_all(grad, ("ctx", "head"), 0, 0, tiled=True)
    grad_qkv = call(
        attend_back_kernel, 20,
        (shape((members, part, half)),) * 2,
        [
            pltpu.VMEM((blocks, 2 * HD, BLK), BF16),
            pltpu.VMEM((blocks, 2 * HD, BLK), BF16),
            pltpu.VMEM((blocks, BLK, part), BF16),
            pltpu.VMEM((blocks, 2 * HD, BLK), F32),
        ],
        1, lists, qkv, p_high, p_low, grad, mixed, streamed_in=(2, 3),
    )
    grad_qkv = [lax.all_to_all(g, "ctx", 0, 0, tiled=True) for g in grad_qkv]
    totals = []
    for e in range(2):
        parts = exchange(
            call(
                functools.partial(input_kernel, e), 16,
                (shape((half, feats)),) * n,
                [pltpu.VMEM((heads * part, width), BF16)] * 2
                + [pltpu.VMEM((quarter, width), F32), pltpu.SemaphoreType.DMA((3,))],
                1, z_ref, high, low, direct_sum, grad_qkv[e], parked=(1, 2, 3),
            )
        )
        totals.append(parts[0] + parts[1] + parts[2] + parts[3])
    return travel * jnp.concatenate(totals) / len(ALPHAS)


def pick_shards(mesh):
    members, n = mesh.shape["ctx"], mesh.shape["head"]
    return shards if n == 4 and members == 2 * HEADS // n else general_shards


def solution(mesh):
    return jax.shard_map(
        pick_shards(mesh),
        mesh=mesh,
        in_specs=(
            P("ctx", "head"),
            P("ctx", "head"),
            P("head", None),
            P("head", None),
            P("head", None),
            P("head", None),
            P("head"),
            P("ctx", "head"),
            P(),
            P("ctx", None),
        ),
        out_specs=P("ctx", "head"),
        check_vma=False,
    )
```

```python
import functools
import math

import jax
import jax.numpy as jnp
from jax import lax
from jax.experimental import pallas as pl
from jax.experimental.pallas import tpu as pltpu
from jax.sharding import PartitionSpec as P

HEADS = 16
BLK = 128
KVB = 5
REACH = 2


ALPHAS = (0.25, 0.75)
EPS = 1e-05
HIGHEST = lax.Precision.HIGHEST


def from_behind(x, axis, by):
    size = lax.axis_size(axis)
    pairs = [(i, i + by) for i in range(size) if 0 <= i + by < size]
    return lax.ppermute(x, axis, pairs)


def integrate(points, weights_qkv, w_out, gain, probe, sessions, block_lists):
    steps, rows, feats = points.shape
    width = weights_qkv.shape[1]
    head_dim = width // HEADS
    local_heads = feats // head_dim
    blocks = rows // BLK
    where = lax.axis_index("ctx")
    first = (where - REACH) * blocks
    slots = (2 * REACH + 1) * blocks
    scale = 1.0 / math.sqrt(head_dim)
    part_cols = weights_qkv
    qkv = jnp.einsum(
        "std,ed->ste",
        lax.all_gather(points, "head", axis=2, tiled=True),
        part_cols,
        precision=HIGHEST,
    )
    query = qkv[:, :, :feats]
    pairs = qkv[:, :, feats:]
    below = []
    above = []
    for dist in range(1, REACH + 1):
        below.append(from_behind(pairs, "ctx", dist))
        above.append(from_behind(pairs, "ctx", -dist))
    window = jnp.concatenate(below[::-1] + [pairs] + above, axis=1)
    local = (block_lists - first).reshape(-1)
    tiles = window.reshape(steps, slots, BLK, 2 * feats)
    picked = jnp.take(tiles, local, axis=1).reshape(
        steps, blocks, KVB * BLK, 2, local_heads, head_dim
    )
    keys = picked[:, :, :, 0]
    values = picked[:, :, :, 1]
    token_index = block_lists[:, :, None] * BLK + jnp.arange(BLK, dtype=jnp.int32)[None, None, :]
    key_sessions = jnp.take(sessions, token_index.reshape(blocks, KVB * BLK), axis=0)
    query_sessions = lax.dynamic_slice_in_dim(sessions, where * rows, rows, 0).reshape(blocks, BLK)
    keep = query_sessions[:, :, None] == key_sessions[:, None, :]
    query_heads = query.reshape(steps, blocks, BLK, local_heads, head_dim)
    scores = jnp.einsum("sbqhd,sbkhd->sbhqk", query_heads, keys, precision=HIGHEST) * scale
    scores = jnp.where(keep[None, :, None], scores, -1e30)
    top = jnp.max(scores, axis=-1, keepdims=True)
    expo = jnp.exp(scores - top)
    probs = expo / jnp.sum(expo, axis=-1, keepdims=True)
    mixed = jnp.einsum("sbhqk,sbkhd->sbqhd", probs, values, precision=HIGHEST)
    heads_out = mixed.reshape(steps, rows, feats)
    part_cols = w_out
    projected = jnp.einsum(
        "std,ed->ste",
        lax.all_gather(heads_out, "head", axis=2, tiled=True),
        part_cols,
        precision=HIGHEST,
    )
    summed = points + projected
    first_sum, second_sum = lax.psum(
        (jnp.sum(summed, axis=-1), jnp.sum(summed * summed, axis=-1)), "head"
    )
    mean = first_sum / width
    inverse = lax.rsqrt(second_sum / width - mean * mean + EPS)
    normed = (summed - mean[..., None]) * inverse[..., None]
    upstream = probe * gain
    upstream_sum, upstream_dot = lax.psum(
        (jnp.sum(upstream, axis=-1), jnp.sum(upstream * normed, axis=-1)), "head"
    )
    direct = inverse[..., None] * (
        upstream - upstream_sum[..., None] / width - normed * (upstream_dot / width)[..., None]
    )
    partial_heads = jnp.einsum("ste,ed->std", direct, w_out, precision=HIGHEST)
    grad_heads = lax.psum_scatter(partial_heads, "head", scatter_dimension=2, tiled=True)
    grad_mixed = grad_heads.reshape(steps, blocks, BLK, local_heads, head_dim)
    delta = jnp.einsum("sbqhd,sbqhd->sbhq", grad_mixed, mixed, precision=HIGHEST)
    grad_probs = jnp.einsum("sbqhd,sbkhd->sbhqk", grad_mixed, values, precision=HIGHEST)
    grad_scores = probs * (grad_probs - delta[..., None]) * scale
    grad_query = jnp.einsum("sbhqk,sbkhd->sbqhd", grad_scores, keys, precision=HIGHEST)
    grad_keys = jnp.einsum("sbhqk,sbqhd->sbkhd", grad_scores, query_heads, precision=HIGHEST)
    grad_values = jnp.einsum("sbhqk,sbqhd->sbkhd", probs, grad_mixed, precision=HIGHEST)
    grad_picked = jnp.stack([grad_keys, grad_values], axis=3).reshape(
        steps, blocks * KVB, BLK, 2 * feats
    )
    selector = (local[:, None] == jnp.arange(slots, dtype=jnp.int32)[None, :]).astype(jnp.float32)
    grad_window = jnp.einsum("snlc,nw->swlc", grad_picked, selector, precision=HIGHEST).reshape(
        steps, slots * BLK, 2 * feats
    )
    owned = grad_window[:, REACH * rows : (REACH + 1) * rows]
    for dist in range(1, REACH + 1):
        upper = grad_window[:, (REACH + dist) * rows : (REACH + dist + 1) * rows]
        lower = grad_window[:, (REACH - dist) * rows : (REACH - dist + 1) * rows]
        owned = owned + from_behind(upper, "ctx", dist)
        owned = owned + from_behind(lower, "ctx", -dist)
    grad_qkv = jnp.concatenate([grad_query.reshape(steps, rows, feats), owned], axis=-1)
    partial_input = jnp.einsum("ste,ed->std", grad_qkv, weights_qkv, precision=HIGHEST)
    return (direct, partial_input)


def collect_inputs(partial_input):
    return lax.psum_scatter(partial_input, "head", scatter_dimension=2, tiled=True)


def general_shards(packets, baseline, w_query, w_key, w_value, w_out, gain, probe, sessions, block_lists):
    weights_qkv = jnp.concatenate([w_query, w_key, w_value], axis=0)
    travel = packets - baseline
    points = jnp.stack([baseline + alpha * travel for alpha in ALPHAS])
    passes = [
        integrate(points[index : index + 1], weights_qkv, w_out, gain, probe, sessions, block_lists)
        for index in range(len(ALPHAS))
    ]
    grads = jnp.zeros_like(packets)
    for direct, partial_input in passes:
        grads = grads + direct.sum(axis=0) + collect_inputs(partial_input).sum(axis=0)
    return travel * grads / len(ALPHAS)


F32 = jnp.float32
BF16 = jnp.bfloat16
MIB = 1 << 20
VM = pl.BlockSpec(memory_space=pltpu.VMEM)
SM = pl.BlockSpec(memory_space=pltpu.SMEM)


def halves(x):
    high = x.astype(BF16)
    low = (x - high.astype(F32)).astype(BF16)
    return high, low


def halves_outside(x):
    rounded = lax.reduce_precision(x, 8, 7)
    return rounded.astype(BF16), (x - rounded).astype(BF16)


def mm(a, b):
    return lax.dot_general(a, b, (((1,), (0,)), ((), ())), preferred_element_type=F32)


def mm_nt(a, b):
    return lax.dot_general(a, b, (((1,), (1,)), ((), ())), preferred_element_type=F32)


def call(kernel, mib, outs, scratch, n_smem, *args, streamed_in=(), streamed_out=(), parked=()):
    grid = (NBLOCKS // GROUP,) if streamed_in or streamed_out else ()
    one_in = pl.BlockSpec((GROUP, KVB * BLK, BLK), lambda c: (c, 0, 0))
    in_specs = [SM] * n_smem + [VM] * (len(args) - n_smem)
    for i in streamed_in:
        in_specs[i] = one_in
    for i in parked:
        in_specs[i] = pl.BlockSpec(memory_space=pl.ANY)
    args = [
        pltpu.with_memory_space_constraint(x, pltpu.HBM) if i in parked + streamed_in else x
        for i, x in enumerate(args)
    ]
    out_specs = jax.tree.map(lambda _: VM, outs)
    if streamed_out:
        out_specs = tuple(one_in if i in streamed_out else VM for i in range(len(outs)))
    return pl.pallas_call(
        kernel,
        out_shape=outs,
        grid=grid,
        in_specs=in_specs,
        out_specs=out_specs,
        scratch_shapes=scratch,
        compiler_params=pltpu.CompilerParams(vmem_limit_bytes=mib * MIB),
    )(*args)


def fetch(sources, places, arrived):
    copies = [
        pltpu.make_async_copy(source, place, arrived.at[i])
        for i, (source, place) in enumerate(zip(sources, places))
    ]
    for copy in copies:
        copy.start()
    return copies


def shift(x, by, low, high):
    return lax.ppermute(x, "head", [(i, i + by) for i in range(low, high + 1)])


def rotate(x, by):
    size = lax.axis_size("head")
    return lax.ppermute(x, "head", [(i, (i + by) % size) for i in range(size)])


def exchange(pieces):
    return [pieces[0]] + [rotate(pieces[k], k) for k in range(1, len(pieces))]


def weights_kernel(w_query, w_key, w_value, high, low):
    for h in range(w_query.shape[0] // HD):
        for i, w in enumerate((w_query, w_key, w_value)):
            at = slice((3 * h + i) * HD, (3 * h + i + 1) * HD)
            high[at], low[at] = halves(w[h * HD : (h + 1) * HD])


def project_kernel(
    z_ref, parked_high, parked_low, listed, own, u1, u2, u3, d1, d2, d3,
    out, rows, x3, w3, arrived,
):
    parts = [w3.at[:, i * rows.shape[2] : (i + 1) * rows.shape[2]] for i in range(3)]
    copies = fetch((parked_high, parked_low, parked_high), parts, arrived)
    ups, downs = (u1, u2, u3), (d1, d2, d3)
    z = z_ref[0]
    n = 4
    quarter, width = rows.shape[1:]
    both, feats = own.shape
    tokens = both // 2
    for k in range(n):
        column = pl.multiple_of(lax.rem(z - k + n, n) * feats, feats)
        for s in range(2):
            span = pl.ds(s * tokens, tokens)
            if k == 0:
                x = own[span]
            else:
                x = ups[k - 1][span] + downs[n - k - 1][span]
            for q in range(n):
                @pl.when(z == q)
                def _(x=x, q=q, s=s):
                    rows[s, :, pl.ds(column, feats)] = x[q * quarter : (q + 1) * quarter]
            high, low = halves(x)
            x3[span, pl.ds(column, feats)] = high
            x3[span, pl.ds(pl.multiple_of(width + column, feats), feats)] = high
            x3[span, pl.ds(pl.multiple_of(2 * width + column, feats), feats)] = low
    part = w3.shape[0] // n
    for copy in copies:
        copy.wait()
    for h in range(n):
        r = mm_nt(w3[h * part : (h + 1) * part, :], x3[...])
        for s in range(2):
            out[2 * h + s, :part] = r[:, s * tokens : (s + 1) * tokens]
            out[2 * h + s, part:] = listed[...]


def fold(x):
    top, bottom = x[: HD // 2], x[HD // 2 :]
    left = lax.broadcasted_iota(jnp.int32, top.shape, 1) < HD
    return jnp.where(left, top, pltpu.roll(bottom, HD, 1)), jnp.where(
        left, pltpu.roll(top, HD, 1), bottom
    )


def unfold(first, second):
    left = lax.broadcasted_iota(jnp.int32, first.shape, 1) < HD
    top = jnp.where(left, first, pltpu.roll(second, HD, 1))
    bottom = jnp.where(left, pltpu.roll(first, HD, 1), second)
    return jnp.concatenate([top, bottom], axis=0)


def attend_kernel(
    lists, session_row, qkv, mixed, folded, p_high, p_low, q3, k3, v2, session_col
):
    c = pl.program_id(0)

    @pl.when(c == 0)
    def _():
        columns = session_row[...].T
        for b in range(NBLOCKS):
            t = qkv[b // 2, : 3 * HD, (b % 2) * BLK : (b % 2 + 1) * BLK]
            q_high, q_low = halves(t[:HD] * SCALE)
            session_col[b] = columns[:, b : b + 1]
            q3[b] = jnp.concatenate([q_high, q_high, q_low], axis=0)
            k_high, k_low = halves(t[HD : 2 * HD].T)
            k3[b] = jnp.concatenate([k_high, k_low, k_high], axis=1)
            v_high, v_low = halves(t[2 * HD :])
            v2[b] = jnp.concatenate([v_high, v_low], axis=0)

    blocks = [GROUP * c + e for e in range(GROUP)]
    scores = []
    for b in blocks:
        mine = session_row[pl.ds(b, 1), :]
        tiles = []
        for j in range(KVB):
            other = lists[b, j]
            s = mm(k3[other], q3[b])
            tiles.append(jnp.where(session_col[other] == mine, s, -1e30))
        scores.append(jnp.concatenate(tiles, axis=0))
    tops = [jnp.max(s, axis=0, keepdims=True) for s in scores]
    expos = [jnp.exp(s - top) for s, top in zip(scores, tops)]
    scales = [1.0 / jnp.sum(expo, axis=0, keepdims=True) for expo in expos]
    for b, e, expo, each in zip(blocks, range(GROUP), expos, scales):
        high, low = halves(expo * each)
        p_high[e] = high
        p_low[e] = low
        values = jnp.concatenate([v2[lists[b, j]] for j in range(KVB)], axis=1)
        both = mm(values, high)
        block = both[:HD] + both[HD:] + mm(values[:HD], low)
        mixed[b] = block
        folded[2 * b], folded[2 * b + 1] = fold(block)


def attend_back_kernel(
    lists, qkv, p_high, p_low, grad, mixed, out0, out1, q2, k2, v3, acc
):
    out = (out0, out1)
    c = pl.program_id(0)

    @pl.when(c == 0)
    def _():
        for b in range(NBLOCKS):
            t = qkv[b // 2, : 3 * HD, (b % 2) * BLK : (b % 2 + 1) * BLK]
            q_high, q_low = halves(t[:HD])
            q2[b] = jnp.concatenate([q_high, q_low], axis=0)
            k_high, k_low = halves(t[HD : 2 * HD])
            k2[b] = jnp.concatenate([k_high, k_low], axis=0)
            v_high, v_low = halves(t[2 * HD :].T)
            v3[b] = jnp.concatenate([v_high, v_low, v_high], axis=1)
        acc[...] = jnp.zeros_like(acc)

    blocks = [GROUP * c + e for e in range(GROUP)]
    grads = [unfold(grad[2 * b], grad[2 * b + 1]) for b in blocks]
    parts = [halves(g) for g in grads]
    probs_grads = []
    for b, (g_high, g_low) in zip(blocks, parts):
        g3 = jnp.concatenate([g_high, g_high, g_low], axis=0)
        probs_grads.append(
            jnp.concatenate([mm(v3[lists[b, j]], g3) for j in range(KVB)], axis=0)
        )
    added = []
    for e, b in enumerate(blocks):
        delta = jnp.sum(grads[e] * mixed[b], axis=0, keepdims=True)
        g2 = jnp.concatenate(parts[e], axis=0)
        ph, pw = p_high[e], p_low[e]
        probs = ph.astype(F32) + pw.astype(F32)
        s_high, s_low = halves(probs * (probs_grads[e] - delta) * SCALE)
        keys = jnp.concatenate([k2[lists[b, j]] for j in range(KVB)], axis=1)
        both = mm(keys, s_high)
        out[e % 2][(GROUP // 2) * c + e // 2, 0:HD] = (
            both[:HD] + both[HD:] + mm(keys[:HD], s_low)
        )
        query = q2[b]
        both = mm_nt(query, s_high)
        grad_keys = both[:HD] + both[HD:] + mm_nt(query[:HD], s_low)
        both = mm_nt(g2, ph)
        grad_values = both[:HD] + both[HD:] + mm_nt(g2[:HD], pw)
        added.append(jnp.concatenate([grad_keys, grad_values], axis=0))
    for b, both in zip(blocks, added):
        for j in range(KVB):
            acc[lists[b, j]] += both[:, j * BLK : (j + 1) * BLK]

    @pl.when(c == NBLOCKS // GROUP - 1)
    def _():
        for b in range(NBLOCKS):
            out[b % 2][b // 2, HD : 3 * HD] = acc[b]


def norm_kernel(
    parked_whole, parked_rows, ups, pieces, out, direct_sum,
    upstream, mixed, w_high, w_low, rows, whole, arrived,
):
    copies = fetch((parked_rows, parked_whole), (rows, whole), arrived)
    n = 4
    quarter, width = direct_sum.shape
    feats = width // n
    for k in range(n):
        upstream[:, k * feats : (k + 1) * feats] = ups[k]
    for group in range(n):
        for h in range(n):
            at = group * feats + h * HD
            mixed[at : at + HD, :] = unfold(pieces[2 * h * n + group], pieces[(2 * h + 1) * n + group])
    m_high, m_low = halves(mixed[...].T)
    for copy in copies:
        copy.wait()
    for group in range(n):
        at = slice(group * feats, (group + 1) * feats)
        w_high[at], w_low[at] = halves(whole[at])
    projected = mm_nt(m_high, w_high[...]) + mm_nt(m_low, w_high[...]) + mm_nt(m_high, w_low[...])
    summed = rows[...].reshape(2 * quarter, width) + projected
    mean = jnp.sum(summed, axis=-1, keepdims=True) / width
    second = jnp.sum(summed * summed, axis=-1, keepdims=True) / width
    inverse = lax.rsqrt(second - mean * mean + EPS)
    normed = (summed - mean) * inverse
    up = jnp.concatenate([upstream[...], upstream[...]], axis=0)
    up_mean = jnp.sum(up, axis=-1, keepdims=True) / width
    up_dot = jnp.sum(up * normed, axis=-1, keepdims=True) / width
    direct = inverse * (up - up_mean - normed * up_dot)
    direct_sum[...] = direct[:quarter] + direct[quarter:]
    d_high, d_low = halves(direct)
    grad = mm(d_high, w_high[...]) + mm(d_low, w_high[...]) + mm(d_high, w_low[...])
    grad = grad.T
    for group in range(n):
        for h in range(n):
            at = group * feats + h * HD
            out[2 * h * n + group], out[(2 * h + 1) * n + group] = fold(grad[at : at + HD])


def input_kernel(
    half, z_ref, parked_high, parked_low, parked_sum, grads, f0, f1, f2, f3,
    weight_high, weight_low, direct_sum, arrived,
):
    copies = fetch(
        (parked_high, parked_low, parked_sum), (weight_high, weight_low, direct_sum), arrived
    )
    z = z_ref[0]
    n = 4
    quarter, width = direct_sum.shape
    feats = width // n
    g = jnp.concatenate([grads[2 * h] + grads[2 * h + 1] for h in range(n)], axis=0).T
    g_high, g_low = halves(g)
    mine = pl.ds(pl.multiple_of(lax.rem(z, 2) * quarter, quarter), quarter)
    here = z // 2 == half
    for copy in copies:
        copy.wait()
    for k, f in enumerate((f0, f1, f2, f3)):
        column = lax.rem(z + k, n) * feats
        at = pl.ds(pl.multiple_of(column, feats), feats)
        w_high, w_low = weight_high[:, at], weight_low[:, at]
        f[...] = mm(g_high, w_high) + mm(g_low, w_high) + mm(g_high, w_low)
        f[mine, :] += jnp.where(here, direct_sum[:, at], 0.0)


HD = 64
NBLOCKS = 16
GROUP = 4
SCALE = 1.0 / math.sqrt(HD)


def shape(dims, kind=F32):
    return jax.ShapeDtypeStruct(dims, kind)


def in_hbm(dims, kind=F32):
    return pltpu.HBM(dims, kind)


def shards(packets, baseline, w_query, w_key, w_value, w_out, gain, probe, sessions, block_lists):
    tokens, feats = packets.shape
    width = w_query.shape[1]
    n = lax.axis_size("head")
    heads = feats // HD
    members = lax.axis_size("ctx")
    quarter = tokens // n
    z = lax.axis_index("head")
    z_ref = z.reshape(1)
    slab = feats // members
    part = 3 * HD

    travel = packets - baseline
    half = tokens // 2
    own = jnp.concatenate([baseline + alpha * travel for alpha in ALPHAS])
    ups, downs = [own], [own]
    high, low = call(
        weights_kernel, 16, (in_hbm((heads * part, width), BF16),) * 2, [], 0,
        w_query, w_key, w_value,
    )
    upstream = (probe * gain).reshape(n, quarter, feats)
    upstream = lax.all_to_all(upstream, "head", 0, 0, tiled=True)
    slab_rows = lax.dynamic_slice_in_dim(w_out, lax.axis_index("ctx") * slab, slab, 0)
    for step in range(1, n):
        ups.append(shift(ups[-1], 1, step - 1, n - 2))
        downs.append(shift(downs[-1], -1, 1, n - step))
        if step == 1:
            ups[-1], downs[-1], high, low = lax.optimization_barrier(
                (ups[-1], downs[-1], high, low)
            )
        if step == n - 2:
            ups[-1], downs[-1], slab_rows, upstream = lax.optimization_barrier(
                (ups[-1], downs[-1], slab_rows, upstream)
            )
    gathered = [own] + ups[1:] + downs[1:]

    whole_out = lax.all_gather(slab_rows, ("head", "ctx"), axis=0, tiled=True)
    listed = block_lists.reshape(1, -1).astype(F32)
    listed = jnp.pad(listed, ((0, 7), (0, tokens - listed.shape[1])))
    qkv, rows = call(
        project_kernel, 20,
        (in_hbm((members, part + 8, tokens)), in_hbm((2, quarter, width))),
        [
            pltpu.VMEM((2 * tokens, 3 * width), BF16),
            pltpu.VMEM((heads * part, 3 * width), BF16),
            pltpu.SemaphoreType.DMA((3,)),
        ],
        1, z_ref, high, low, listed, *gathered, parked=(1, 2),
    )
    qkv = lax.all_to_all(qkv, "ctx", 0, 0, tiled=True)
    lists = qkv[:, part, : block_lists.size].astype(jnp.int32).reshape(-1, KVB)

    blocks = members * tokens // BLK
    everyone = members * n
    session_row = sessions.astype(F32).reshape(blocks, BLK)
    mixed, folded, p_high, p_low = call(
        attend_kernel, 20,
        (
            in_hbm((blocks, HD, BLK)),
            in_hbm((everyone, HD // 2, BLK)),
            in_hbm((blocks, KVB * BLK, BLK), BF16),
            in_hbm((blocks, KVB * BLK, BLK), BF16),
        ),
        [
            pltpu.VMEM((blocks, part, BLK), BF16),
            pltpu.VMEM((blocks, BLK, part), BF16),
            pltpu.VMEM((blocks, 2 * HD, BLK), BF16),
            pltpu.VMEM((blocks, BLK, 1), F32),
        ],
        1, lists, session_row, qkv, streamed_out=(2, 3),
    )
    folded = lax.all_to_all(folded, ("ctx", "head"), 0, 0, tiled=True)
    grad, direct_sum = call(
        norm_kernel, 24,
        (shape((everyone, HD // 2, BLK)), in_hbm((quarter, width))),
        [
            pltpu.VMEM((quarter, width), F32),
            pltpu.VMEM((width, 2 * quarter), F32),
            pltpu.VMEM((width, width), BF16),
            pltpu.VMEM((width, width), BF16),
            pltpu.VMEM((2, quarter, width), F32),
            pltpu.VMEM((width, width), F32),
            pltpu.SemaphoreType.DMA((2,)),
        ],
        0, whole_out, rows, upstream, folded, parked=(0, 1),
    )
    grad = lax.all_to_all(grad, ("ctx", "head"), 0, 0, tiled=True)
    grad_qkv = call(
        attend_back_kernel, 20,
        (shape((members, part, half)),) * 2,
        [
            pltpu.VMEM((blocks, 2 * HD, BLK), BF16),
            pltpu.VMEM((blocks, 2 * HD, BLK), BF16),
            pltpu.VMEM((blocks, BLK, part), BF16),
            pltpu.VMEM((blocks, 2 * HD, BLK), F32),
        ],
        1, lists, qkv, p_high, p_low, grad, mixed, streamed_in=(2, 3),
    )
    grad_qkv = [lax.all_to_all(g, "ctx", 0, 0, tiled=True) for g in grad_qkv]
    totals = []
    for e in range(2):
        parts = exchange(
            call(
                functools.partial(input_kernel, e), 16,
                (shape((half, feats)),) * n,
                [pltpu.VMEM((heads * part, width), BF16)] * 2
                + [pltpu.VMEM((quarter, width), F32), pltpu.SemaphoreType.DMA((3,))],
                1, z_ref, high, low, direct_sum, grad_qkv[e], parked=(1, 2, 3),
            )
        )
        totals.append(parts[0] + parts[1] + parts[2] + parts[3])
    return travel * jnp.concatenate(totals) / len(ALPHAS)


def pick_shards(mesh):
    members, n = mesh.shape["ctx"], mesh.shape["head"]
    return shards if n == 4 and members == 2 * HEADS // n else general_shards


def solution(mesh):
    return jax.shard_map(
        pick_shards(mesh),
        mesh=mesh,
        in_specs=(
            P("ctx", "head"),
            P("ctx", "head"),
            P("head", None),
            P("head", None),
            P("head", None),
            P("head", None),
            P("head"),
            P("ctx", "head"),
            P(),
            P("ctx", None),
        ),
        out_specs=P("ctx", "head"),
        check_vma=False,
    )
```

```python
import functools
import math

import jax
import jax.numpy as jnp
from jax import lax
from jax.experimental import pallas as pl
from jax.experimental.pallas import tpu as pltpu
from jax.sharding import PartitionSpec as P

HEADS = 16
BLK = 128
KVB = 5
REACH = 2


ALPHAS = (0.25, 0.75)
EPS = 1e-05
HIGHEST = lax.Precision.HIGHEST


def from_behind(x, axis, by):
    size = lax.axis_size(axis)
    pairs = [(i, i + by) for i in range(size) if 0 <= i + by < size]
    return lax.ppermute(x, axis, pairs)


def integrate(points, weights_qkv, w_out, gain, probe, sessions, block_lists):
    steps, rows, feats = points.shape
    width = weights_qkv.shape[1]
    head_dim = width // HEADS
    local_heads = feats // head_dim
    blocks = rows // BLK
    where = lax.axis_index("ctx")
    first = (where - REACH) * blocks
    slots = (2 * REACH + 1) * blocks
    scale = 1.0 / math.sqrt(head_dim)
    part_cols = weights_qkv
    qkv = jnp.einsum(
        "std,ed->ste",
        lax.all_gather(points, "head", axis=2, tiled=True),
        part_cols,
        precision=HIGHEST,
    )
    query = qkv[:, :, :feats]
    pairs = qkv[:, :, feats:]
    below = []
    above = []
    for dist in range(1, REACH + 1):
        below.append(from_behind(pairs, "ctx", dist))
        above.append(from_behind(pairs, "ctx", -dist))
    window = jnp.concatenate(below[::-1] + [pairs] + above, axis=1)
    local = (block_lists - first).reshape(-1)
    tiles = window.reshape(steps, slots, BLK, 2 * feats)
    picked = jnp.take(tiles, local, axis=1).reshape(
        steps, blocks, KVB * BLK, 2, local_heads, head_dim
    )
    keys = picked[:, :, :, 0]
    values = picked[:, :, :, 1]
    token_index = block_lists[:, :, None] * BLK + jnp.arange(BLK, dtype=jnp.int32)[None, None, :]
    key_sessions = jnp.take(sessions, token_index.reshape(blocks, KVB * BLK), axis=0)
    query_sessions = lax.dynamic_slice_in_dim(sessions, where * rows, rows, 0).reshape(blocks, BLK)
    keep = query_sessions[:, :, None] == key_sessions[:, None, :]
    query_heads = query.reshape(steps, blocks, BLK, local_heads, head_dim)
    scores = jnp.einsum("sbqhd,sbkhd->sbhqk", query_heads, keys, precision=HIGHEST) * scale
    scores = jnp.where(keep[None, :, None], scores, -1e30)
    top = jnp.max(scores, axis=-1, keepdims=True)
    expo = jnp.exp(scores - top)
    probs = expo / jnp.sum(expo, axis=-1, keepdims=True)
    mixed = jnp.einsum("sbhqk,sbkhd->sbqhd", probs, values, precision=HIGHEST)
    heads_out = mixed.reshape(steps, rows, feats)
    part_cols = w_out
    projected = jnp.einsum(
        "std,ed->ste",
        lax.all_gather(heads_out, "head", axis=2, tiled=True),
        part_cols,
        precision=HIGHEST,
    )
    summed = points + projected
    first_sum, second_sum = lax.psum(
        (jnp.sum(summed, axis=-1), jnp.sum(summed * summed, axis=-1)), "head"
    )
    mean = first_sum / width
    inverse = lax.rsqrt(second_sum / width - mean * mean + EPS)
    normed = (summed - mean[..., None]) * inverse[..., None]
    upstream = probe * gain
    upstream_sum, upstream_dot = lax.psum(
        (jnp.sum(upstream, axis=-1), jnp.sum(upstream * normed, axis=-1)), "head"
    )
    direct = inverse[..., None] * (
        upstream - upstream_sum[..., None] / width - normed * (upstream_dot / width)[..., None]
    )
    partial_heads = jnp.einsum("ste,ed->std", direct, w_out, precision=HIGHEST)
    grad_heads = lax.psum_scatter(partial_heads, "head", scatter_dimension=2, tiled=True)
    grad_mixed = grad_heads.reshape(steps, blocks, BLK, local_heads, head_dim)
    delta = jnp.einsum("sbqhd,sbqhd->sbhq", grad_mixed, mixed, precision=HIGHEST)
    grad_probs = jnp.einsum("sbqhd,sbkhd->sbhqk", grad_mixed, values, precision=HIGHEST)
    grad_scores = probs * (grad_probs - delta[..., None]) * scale
    grad_query = jnp.einsum("sbhqk,sbkhd->sbqhd", grad_scores, keys, precision=HIGHEST)
    grad_keys = jnp.einsum("sbhqk,sbqhd->sbkhd", grad_scores, query_heads, precision=HIGHEST)
    grad_values = jnp.einsum("sbhqk,sbqhd->sbkhd", probs, grad_mixed, precision=HIGHEST)
    grad_picked = jnp.stack([grad_keys, grad_values], axis=3).reshape(
        steps, blocks * KVB, BLK, 2 * feats
    )
    selector = (local[:, None] == jnp.arange(slots, dtype=jnp.int32)[None, :]).astype(jnp.float32)
    grad_window = jnp.einsum("snlc,nw->swlc", grad_picked, selector, precision=HIGHEST).reshape(
        steps, slots * BLK, 2 * feats
    )
    owned = grad_window[:, REACH * rows : (REACH + 1) * rows]
    for dist in range(1, REACH + 1):
        upper = grad_window[:, (REACH + dist) * rows : (REACH + dist + 1) * rows]
        lower = grad_window[:, (REACH - dist) * rows : (REACH - dist + 1) * rows]
        owned = owned + from_behind(upper, "ctx", dist)
        owned = owned + from_behind(lower, "ctx", -dist)
    grad_qkv = jnp.concatenate([grad_query.reshape(steps, rows, feats), owned], axis=-1)
    partial_input = jnp.einsum("ste,ed->std", grad_qkv, weights_qkv, precision=HIGHEST)
    return (direct, partial_input)


def collect_inputs(partial_input):
    return lax.psum_scatter(partial_input, "head", scatter_dimension=2, tiled=True)


def general_shards(packets, baseline, w_query, w_key, w_value, w_out, gain, probe, sessions, block_lists):
    weights_qkv = jnp.concatenate([w_query, w_key, w_value], axis=0)
    travel = packets - baseline
    points = jnp.stack([baseline + alpha * travel for alpha in ALPHAS])
    passes = [
        integrate(points[index : index + 1], weights_qkv, w_out, gain, probe, sessions, block_lists)
        for index in range(len(ALPHAS))
    ]
    grads = jnp.zeros_like(packets)
    for direct, partial_input in passes:
        grads = grads + direct.sum(axis=0) + collect_inputs(partial_input).sum(axis=0)
    return travel * grads / len(ALPHAS)


F32 = jnp.float32
BF16 = jnp.bfloat16
MIB = 1 << 20
VM = pl.BlockSpec(memory_space=pltpu.VMEM)
SM = pl.BlockSpec(memory_space=pltpu.SMEM)


def halves(x):
    high = x.astype(BF16)
    low = (x - high.astype(F32)).astype(BF16)
    return high, low


def halves_outside(x):
    rounded = lax.reduce_precision(x, 8, 7)
    return rounded.astype(BF16), (x - rounded).astype(BF16)


def mm(a, b):
    return lax.dot_general(a, b, (((1,), (0,)), ((), ())), preferred_element_type=F32)


def mm_nt(a, b):
    return lax.dot_general(a, b, (((1,), (1,)), ((), ())), preferred_element_type=F32)


def call(kernel, mib, outs, scratch, n_smem, *args, streamed_in=(), streamed_out=(), parked=(), parked_out=False):
    grid = (NBLOCKS // GROUP,) if streamed_in or streamed_out else ()
    one_in = pl.BlockSpec((GROUP, KVB * BLK, BLK), lambda c: (c, 0, 0))
    in_specs = [SM] * n_smem + [VM] * (len(args) - n_smem)
    for i in streamed_in:
        in_specs[i] = one_in
    for i in parked:
        in_specs[i] = pl.BlockSpec(memory_space=pl.ANY)
    args = [
        pltpu.with_memory_space_constraint(x, pltpu.HBM) if i in parked else x
        for i, x in enumerate(args)
    ]
    out_specs = jax.tree.map(
        lambda _: pl.BlockSpec(memory_space=pl.ANY) if parked_out else VM, outs
    )
    if streamed_out:
        out_specs = tuple(one_in if i in streamed_out else VM for i in range(len(outs)))
    return pl.pallas_call(
        kernel,
        out_shape=outs,
        grid=grid,
        in_specs=in_specs,
        out_specs=out_specs,
        scratch_shapes=scratch,
        compiler_params=pltpu.CompilerParams(vmem_limit_bytes=mib * MIB),
    )(*args)


def fetch(sources, places, arrived):
    copies = [
        pltpu.make_async_copy(source, place, arrived.at[i])
        for i, (source, place) in enumerate(zip(sources, places))
    ]
    for copy in copies:
        copy.start()
    return copies


def shift(x, by, low, high):
    return lax.ppermute(x, "head", [(i, i + by) for i in range(low, high + 1)])


def rotate(x, by):
    size = lax.axis_size("head")
    return lax.ppermute(x, "head", [(i, (i + by) % size) for i in range(size)])


def exchange(pieces):
    return [pieces[0]] + [rotate(pieces[k], k) for k in range(1, len(pieces))]


def weights_kernel(w_query, w_key, w_value, high, low):
    for h in range(w_query.shape[0] // HD):
        for i, w in enumerate((w_query, w_key, w_value)):
            at = slice((3 * h + i) * HD, (3 * h + i + 1) * HD)
            high[at], low[at] = halves(w[h * HD : (h + 1) * HD])


def project_kernel(z_ref, w_high, w_low, own, u1, u2, d1, d2, out, rows, x_high, x_low):
    z = z_ref[0]
    n = 4
    quarter, width = rows.shape[1:]
    both, feats = own.shape
    tokens = both // 2
    for k, sources in enumerate(((own,), (u1,), (u2, d2), (d1,))):
        column = pl.multiple_of(lax.rem(z - k + n, n) * feats, feats)
        for s in range(2):
            span = pl.ds(s * tokens, tokens)
            mine = pl.ds(pl.multiple_of(s * tokens + z * quarter, quarter), quarter)
            x = sum(source[span] for source in sources)
            rows[s, :, pl.ds(column, feats)] = sum(source[mine] for source in sources)
            high, low = halves(x)
            x_high[span, pl.ds(column, feats)] = high
            x_low[span, pl.ds(column, feats)] = low
    part = out.shape[1]
    for h in range(n):
        at = slice(h * part, (h + 1) * part)
        r = mm_nt(w_high[at], x_high[...]) + mm_nt(w_low[at], x_high[...])
        r = r + mm_nt(w_high[at], x_low[...])
        for s in range(2):
            out[2 * h + s] = r[:, s * tokens : (s + 1) * tokens]


def project_last_kernel(
    z_ref, w_high, w_low, listed, u3, d3, first, first_rows,
    parked_out, parked_rows, out, rows, left,
):
    z = z_ref[0]
    n = 4
    quarter, width = rows.shape[1:]
    both, feats = u3.shape
    tokens = both // 2
    rows[...] = first_rows[...]
    columns, pieces = [], []
    for k, source in ((1, d3), (3, u3)):
        column = pl.multiple_of(lax.rem(z - k + n, n) * feats, feats)
        for s in range(2):
            mine = pl.ds(pl.multiple_of(s * tokens + z * quarter, quarter), quarter)
            rows[s, :, pl.ds(column, feats)] += source[mine]
        columns.append(pl.ds(column, feats))
        pieces.append(halves(source[...]))
    leaving = [pltpu.make_async_copy(rows, parked_rows, left.at[n])]
    leaving[0].start()
    part = first.shape[1]
    for h in range(n):
        at = slice(h * part, (h + 1) * part)
        r = 0.0
        for column, (high, low) in zip(columns, pieces):
            r = r + mm_nt(w_high[at, column], high) + mm_nt(w_low[at, column], high)
            r = r + mm_nt(w_high[at, column], low)
        for s in range(2):
            out[2 * h + s, :part] = first[2 * h + s] + r[:, s * tokens : (s + 1) * tokens]
            out[2 * h + s, part:] = listed[...]
        pair = pl.ds(2 * h, 2)
        leaving.append(pltpu.make_async_copy(out.at[pair], parked_out.at[pair], left.at[h]))
        leaving[-1].start()
    for copy in leaving:
        copy.wait()


def fold(x):
    top, bottom = x[: HD // 2], x[HD // 2 :]
    left = lax.broadcasted_iota(jnp.int32, top.shape, 1) < HD
    return jnp.where(left, top, pltpu.roll(bottom, HD, 1)), jnp.where(
        left, pltpu.roll(top, HD, 1), bottom
    )


def unfold(first, second):
    left = lax.broadcasted_iota(jnp.int32, first.shape, 1) < HD
    top = jnp.where(left, first, pltpu.roll(second, HD, 1))
    bottom = jnp.where(left, pltpu.roll(first, HD, 1), second)
    return jnp.concatenate([top, bottom], axis=0)


def attend_kernel(
    lists, session_row, qkv, mixed, folded, p_high, p_low, q3, k3, v2, session_col
):
    c = pl.program_id(0)

    @pl.when(c == 0)
    def _():
        columns = session_row[...].T
        for b in range(NBLOCKS):
            t = qkv[b // 2, : 3 * HD, (b % 2) * BLK : (b % 2 + 1) * BLK]
            q_high, q_low = halves(t[:HD] * SCALE)
            session_col[b] = columns[:, b : b + 1]
            q3[b] = jnp.concatenate([q_high, q_high, q_low], axis=0)
            k_high, k_low = halves(t[HD : 2 * HD].T)
            k3[b] = jnp.concatenate([k_high, k_low, k_high], axis=1)
            v_high, v_low = halves(t[2 * HD :])
            v2[b] = jnp.concatenate([v_high, v_low], axis=0)

    blocks = [GROUP * c + e for e in range(GROUP)]
    scores = []
    for b in blocks:
        mine = session_row[pl.ds(b, 1), :]
        tiles = []
        for j in range(KVB):
            other = lists[b, j]
            s = mm(k3[other], q3[b])
            tiles.append(jnp.where(session_col[other] == mine, s, -1e30))
        scores.append(jnp.concatenate(tiles, axis=0))
    tops = [jnp.max(s, axis=0, keepdims=True) for s in scores]
    expos = [jnp.exp(s - top) for s, top in zip(scores, tops)]
    scales = [1.0 / jnp.sum(expo, axis=0, keepdims=True) for expo in expos]
    for b, e, expo, each in zip(blocks, range(GROUP), expos, scales):
        high, low = halves(expo * each)
        p_high[e] = high
        p_low[e] = low
        values = jnp.concatenate([v2[lists[b, j]] for j in range(KVB)], axis=1)
        both = mm(values, high)
        block = both[:HD] + both[HD:] + mm(values[:HD], low)
        mixed[b] = block
        folded[2 * b], folded[2 * b + 1] = fold(block)


def attend_back_kernel(
    lists, qkv, p_high, p_low, grad, mixed, out0, out1, q2, k2, v3, acc
):
    out = (out0, out1)
    c = pl.program_id(0)

    @pl.when(c == 0)
    def _():
        for b in range(NBLOCKS):
            t = qkv[b // 2, : 3 * HD, (b % 2) * BLK : (b % 2 + 1) * BLK]
            q_high, q_low = halves(t[:HD])
            q2[b] = jnp.concatenate([q_high, q_low], axis=0)
            k_high, k_low = halves(t[HD : 2 * HD])
            k2[b] = jnp.concatenate([k_high, k_low], axis=0)
            v_high, v_low = halves(t[2 * HD :].T)
            v3[b] = jnp.concatenate([v_high, v_low, v_high], axis=1)
        acc[...] = jnp.zeros_like(acc)

    blocks = [GROUP * c + e for e in range(GROUP)]
    grads = [unfold(grad[2 * b], grad[2 * b + 1]) for b in blocks]
    parts = [halves(g) for g in grads]
    probs_grads = []
    for b, (g_high, g_low) in zip(blocks, parts):
        g3 = jnp.concatenate([g_high, g_high, g_low], axis=0)
        probs_grads.append(
            jnp.concatenate([mm(v3[lists[b, j]], g3) for j in range(KVB)], axis=0)
        )
    added = []
    for e, b in enumerate(blocks):
        delta = jnp.sum(grads[e] * mixed[b], axis=0, keepdims=True)
        g2 = jnp.concatenate(parts[e], axis=0)
        ph, pw = p_high[e], p_low[e]
        probs = ph.astype(F32) + pw.astype(F32)
        s_high, s_low = halves(probs * (probs_grads[e] - delta) * SCALE)
        keys = jnp.concatenate([k2[lists[b, j]] for j in range(KVB)], axis=1)
        both = mm(keys, s_high)
        out[e % 2][(GROUP // 2) * c + e // 2, 0:HD] = (
            both[:HD] + both[HD:] + mm(keys[:HD], s_low)
        )
        query = q2[b]
        both = mm_nt(query, s_high)
        grad_keys = both[:HD] + both[HD:] + mm_nt(query[:HD], s_low)
        both = mm_nt(g2, ph)
        grad_values = both[:HD] + both[HD:] + mm_nt(g2[:HD], pw)
        added.append(jnp.concatenate([grad_keys, grad_values], axis=0))
    for b, both in zip(blocks, added):
        for j in range(KVB):
            acc[lists[b, j]] += both[:, j * BLK : (j + 1) * BLK]

    @pl.when(c == NBLOCKS // GROUP - 1)
    def _():
        for b in range(NBLOCKS):
            out[b % 2][b // 2, HD : 3 * HD] = acc[b]


def norm_kernel(
    z_ref, parked_whole, parked_rows, u0, u1, u2, u3, pieces, out, direct_sum,
    upstream, mixed, w_high, w_low, rows, whole, arrived,
):
    copies = fetch((parked_rows, parked_whole), (rows, whole), arrived)
    n = 4
    quarter, width = direct_sum.shape
    feats = width // n
    for k, u in enumerate((u0, u1, u2, u3)):
        column = lax.rem(z_ref[0] - k + n, n) * feats
        upstream[:, pl.ds(pl.multiple_of(column, feats), feats)] = u[...]
    for group in range(n):
        for h in range(n):
            at = group * feats + h * HD
            mixed[at : at + HD, :] = unfold(pieces[2 * h * n + group], pieces[(2 * h + 1) * n + group])
    m_high, m_low = halves(mixed[...].T)
    for copy in copies:
        copy.wait()
    for group in range(n):
        at = slice(group * feats, (group + 1) * feats)
        w_high[at], w_low[at] = halves(whole[at])
    projected = mm_nt(m_high, w_high[...]) + mm_nt(m_low, w_high[...]) + mm_nt(m_high, w_low[...])
    summed = rows[...].reshape(2 * quarter, width) + projected
    mean = jnp.sum(summed, axis=-1, keepdims=True) / width
    second = jnp.sum(summed * summed, axis=-1, keepdims=True) / width
    inverse = lax.rsqrt(second - mean * mean + EPS)
    normed = (summed - mean) * inverse
    up = jnp.concatenate([upstream[...], upstream[...]], axis=0)
    up_mean = jnp.sum(up, axis=-1, keepdims=True) / width
    up_dot = jnp.sum(up * normed, axis=-1, keepdims=True) / width
    direct = inverse * (up - up_mean - normed * up_dot)
    direct_sum[...] = direct[:quarter] + direct[quarter:]
    d_high, d_low = halves(direct)
    grad = mm(d_high, w_high[...]) + mm(d_low, w_high[...]) + mm(d_high, w_low[...])
    grad = grad.T
    for group in range(n):
        for h in range(n):
            at = group * feats + h * HD
            out[2 * h * n + group], out[(2 * h + 1) * n + group] = fold(grad[at : at + HD])


def input_kernel(
    half, z_ref, parked_high, parked_low, parked_sum, grads, f0, f1, f2, f3,
    weight_high, weight_low, direct_sum, arrived,
):
    copies = fetch(
        (parked_high, parked_low, parked_sum), (weight_high, weight_low, direct_sum), arrived
    )
    z = z_ref[0]
    n = 4
    quarter, width = direct_sum.shape
    feats = width // n
    g = jnp.concatenate([grads[2 * h] + grads[2 * h + 1] for h in range(n)], axis=0).T
    g_high, g_low = halves(g)
    mine = pl.ds(pl.multiple_of(lax.rem(z, 2) * quarter, quarter), quarter)
    here = z // 2 == half
    for copy in copies:
        copy.wait()
    for k, f in enumerate((f0, f1, f2, f3)):
        column = lax.rem(z + k, n) * feats
        at = pl.ds(pl.multiple_of(column, feats), feats)
        w_high, w_low = weight_high[:, at], weight_low[:, at]
        f[...] = mm(g_high, w_high) + mm(g_low, w_high) + mm(g_high, w_low)
        f[mine, :] += jnp.where(here, direct_sum[:, at], 0.0)


HD = 64
NBLOCKS = 16
GROUP = 4
SCALE = 1.0 / math.sqrt(HD)


def shape(dims, kind=F32):
    return jax.ShapeDtypeStruct(dims, kind)


def in_hbm(dims, kind=F32):
    return pltpu.HBM(dims, kind)


def shards(packets, baseline, w_query, w_key, w_value, w_out, gain, probe, sessions, block_lists):
    tokens, feats = packets.shape
    width = w_query.shape[1]
    n = lax.axis_size("head")
    heads = feats // HD
    members = lax.axis_size("ctx")
    quarter = tokens // n
    z = lax.axis_index("head")
    z_ref = z.reshape(1)
    slab = feats // members
    part = 3 * HD

    travel = packets - baseline
    half = tokens // 2
    own = jnp.concatenate([baseline + alpha * travel for alpha in ALPHAS])
    ups, downs = [own], [own]
    high, low = call(
        weights_kernel, 16, (in_hbm((heads * part, width), BF16),) * 2, [], 0,
        w_query, w_key, w_value,
    )
    slab_rows = lax.dynamic_slice_in_dim(w_out, lax.axis_index("ctx") * slab, slab, 0)
    for step in range(1, n):
        ups.append(shift(ups[-1], 1, step - 1, n - 2))
        downs.append(shift(downs[-1], -1, 1, n - step))
        if step == 1:
            ups[-1], downs[-1], high, low = lax.optimization_barrier(
                (ups[-1], downs[-1], high, low)
            )
        if step == n - 2:
            ups[-1], downs[-1], slab_rows = lax.optimization_barrier(
                (ups[-1], downs[-1], slab_rows)
            )

    whole_out = lax.all_gather(slab_rows, ("head", "ctx"), axis=0, tiled=True)
    listed = block_lists.reshape(1, -1).astype(F32)
    listed = jnp.pad(listed, ((0, 7), (0, tokens - listed.shape[1])))
    first, first_rows = call(
        project_kernel, 20,
        (shape((members, part, tokens)), shape((2, quarter, width))),
        [pltpu.VMEM((2 * tokens, width), BF16)] * 2,
        1, z_ref, high, low, own, ups[1], ups[2], downs[1], downs[2],
    )
    qkv, rows = call(
        project_last_kernel, 20,
        (in_hbm((members, part + 8, tokens)), in_hbm((2, quarter, width))),
        [
            pltpu.VMEM((members, part + 8, tokens), F32),
            pltpu.VMEM((2, quarter, width), F32),
            pltpu.SemaphoreType.DMA((n + 1,)),
        ],
        1, z_ref, high, low, listed, ups[3], downs[3], first, first_rows, parked_out=True,
    )
    qkv, probe = lax.optimization_barrier((qkv, probe))
    qkv = lax.all_to_all(qkv, "ctx", 0, 0, tiled=True)
    upstream = probe * gain
    upstream = exchange(
        [
            lax.dynamic_slice_in_dim(upstream, lax.rem(z + k, n) * quarter, quarter, 0)
            for k in range(n)
        ]
    )
    qkv, upstream = lax.optimization_barrier((qkv, upstream))
    lists = qkv[:, part, : block_lists.size].astype(jnp.int32).reshape(-1, KVB)

    blocks = members * tokens // BLK
    everyone = members * n
    session_row = sessions.astype(F32).reshape(blocks, BLK)
    mixed, folded, p_high, p_low = call(
        attend_kernel, 20,
        (
            in_hbm((blocks, HD, BLK)),
            in_hbm((everyone, HD // 2, BLK)),
            in_hbm((blocks, KVB * BLK, BLK), BF16),
            in_hbm((blocks, KVB * BLK, BLK), BF16),
        ),
        [
            pltpu.VMEM((blocks, part, BLK), BF16),
            pltpu.VMEM((blocks, BLK, part), BF16),
            pltpu.VMEM((blocks, 2 * HD, BLK), BF16),
            pltpu.VMEM((blocks, BLK, 1), F32),
        ],
        1, lists, session_row, qkv, streamed_out=(2, 3),
    )
    folded = lax.all_to_all(folded, ("ctx", "head"), 0, 0, tiled=True)
    grad, direct_sum = call(
        norm_kernel, 24,
        (shape((everyone, HD // 2, BLK)), in_hbm((quarter, width))),
        [
            pltpu.VMEM((quarter, width), F32),
            pltpu.VMEM((width, 2 * quarter), F32),
            pltpu.VMEM((width, width), BF16),
            pltpu.VMEM((width, width), BF16),
            pltpu.VMEM((2, quarter, width), F32),
            pltpu.VMEM((width, width), F32),
            pltpu.SemaphoreType.DMA((2,)),
        ],
        1, z_ref, whole_out, rows, *upstream, folded, parked=(1, 2),
    )
    grad = lax.all_to_all(grad, ("ctx", "head"), 0, 0, tiled=True)
    grad_qkv = call(
        attend_back_kernel, 20,
        (shape((members, part, half)),) * 2,
        [
            pltpu.VMEM((blocks, 2 * HD, BLK), BF16),
            pltpu.VMEM((blocks, 2 * HD, BLK), BF16),
            pltpu.VMEM((blocks, BLK, part), BF16),
            pltpu.VMEM((blocks, 2 * HD, BLK), F32),
        ],
        1, lists, qkv, p_high, p_low, grad, mixed, streamed_in=(2, 3),
    )
    grad_qkv = [lax.all_to_all(g, "ctx", 0, 0, tiled=True) for g in grad_qkv]
    totals = []
    for e in range(2):
        parts = exchange(
            call(
                functools.partial(input_kernel, e), 16,
                (shape((half, feats)),) * n,
                [pltpu.VMEM((heads * part, width), BF16)] * 2
                + [pltpu.VMEM((quarter, width), F32), pltpu.SemaphoreType.DMA((3,))],
                1, z_ref, high, low, direct_sum, grad_qkv[e], parked=(1, 2, 3),
            )
        )
        totals.append(parts[0] + parts[1] + parts[2] + parts[3])
    return travel * jnp.concatenate(totals) / len(ALPHAS)


def pick_shards(mesh):
    members, n = mesh.shape["ctx"], mesh.shape["head"]
    return shards if n == 4 and members == 2 * HEADS // n else general_shards


def solution(mesh):
    return jax.shard_map(
        pick_shards(mesh),
        mesh=mesh,
        in_specs=(
            P("ctx", "head"),
            P("ctx", "head"),
            P("head", None),
            P("head", None),
            P("head", None),
            P("head", None),
            P("head"),
            P("ctx", "head"),
            P(),
            P("ctx", None),
        ),
        out_specs=P("ctx", "head"),
        check_vma=False,
    )
```

```python
import functools
import math

import jax
import jax.numpy as jnp
from jax import lax
from jax.experimental import pallas as pl
from jax.experimental.pallas import tpu as pltpu
from jax.sharding import PartitionSpec as P

HEADS = 16
BLK = 128
KVB = 5
REACH = 2


ALPHAS = (0.25, 0.75)
EPS = 1e-05
HIGHEST = lax.Precision.HIGHEST


def from_behind(x, axis, by):
    size = lax.axis_size(axis)
    pairs = [(i, i + by) for i in range(size) if 0 <= i + by < size]
    return lax.ppermute(x, axis, pairs)


def integrate(points, weights_qkv, w_out, gain, probe, sessions, block_lists):
    steps, rows, feats = points.shape
    width = weights_qkv.shape[1]
    head_dim = width // HEADS
    local_heads = feats // head_dim
    blocks = rows // BLK
    where = lax.axis_index("ctx")
    first = (where - REACH) * blocks
    slots = (2 * REACH + 1) * blocks
    scale = 1.0 / math.sqrt(head_dim)
    part_cols = weights_qkv
    qkv = jnp.einsum(
        "std,ed->ste",
        lax.all_gather(points, "head", axis=2, tiled=True),
        part_cols,
        precision=HIGHEST,
    )
    query = qkv[:, :, :feats]
    pairs = qkv[:, :, feats:]
    below = []
    above = []
    for dist in range(1, REACH + 1):
        below.append(from_behind(pairs, "ctx", dist))
        above.append(from_behind(pairs, "ctx", -dist))
    window = jnp.concatenate(below[::-1] + [pairs] + above, axis=1)
    local = (block_lists - first).reshape(-1)
    tiles = window.reshape(steps, slots, BLK, 2 * feats)
    picked = jnp.take(tiles, local, axis=1).reshape(
        steps, blocks, KVB * BLK, 2, local_heads, head_dim
    )
    keys = picked[:, :, :, 0]
    values = picked[:, :, :, 1]
    token_index = block_lists[:, :, None] * BLK + jnp.arange(BLK, dtype=jnp.int32)[None, None, :]
    key_sessions = jnp.take(sessions, token_index.reshape(blocks, KVB * BLK), axis=0)
    query_sessions = lax.dynamic_slice_in_dim(sessions, where * rows, rows, 0).reshape(blocks, BLK)
    keep = query_sessions[:, :, None] == key_sessions[:, None, :]
    query_heads = query.reshape(steps, blocks, BLK, local_heads, head_dim)
    scores = jnp.einsum("sbqhd,sbkhd->sbhqk", query_heads, keys, precision=HIGHEST) * scale
    scores = jnp.where(keep[None, :, None], scores, -1e30)
    top = jnp.max(scores, axis=-1, keepdims=True)
    expo = jnp.exp(scores - top)
    probs = expo / jnp.sum(expo, axis=-1, keepdims=True)
    mixed = jnp.einsum("sbhqk,sbkhd->sbqhd", probs, values, precision=HIGHEST)
    heads_out = mixed.reshape(steps, rows, feats)
    part_cols = w_out
    projected = jnp.einsum(
        "std,ed->ste",
        lax.all_gather(heads_out, "head", axis=2, tiled=True),
        part_cols,
        precision=HIGHEST,
    )
    summed = points + projected
    first_sum, second_sum = lax.psum(
        (jnp.sum(summed, axis=-1), jnp.sum(summed * summed, axis=-1)), "head"
    )
    mean = first_sum / width
    inverse = lax.rsqrt(second_sum / width - mean * mean + EPS)
    normed = (summed - mean[..., None]) * inverse[..., None]
    upstream = probe * gain
    upstream_sum, upstream_dot = lax.psum(
        (jnp.sum(upstream, axis=-1), jnp.sum(upstream * normed, axis=-1)), "head"
    )
    direct = inverse[..., None] * (
        upstream - upstream_sum[..., None] / width - normed * (upstream_dot / width)[..., None]
    )
    partial_heads = jnp.einsum("ste,ed->std", direct, w_out, precision=HIGHEST)
    grad_heads = lax.psum_scatter(partial_heads, "head", scatter_dimension=2, tiled=True)
    grad_mixed = grad_heads.reshape(steps, blocks, BLK, local_heads, head_dim)
    delta = jnp.einsum("sbqhd,sbqhd->sbhq", grad_mixed, mixed, precision=HIGHEST)
    grad_probs = jnp.einsum("sbqhd,sbkhd->sbhqk", grad_mixed, values, precision=HIGHEST)
    grad_scores = probs * (grad_probs - delta[..., None]) * scale
    grad_query = jnp.einsum("sbhqk,sbkhd->sbqhd", grad_scores, keys, precision=HIGHEST)
    grad_keys = jnp.einsum("sbhqk,sbqhd->sbkhd", grad_scores, query_heads, precision=HIGHEST)
    grad_values = jnp.einsum("sbhqk,sbqhd->sbkhd", probs, grad_mixed, precision=HIGHEST)
    grad_picked = jnp.stack([grad_keys, grad_values], axis=3).reshape(
        steps, blocks * KVB, BLK, 2 * feats
    )
    selector = (local[:, None] == jnp.arange(slots, dtype=jnp.int32)[None, :]).astype(jnp.float32)
    grad_window = jnp.einsum("snlc,nw->swlc", grad_picked, selector, precision=HIGHEST).reshape(
        steps, slots * BLK, 2 * feats
    )
    owned = grad_window[:, REACH * rows : (REACH + 1) * rows]
    for dist in range(1, REACH + 1):
        upper = grad_window[:, (REACH + dist) * rows : (REACH + dist + 1) * rows]
        lower = grad_window[:, (REACH - dist) * rows : (REACH - dist + 1) * rows]
        owned = owned + from_behind(upper, "ctx", dist)
        owned = owned + from_behind(lower, "ctx", -dist)
    grad_qkv = jnp.concatenate([grad_query.reshape(steps, rows, feats), owned], axis=-1)
    partial_input = jnp.einsum("ste,ed->std", grad_qkv, weights_qkv, precision=HIGHEST)
    return (direct, partial_input)


def collect_inputs(partial_input):
    return lax.psum_scatter(partial_input, "head", scatter_dimension=2, tiled=True)


def general_shards(packets, baseline, w_query, w_key, w_value, w_out, gain, probe, sessions, block_lists):
    weights_qkv = jnp.concatenate([w_query, w_key, w_value], axis=0)
    travel = packets - baseline
    points = jnp.stack([baseline + alpha * travel for alpha in ALPHAS])
    passes = [
        integrate(points[index : index + 1], weights_qkv, w_out, gain, probe, sessions, block_lists)
        for index in range(len(ALPHAS))
    ]
    grads = jnp.zeros_like(packets)
    for direct, partial_input in passes:
        grads = grads + direct.sum(axis=0) + collect_inputs(partial_input).sum(axis=0)
    return travel * grads / len(ALPHAS)


F32 = jnp.float32
BF16 = jnp.bfloat16
MIB = 1 << 20
VM = pl.BlockSpec(memory_space=pltpu.VMEM)
SM = pl.BlockSpec(memory_space=pltpu.SMEM)


def halves(x):
    high = x.astype(BF16)
    low = (x - high.astype(F32)).astype(BF16)
    return high, low


def halves_outside(x):
    rounded = lax.reduce_precision(x, 8, 7)
    return rounded.astype(BF16), (x - rounded).astype(BF16)


def mm(a, b):
    return lax.dot_general(a, b, (((1,), (0,)), ((), ())), preferred_element_type=F32)


def mm_nt(a, b):
    return lax.dot_general(a, b, (((1,), (1,)), ((), ())), preferred_element_type=F32)


def call(kernel, mib, outs, scratch, n_smem, *args, streamed_in=(), streamed_out=(), parked=(), parked_out=False):
    grid = (NBLOCKS // GROUP,) if streamed_in or streamed_out else ()
    one_in = pl.BlockSpec((GROUP, KVB * BLK, BLK), lambda c: (c, 0, 0))
    in_specs = [SM] * n_smem + [VM] * (len(args) - n_smem)
    for i in streamed_in:
        in_specs[i] = one_in
    for i in parked:
        in_specs[i] = pl.BlockSpec(memory_space=pl.ANY)
    args = [
        pltpu.with_memory_space_constraint(x, pltpu.HBM) if i in parked else x
        for i, x in enumerate(args)
    ]
    out_specs = jax.tree.map(
        lambda _: pl.BlockSpec(memory_space=pl.ANY) if parked_out else VM, outs
    )
    if streamed_out:
        out_specs = tuple(one_in if i in streamed_out else VM for i in range(len(outs)))
    return pl.pallas_call(
        kernel,
        out_shape=outs,
        grid=grid,
        in_specs=in_specs,
        out_specs=out_specs,
        scratch_shapes=scratch,
        compiler_params=pltpu.CompilerParams(vmem_limit_bytes=mib * MIB),
    )(*args)


def fetch(sources, places, arrived):
    copies = [
        pltpu.make_async_copy(source, place, arrived.at[i])
        for i, (source, place) in enumerate(zip(sources, places))
    ]
    for copy in copies:
        copy.start()
    return copies


def shift(x, by, low, high):
    return lax.ppermute(x, "head", [(i, i + by) for i in range(low, high + 1)])


def rotate(x, by):
    size = lax.axis_size("head")
    return lax.ppermute(x, "head", [(i, (i + by) % size) for i in range(size)])


def exchange(pieces):
    return [pieces[0]] + [rotate(pieces[k], k) for k in range(1, len(pieces))]


def weights_kernel(w_query, w_key, w_value, high, low):
    for h in range(w_query.shape[0] // HD):
        for i, w in enumerate((w_query, w_key, w_value)):
            at = slice((3 * h + i) * HD, (3 * h + i + 1) * HD)
            high[at], low[at] = halves(w[h * HD : (h + 1) * HD])


def project_kernel(z_ref, w_high, w_low, own, u1, u2, d1, d2, out, rows, x_high, x_low):
    z = z_ref[0]
    n = 4
    quarter, width = rows.shape[1:]
    both, feats = own.shape
    tokens = both // 2
    for k, sources in enumerate(((own,), (u1,), (u2, d2), (d1,))):
        column = pl.multiple_of(lax.rem(z - k + n, n) * feats, feats)
        for s in range(2):
            span = pl.ds(s * tokens, tokens)
            mine = pl.ds(pl.multiple_of(s * tokens + z * quarter, quarter), quarter)
            x = sum(source[span] for source in sources)
            rows[s, :, pl.ds(column, feats)] = sum(source[mine] for source in sources)
            high, low = halves(x)
            x_high[span, pl.ds(column, feats)] = high
            x_low[span, pl.ds(column, feats)] = low
    part = out.shape[1]
    for h in range(n):
        at = slice(h * part, (h + 1) * part)
        r = mm_nt(w_high[at], x_high[...]) + mm_nt(w_low[at], x_high[...])
        r = r + mm_nt(w_high[at], x_low[...])
        for s in range(2):
            out[2 * h + s] = r[:, s * tokens : (s + 1) * tokens]


def project_last_kernel(
    z_ref, w_high, w_low, listed, u3, d3, first, first_rows,
    parked_out, parked_rows, out, rows, left,
):
    z = z_ref[0]
    n = 4
    quarter, width = rows.shape[1:]
    both, feats = u3.shape
    tokens = both // 2
    rows[...] = first_rows[...]
    columns, pieces = [], []
    for k, source in ((1, d3), (3, u3)):
        column = pl.multiple_of(lax.rem(z - k + n, n) * feats, feats)
        for s in range(2):
            mine = pl.ds(pl.multiple_of(s * tokens + z * quarter, quarter), quarter)
            rows[s, :, pl.ds(column, feats)] += source[mine]
        columns.append(pl.ds(column, feats))
        pieces.append(halves(source[...]))
    leaving = [pltpu.make_async_copy(rows, parked_rows, left.at[n])]
    leaving[0].start()
    part = first.shape[1]
    for h in range(n):
        at = slice(h * part, (h + 1) * part)
        r = 0.0
        for column, (high, low) in zip(columns, pieces):
            r = r + mm_nt(w_high[at, column], high) + mm_nt(w_low[at, column], high)
            r = r + mm_nt(w_high[at, column], low)
        for s in range(2):
            out[2 * h + s, :part] = first[2 * h + s] + r[:, s * tokens : (s + 1) * tokens]
            out[2 * h + s, part:] = listed[...]
        pair = pl.ds(2 * h, 2)
        leaving.append(pltpu.make_async_copy(out.at[pair], parked_out.at[pair], left.at[h]))
        leaving[-1].start()
    for copy in leaving:
        copy.wait()


def fold(x):
    top, bottom = x[: HD // 2], x[HD // 2 :]
    left = lax.broadcasted_iota(jnp.int32, top.shape, 1) < HD
    return jnp.where(left, top, pltpu.roll(bottom, HD, 1)), jnp.where(
        left, pltpu.roll(top, HD, 1), bottom
    )


def unfold(first, second):
    left = lax.broadcasted_iota(jnp.int32, first.shape, 1) < HD
    top = jnp.where(left, first, pltpu.roll(second, HD, 1))
    bottom = jnp.where(left, pltpu.roll(first, HD, 1), second)
    return jnp.concatenate([top, bottom], axis=0)


def attend_kernel(
    lists, session_row, qkv, mixed, folded, p_high, p_low, q3, k3, v2, session_col
):
    c = pl.program_id(0)

    @pl.when(c == 0)
    def _():
        columns = session_row[...].T
        for b in range(NBLOCKS):
            t = qkv[b // 2, : 3 * HD, (b % 2) * BLK : (b % 2 + 1) * BLK]
            q_high, q_low = halves(t[:HD] * SCALE)
            session_col[b] = columns[:, b : b + 1]
            q3[b] = jnp.concatenate([q_high, q_high, q_low], axis=0)
            k_high, k_low = halves(t[HD : 2 * HD].T)
            k3[b] = jnp.concatenate([k_high, k_low, k_high], axis=1)
            v_high, v_low = halves(t[2 * HD :])
            v2[b] = jnp.concatenate([v_high, v_low], axis=0)

    blocks = [GROUP * c + e for e in range(GROUP)]
    scores = []
    for b in blocks:
        mine = session_row[pl.ds(b, 1), :]
        tiles = []
        for j in range(KVB):
            other = lists[b, j]
            s = mm(k3[other], q3[b])
            tiles.append(jnp.where(session_col[other] == mine, s, -1e30))
        scores.append(jnp.concatenate(tiles, axis=0))
    tops = [jnp.max(s, axis=0, keepdims=True) for s in scores]
    expos = [jnp.exp(s - top) for s, top in zip(scores, tops)]
    scales = [1.0 / jnp.sum(expo, axis=0, keepdims=True) for expo in expos]
    for b, e, expo, each in zip(blocks, range(GROUP), expos, scales):
        high, low = halves(expo * each)
        p_high[e] = high
        p_low[e] = low
        values = jnp.concatenate([v2[lists[b, j]] for j in range(KVB)], axis=1)
        both = mm(values, high)
        block = both[:HD] + both[HD:] + mm(values[:HD], low)
        mixed[b] = block
        folded[2 * b], folded[2 * b + 1] = fold(block)


def attend_back_kernel(
    lists, qkv, p_high, p_low, grad, mixed, out0, out1, q2, k2, v3, acc
):
    out = (out0, out1)
    c = pl.program_id(0)

    @pl.when(c == 0)
    def _():
        for b in range(NBLOCKS):
            t = qkv[b // 2, : 3 * HD, (b % 2) * BLK : (b % 2 + 1) * BLK]
            q_high, q_low = halves(t[:HD])
            q2[b] = jnp.concatenate([q_high, q_low], axis=0)
            k_high, k_low = halves(t[HD : 2 * HD])
            k2[b] = jnp.concatenate([k_high, k_low], axis=0)
            v_high, v_low = halves(t[2 * HD :].T)
            v3[b] = jnp.concatenate([v_high, v_low, v_high], axis=1)
        acc[...] = jnp.zeros_like(acc)

    blocks = [GROUP * c + e for e in range(GROUP)]
    grads = [unfold(grad[2 * b], grad[2 * b + 1]) for b in blocks]
    parts = [halves(g) for g in grads]
    probs_grads = []
    for b, (g_high, g_low) in zip(blocks, parts):
        g3 = jnp.concatenate([g_high, g_high, g_low], axis=0)
        probs_grads.append(
            jnp.concatenate([mm(v3[lists[b, j]], g3) for j in range(KVB)], axis=0)
        )
    added = []
    for e, b in enumerate(blocks):
        delta = jnp.sum(grads[e] * mixed[b], axis=0, keepdims=True)
        g2 = jnp.concatenate(parts[e], axis=0)
        ph, pw = p_high[e], p_low[e]
        probs = ph.astype(F32) + pw.astype(F32)
        s_high, s_low = halves(probs * (probs_grads[e] - delta) * SCALE)
        keys = jnp.concatenate([k2[lists[b, j]] for j in range(KVB)], axis=1)
        both = mm(keys, s_high)
        out[e % 2][(GROUP // 2) * c + e // 2, 0:HD] = (
            both[:HD] + both[HD:] + mm(keys[:HD], s_low)
        )
        query = q2[b]
        both = mm_nt(query, s_high)
        grad_keys = both[:HD] + both[HD:] + mm_nt(query[:HD], s_low)
        both = mm_nt(g2, ph)
        grad_values = both[:HD] + both[HD:] + mm_nt(g2[:HD], pw)
        added.append(jnp.concatenate([grad_keys, grad_values], axis=0))
    for b, both in zip(blocks, added):
        for j in range(KVB):
            acc[lists[b, j]] += both[:, j * BLK : (j + 1) * BLK]

    @pl.when(c == NBLOCKS // GROUP - 1)
    def _():
        for b in range(NBLOCKS):
            out[b % 2][b // 2, HD : 3 * HD] = acc[b]


def norm_kernel(
    z_ref, parked_whole, parked_rows, u0, u1, u2, u3, pieces, out, direct_sum,
    upstream, mixed, w_high, w_low, rows, whole, arrived,
):
    bands = [pl.ds(group * HD * 4, HD * 4) for group in range(4)]
    copies = fetch(
        [parked_whole.at[band] for band in bands] + [parked_rows],
        [whole.at[band] for band in bands] + [rows],
        arrived,
    )
    n = 4
    quarter, width = direct_sum.shape
    feats = width // n
    for k, u in enumerate((u0, u1, u2, u3)):
        column = lax.rem(z_ref[0] - k + n, n) * feats
        upstream[:, pl.ds(pl.multiple_of(column, feats), feats)] = u[...]
    for group in range(n):
        for h in range(n):
            at = group * feats + h * HD
            mixed[at : at + HD, :] = unfold(pieces[2 * h * n + group], pieces[(2 * h + 1) * n + group])
    m_high, m_low = halves(mixed[...].T)
    projected = []
    for group in range(n):
        at = slice(group * feats, (group + 1) * feats)
        copies[group].wait()
        high, low = halves(whole[at])
        w_high[at], w_low[at] = high, low
        projected.append(mm_nt(m_high, high) + mm_nt(m_low, high) + mm_nt(m_high, low))
    copies[n].wait()
    projected = jnp.concatenate(projected, axis=1)
    summed = rows[...].reshape(2 * quarter, width) + projected
    mean = jnp.sum(summed, axis=-1, keepdims=True) / width
    second = jnp.sum(summed * summed, axis=-1, keepdims=True) / width
    inverse = lax.rsqrt(second - mean * mean + EPS)
    normed = (summed - mean) * inverse
    up = jnp.concatenate([upstream[...], upstream[...]], axis=0)
    up_mean = jnp.sum(up, axis=-1, keepdims=True) / width
    up_dot = jnp.sum(up * normed, axis=-1, keepdims=True) / width
    direct = inverse * (up - up_mean - normed * up_dot)
    direct_sum[...] = direct[:quarter] + direct[quarter:]
    d_high, d_low = halves(direct)
    grad = mm(d_high, w_high[...]) + mm(d_low, w_high[...]) + mm(d_high, w_low[...])
    grad = grad.T
    for group in range(n):
        for h in range(n):
            at = group * feats + h * HD
            out[2 * h * n + group], out[(2 * h + 1) * n + group] = fold(grad[at : at + HD])


def input_kernel(
    half, z_ref, parked_high, parked_low, parked_sum, grads, f0, f1, f2, f3,
    weight_high, weight_low, direct_sum, arrived,
):
    copies = fetch(
        (parked_high, parked_low, parked_sum), (weight_high, weight_low, direct_sum), arrived
    )
    z = z_ref[0]
    n = 4
    quarter, width = direct_sum.shape
    feats = width // n
    g = jnp.concatenate([grads[2 * h] + grads[2 * h + 1] for h in range(n)], axis=0).T
    g_high, g_low = halves(g)
    mine = pl.ds(pl.multiple_of(lax.rem(z, 2) * quarter, quarter), quarter)
    here = z // 2 == half
    for copy in copies:
        copy.wait()
    for k, f in enumerate((f0, f1, f2, f3)):
        column = lax.rem(z + k, n) * feats
        at = pl.ds(pl.multiple_of(column, feats), feats)
        w_high, w_low = weight_high[:, at], weight_low[:, at]
        f[...] = mm(g_high, w_high) + mm(g_low, w_high) + mm(g_high, w_low)
        f[mine, :] += jnp.where(here, direct_sum[:, at], 0.0)


HD = 64
NBLOCKS = 16
GROUP = 4
SCALE = 1.0 / math.sqrt(HD)


def shape(dims, kind=F32):
    return jax.ShapeDtypeStruct(dims, kind)


def in_hbm(dims, kind=F32):
    return pltpu.HBM(dims, kind)


def shards(packets, baseline, w_query, w_key, w_value, w_out, gain, probe, sessions, block_lists):
    tokens, feats = packets.shape
    width = w_query.shape[1]
    n = lax.axis_size("head")
    heads = feats // HD
    members = lax.axis_size("ctx")
    quarter = tokens // n
    z = lax.axis_index("head")
    z_ref = z.reshape(1)
    slab = feats // members
    part = 3 * HD

    travel = packets - baseline
    half = tokens // 2
    own = jnp.concatenate([baseline + alpha * travel for alpha in ALPHAS])
    ups, downs = [own], [own]
    high, low = call(
        weights_kernel, 16, (in_hbm((heads * part, width), BF16),) * 2, [], 0,
        w_query, w_key, w_value,
    )
    slab_rows = lax.dynamic_slice_in_dim(w_out, lax.axis_index("ctx") * slab, slab, 0)
    for step in range(1, n):
        ups.append(shift(ups[-1], 1, step - 1, n - 2))
        downs.append(shift(downs[-1], -1, 1, n - step))
        if step == 1:
            ups[-1], downs[-1], high, low = lax.optimization_barrier(
                (ups[-1], downs[-1], high, low)
            )
        if step == n - 2:
            ups[-1], downs[-1], slab_rows = lax.optimization_barrier(
                (ups[-1], downs[-1], slab_rows)
            )

    whole_out = lax.all_gather(slab_rows, ("head", "ctx"), axis=0, tiled=True)
    listed = block_lists.reshape(1, -1).astype(F32)
    listed = jnp.pad(listed, ((0, 7), (0, tokens - listed.shape[1])))
    first, first_rows = call(
        project_kernel, 20,
        (shape((members, part, tokens)), shape((2, quarter, width))),
        [pltpu.VMEM((2 * tokens, width), BF16)] * 2,
        1, z_ref, high, low, own, ups[1], ups[2], downs[1], downs[2],
    )
    qkv, rows = call(
        project_last_kernel, 20,
        (in_hbm((members, part + 8, tokens)), in_hbm((2, quarter, width))),
        [
            pltpu.VMEM((members, part + 8, tokens), F32),
            pltpu.VMEM((2, quarter, width), F32),
            pltpu.SemaphoreType.DMA((n + 1,)),
        ],
        1, z_ref, high, low, listed, ups[3], downs[3], first, first_rows, parked_out=True,
    )
    qkv, probe = lax.optimization_barrier((qkv, probe))
    qkv = lax.all_to_all(qkv, "ctx", 0, 0, tiled=True)
    upstream = probe * gain
    upstream = exchange(
        [
            lax.dynamic_slice_in_dim(upstream, lax.rem(z + k, n) * quarter, quarter, 0)
            for k in range(n)
        ]
    )
    qkv, upstream = lax.optimization_barrier((qkv, upstream))
    lists = qkv[:, part, : block_lists.size].astype(jnp.int32).reshape(-1, KVB)

    blocks = members * tokens // BLK
    everyone = members * n
    session_row = sessions.astype(F32).reshape(blocks, BLK)
    mixed, folded, p_high, p_low = call(
        attend_kernel, 20,
        (
            in_hbm((blocks, HD, BLK)),
            in_hbm((everyone, HD // 2, BLK)),
            in_hbm((blocks, KVB * BLK, BLK), BF16),
            in_hbm((blocks, KVB * BLK, BLK), BF16),
        ),
        [
            pltpu.VMEM((blocks, part, BLK), BF16),
            pltpu.VMEM((blocks, BLK, part), BF16),
            pltpu.VMEM((blocks, 2 * HD, BLK), BF16),
            pltpu.VMEM((blocks, BLK, 1), F32),
        ],
        1, lists, session_row, qkv, streamed_out=(2, 3),
    )
    folded = lax.all_to_all(folded, ("ctx", "head"), 0, 0, tiled=True)
    grad, direct_sum = call(
        norm_kernel, 24,
        (shape((everyone, HD // 2, BLK)), in_hbm((quarter, width))),
        [
            pltpu.VMEM((quarter, width), F32),
            pltpu.VMEM((width, 2 * quarter), F32),
            pltpu.VMEM((width, width), BF16),
            pltpu.VMEM((width, width), BF16),
            pltpu.VMEM((2, quarter, width), F32),
            pltpu.VMEM((width, width), F32),
            pltpu.SemaphoreType.DMA((n + 1,)),
        ],
        1, z_ref, whole_out, rows, *upstream, folded, parked=(1, 2),
    )
    grad = lax.all_to_all(grad, ("ctx", "head"), 0, 0, tiled=True)
    grad_qkv = call(
        attend_back_kernel, 20,
        (shape((members, part, half)),) * 2,
        [
            pltpu.VMEM((blocks, 2 * HD, BLK), BF16),
            pltpu.VMEM((blocks, 2 * HD, BLK), BF16),
            pltpu.VMEM((blocks, BLK, part), BF16),
            pltpu.VMEM((blocks, 2 * HD, BLK), F32),
        ],
        1, lists, qkv, p_high, p_low, grad, mixed, streamed_in=(2, 3),
    )
    grad_qkv = [lax.all_to_all(g, "ctx", 0, 0, tiled=True) for g in grad_qkv]
    totals = []
    for e in range(2):
        parts = exchange(
            call(
                functools.partial(input_kernel, e), 16,
                (shape((half, feats)),) * n,
                [pltpu.VMEM((heads * part, width), BF16)] * 2
                + [pltpu.VMEM((quarter, width), F32), pltpu.SemaphoreType.DMA((3,))],
                1, z_ref, high, low, direct_sum, grad_qkv[e], parked=(1, 2, 3),
            )
        )
        totals.append(parts[0] + parts[1] + parts[2] + parts[3])
    return travel * jnp.concatenate(totals) / len(ALPHAS)


def pick_shards(mesh):
    members, n = mesh.shape["ctx"], mesh.shape["head"]
    return shards if n == 4 and members == 2 * HEADS // n else general_shards


def solution(mesh):
    return jax.shard_map(
        pick_shards(mesh),
        mesh=mesh,
        in_specs=(
            P("ctx", "head"),
            P("ctx", "head"),
            P("head", None),
            P("head", None),
            P("head", None),
            P("head", None),
            P("head"),
            P("ctx", "head"),
            P(),
            P("ctx", None),
        ),
        out_specs=P("ctx", "head"),
        check_vma=False,
    )
```

```python
import functools
import math

import jax
import jax.numpy as jnp
from jax import lax
from jax.experimental import pallas as pl
from jax.experimental.pallas import tpu as pltpu
from jax.sharding import PartitionSpec as P

HEADS = 16
BLK = 128
KVB = 5
REACH = 2


ALPHAS = (0.25, 0.75)
EPS = 1e-05
HIGHEST = lax.Precision.HIGHEST


def from_behind(x, axis, by):
    size = lax.axis_size(axis)
    pairs = [(i, i + by) for i in range(size) if 0 <= i + by < size]
    return lax.ppermute(x, axis, pairs)


def integrate(points, weights_qkv, w_out, gain, probe, sessions, block_lists):
    steps, rows, feats = points.shape
    width = weights_qkv.shape[1]
    head_dim = width // HEADS
    local_heads = feats // head_dim
    blocks = rows // BLK
    where = lax.axis_index("ctx")
    first = (where - REACH) * blocks
    slots = (2 * REACH + 1) * blocks
    scale = 1.0 / math.sqrt(head_dim)
    part_cols = weights_qkv
    qkv = jnp.einsum(
        "std,ed->ste",
        lax.all_gather(points, "head", axis=2, tiled=True),
        part_cols,
        precision=HIGHEST,
    )
    query = qkv[:, :, :feats]
    pairs = qkv[:, :, feats:]
    below = []
    above = []
    for dist in range(1, REACH + 1):
        below.append(from_behind(pairs, "ctx", dist))
        above.append(from_behind(pairs, "ctx", -dist))
    window = jnp.concatenate(below[::-1] + [pairs] + above, axis=1)
    local = (block_lists - first).reshape(-1)
    tiles = window.reshape(steps, slots, BLK, 2 * feats)
    picked = jnp.take(tiles, local, axis=1).reshape(
        steps, blocks, KVB * BLK, 2, local_heads, head_dim
    )
    keys = picked[:, :, :, 0]
    values = picked[:, :, :, 1]
    token_index = block_lists[:, :, None] * BLK + jnp.arange(BLK, dtype=jnp.int32)[None, None, :]
    key_sessions = jnp.take(sessions, token_index.reshape(blocks, KVB * BLK), axis=0)
    query_sessions = lax.dynamic_slice_in_dim(sessions, where * rows, rows, 0).reshape(blocks, BLK)
    keep = query_sessions[:, :, None] == key_sessions[:, None, :]
    query_heads = query.reshape(steps, blocks, BLK, local_heads, head_dim)
    scores = jnp.einsum("sbqhd,sbkhd->sbhqk", query_heads, keys, precision=HIGHEST) * scale
    scores = jnp.where(keep[None, :, None], scores, -1e30)
    top = jnp.max(scores, axis=-1, keepdims=True)
    expo = jnp.exp(scores - top)
    probs = expo / jnp.sum(expo, axis=-1, keepdims=True)
    mixed = jnp.einsum("sbhqk,sbkhd->sbqhd", probs, values, precision=HIGHEST)
    heads_out = mixed.reshape(steps, rows, feats)
    part_cols = w_out
    projected = jnp.einsum(
        "std,ed->ste",
        lax.all_gather(heads_out, "head", axis=2, tiled=True),
        part_cols,
        precision=HIGHEST,
    )
    summed = points + projected
    first_sum, second_sum = lax.psum(
        (jnp.sum(summed, axis=-1), jnp.sum(summed * summed, axis=-1)), "head"
    )
    mean = first_sum / width
    inverse = lax.rsqrt(second_sum / width - mean * mean + EPS)
    normed = (summed - mean[..., None]) * inverse[..., None]
    upstream = probe * gain
    upstream_sum, upstream_dot = lax.psum(
        (jnp.sum(upstream, axis=-1), jnp.sum(upstream * normed, axis=-1)), "head"
    )
    direct = inverse[..., None] * (
        upstream - upstream_sum[..., None] / width - normed * (upstream_dot / width)[..., None]
    )
    partial_heads = jnp.einsum("ste,ed->std", direct, w_out, precision=HIGHEST)
    grad_heads = lax.psum_scatter(partial_heads, "head", scatter_dimension=2, tiled=True)
    grad_mixed = grad_heads.reshape(steps, blocks, BLK, local_heads, head_dim)
    delta = jnp.einsum("sbqhd,sbqhd->sbhq", grad_mixed, mixed, precision=HIGHEST)
    grad_probs = jnp.einsum("sbqhd,sbkhd->sbhqk", grad_mixed, values, precision=HIGHEST)
    grad_scores = probs * (grad_probs - delta[..., None]) * scale
    grad_query = jnp.einsum("sbhqk,sbkhd->sbqhd", grad_scores, keys, precision=HIGHEST)
    grad_keys = jnp.einsum("sbhqk,sbqhd->sbkhd", grad_scores, query_heads, precision=HIGHEST)
    grad_values = jnp.einsum("sbhqk,sbqhd->sbkhd", probs, grad_mixed, precision=HIGHEST)
    grad_picked = jnp.stack([grad_keys, grad_values], axis=3).reshape(
        steps, blocks * KVB, BLK, 2 * feats
    )
    selector = (local[:, None] == jnp.arange(slots, dtype=jnp.int32)[None, :]).astype(jnp.float32)
    grad_window = jnp.einsum("snlc,nw->swlc", grad_picked, selector, precision=HIGHEST).reshape(
        steps, slots * BLK, 2 * feats
    )
    owned = grad_window[:, REACH * rows : (REACH + 1) * rows]
    for dist in range(1, REACH + 1):
        upper = grad_window[:, (REACH + dist) * rows : (REACH + dist + 1) * rows]
        lower = grad_window[:, (REACH - dist) * rows : (REACH - dist + 1) * rows]
        owned = owned + from_behind(upper, "ctx", dist)
        owned = owned + from_behind(lower, "ctx", -dist)
    grad_qkv = jnp.concatenate([grad_query.reshape(steps, rows, feats), owned], axis=-1)
    partial_input = jnp.einsum("ste,ed->std", grad_qkv, weights_qkv, precision=HIGHEST)
    return (direct, partial_input)


def collect_inputs(partial_input):
    return lax.psum_scatter(partial_input, "head", scatter_dimension=2, tiled=True)


def general_shards(packets, baseline, w_query, w_key, w_value, w_out, gain, probe, sessions, block_lists):
    weights_qkv = jnp.concatenate([w_query, w_key, w_value], axis=0)
    travel = packets - baseline
    points = jnp.stack([baseline + alpha * travel for alpha in ALPHAS])
    passes = [
        integrate(points[index : index + 1], weights_qkv, w_out, gain, probe, sessions, block_lists)
        for index in range(len(ALPHAS))
    ]
    grads = jnp.zeros_like(packets)
    for direct, partial_input in passes:
        grads = grads + direct.sum(axis=0) + collect_inputs(partial_input).sum(axis=0)
    return travel * grads / len(ALPHAS)


F32 = jnp.float32
BF16 = jnp.bfloat16
MIB = 1 << 20
VM = pl.BlockSpec(memory_space=pltpu.VMEM)
SM = pl.BlockSpec(memory_space=pltpu.SMEM)


def halves(x):
    high = x.astype(BF16)
    low = (x - high.astype(F32)).astype(BF16)
    return high, low


def halves_outside(x):
    rounded = lax.reduce_precision(x, 8, 7)
    return rounded.astype(BF16), (x - rounded).astype(BF16)


def mm(a, b):
    return lax.dot_general(a, b, (((1,), (0,)), ((), ())), preferred_element_type=F32)


def mm_nt(a, b):
    return lax.dot_general(a, b, (((1,), (1,)), ((), ())), preferred_element_type=F32)


def call(kernel, mib, outs, scratch, n_smem, *args, streamed_in=(), streamed_out=(), parked=(), parked_out=False):
    grid = (NBLOCKS // GROUP,) if streamed_in or streamed_out else ()
    one_in = pl.BlockSpec((GROUP, KVB * BLK, BLK), lambda c: (c, 0, 0))
    in_specs = [SM] * n_smem + [VM] * (len(args) - n_smem)
    for i in streamed_in:
        in_specs[i] = one_in
    for i in parked:
        in_specs[i] = pl.BlockSpec(memory_space=pl.ANY)
    args = [
        pltpu.with_memory_space_constraint(x, pltpu.HBM) if i in parked else x
        for i, x in enumerate(args)
    ]
    out_specs = jax.tree.map(
        lambda _: pl.BlockSpec(memory_space=pl.ANY) if parked_out else VM, outs
    )
    if streamed_out:
        out_specs = tuple(one_in if i in streamed_out else VM for i in range(len(outs)))
    return pl.pallas_call(
        kernel,
        out_shape=outs,
        grid=grid,
        in_specs=in_specs,
        out_specs=out_specs,
        scratch_shapes=scratch,
        compiler_params=pltpu.CompilerParams(vmem_limit_bytes=mib * MIB),
    )(*args)


def fetch(sources, places, arrived):
    copies = [
        pltpu.make_async_copy(source, place, arrived.at[i])
        for i, (source, place) in enumerate(zip(sources, places))
    ]
    for copy in copies:
        copy.start()
    return copies


def shift(x, by, low, high):
    return lax.ppermute(x, "head", [(i, i + by) for i in range(low, high + 1)])


def rotate(x, by):
    size = lax.axis_size("head")
    return lax.ppermute(x, "head", [(i, (i + by) % size) for i in range(size)])


def exchange(pieces):
    return [pieces[0]] + [rotate(pieces[k], k) for k in range(1, len(pieces))]


def weights_kernel(w_query, w_key, w_value, high, low):
    for h in range(w_query.shape[0] // HD):
        for i, w in enumerate((w_query, w_key, w_value)):
            at = slice((3 * h + i) * HD, (3 * h + i + 1) * HD)
            high[at], low[at] = halves(w[h * HD : (h + 1) * HD])


def project_kernel(z_ref, w_high, w_low, own, u1, u2, d1, d2, out, rows, x_high, x_low):
    z = z_ref[0]
    n = 4
    quarter, width = rows.shape[1:]
    both, feats = own.shape
    tokens = both // 2
    for k, sources in enumerate(((own,), (u1,), (u2, d2), (d1,))):
        column = pl.multiple_of(lax.rem(z - k + n, n) * feats, feats)
        for s in range(2):
            span = pl.ds(s * tokens, tokens)
            mine = pl.ds(pl.multiple_of(s * tokens + z * quarter, quarter), quarter)
            x = sum(source[span] for source in sources)
            rows[s, :, pl.ds(column, feats)] = sum(source[mine] for source in sources)
            high, low = halves(x)
            x_high[span, pl.ds(column, feats)] = high
            x_low[span, pl.ds(column, feats)] = low
    part = out.shape[1]
    for h in range(n):
        at = slice(h * part, (h + 1) * part)
        r = mm_nt(w_high[at], x_high[...]) + mm_nt(w_low[at], x_high[...])
        r = r + mm_nt(w_high[at], x_low[...])
        for s in range(2):
            out[2 * h + s] = r[:, s * tokens : (s + 1) * tokens]


def project_last_kernel(
    z_ref, w_high, w_low, listed, u3, d3, first, first_rows,
    parked_out, parked_rows, out, rows, left,
):
    z = z_ref[0]
    n = 4
    quarter, width = rows.shape[1:]
    both, feats = u3.shape
    tokens = both // 2
    rows[...] = first_rows[...]
    columns, pieces = [], []
    for k, source in ((1, d3), (3, u3)):
        column = pl.multiple_of(lax.rem(z - k + n, n) * feats, feats)
        for s in range(2):
            mine = pl.ds(pl.multiple_of(s * tokens + z * quarter, quarter), quarter)
            rows[s, :, pl.ds(column, feats)] += source[mine]
        columns.append(pl.ds(column, feats))
        pieces.append(halves(source[...]))
    leaving = [pltpu.make_async_copy(rows, parked_rows, left.at[n])]
    leaving[0].start()
    part = first.shape[1]
    for h in range(n):
        at = slice(h * part, (h + 1) * part)
        r = 0.0
        for column, (high, low) in zip(columns, pieces):
            r = r + mm_nt(w_high[at, column], high) + mm_nt(w_low[at, column], high)
            r = r + mm_nt(w_high[at, column], low)
        for s in range(2):
            out[2 * h + s, :part] = first[2 * h + s] + r[:, s * tokens : (s + 1) * tokens]
            out[2 * h + s, part:] = listed[...]
        pair = pl.ds(2 * h, 2)
        leaving.append(pltpu.make_async_copy(out.at[pair], parked_out.at[pair], left.at[h]))
        leaving[-1].start()
    for copy in leaving:
        copy.wait()


def fold(x):
    top, bottom = x[: HD // 2], x[HD // 2 :]
    left = lax.broadcasted_iota(jnp.int32, top.shape, 1) < HD
    return jnp.where(left, top, pltpu.roll(bottom, HD, 1)), jnp.where(
        left, pltpu.roll(top, HD, 1), bottom
    )


def unfold(first, second):
    left = lax.broadcasted_iota(jnp.int32, first.shape, 1) < HD
    top = jnp.where(left, first, pltpu.roll(second, HD, 1))
    bottom = jnp.where(left, pltpu.roll(first, HD, 1), second)
    return jnp.concatenate([top, bottom], axis=0)


def attend_kernel(
    lists, session_row, qkv, mixed, folded, p_high, p_low, q3, k3, v2, session_col
):
    c = pl.program_id(0)

    @pl.when(c == 0)
    def _():
        columns = session_row[...].T
        for b in range(NBLOCKS):
            t = qkv[b // 2, : 3 * HD, (b % 2) * BLK : (b % 2 + 1) * BLK]
            q_high, q_low = halves(t[:HD] * SCALE)
            session_col[b] = columns[:, b : b + 1]
            q3[b] = jnp.concatenate([q_high, q_high, q_low], axis=0)
            k_high, k_low = halves(t[HD : 2 * HD].T)
            k3[b] = jnp.concatenate([k_high, k_low, k_high], axis=1)
            v_high, v_low = halves(t[2 * HD :])
            v2[b] = jnp.concatenate([v_high, v_low], axis=0)

    blocks = [GROUP * c + e for e in range(GROUP)]
    scores = []
    for b in blocks:
        mine = session_row[pl.ds(b, 1), :]
        tiles = []
        for j in range(KVB):
            other = lists[b, j]
            s = mm(k3[other], q3[b])
            tiles.append(jnp.where(session_col[other] == mine, s, -1e30))
        scores.append(jnp.concatenate(tiles, axis=0))
    tops = [jnp.max(s, axis=0, keepdims=True) for s in scores]
    expos = [jnp.exp(s - top) for s, top in zip(scores, tops)]
    scales = [1.0 / jnp.sum(expo, axis=0, keepdims=True) for expo in expos]
    for b, e, expo, each in zip(blocks, range(GROUP), expos, scales):
        high, low = halves(expo * each)
        p_high[e] = high
        p_low[e] = low
        values = jnp.concatenate([v2[lists[b, j]] for j in range(KVB)], axis=1)
        both = mm(values, high)
        block = both[:HD] + both[HD:] + mm(values[:HD], low)
        mixed[b] = block
        folded[2 * b], folded[2 * b + 1] = fold(block)


def attend_back_kernel(
    lists, qkv, p_high, p_low, grad, mixed, out0, out1, q2, k2, v3, acc
):
    out = (out0, out1)
    c = pl.program_id(0)

    @pl.when(c == 0)
    def _():
        for b in range(NBLOCKS):
            t = qkv[b // 2, : 3 * HD, (b % 2) * BLK : (b % 2 + 1) * BLK]
            q_high, q_low = halves(t[:HD])
            q2[b] = jnp.concatenate([q_high, q_low], axis=0)
            k_high, k_low = halves(t[HD : 2 * HD])
            k2[b] = jnp.concatenate([k_high, k_low], axis=0)
            v_high, v_low = halves(t[2 * HD :].T)
            v3[b] = jnp.concatenate([v_high, v_low, v_high], axis=1)
        acc[...] = jnp.zeros_like(acc)

    blocks = [GROUP * c + e for e in range(GROUP)]
    grads = [unfold(grad[2 * b], grad[2 * b + 1]) for b in blocks]
    parts = [halves(g) for g in grads]
    probs_grads = []
    for b, (g_high, g_low) in zip(blocks, parts):
        g3 = jnp.concatenate([g_high, g_high, g_low], axis=0)
        probs_grads.append(
            jnp.concatenate([mm(v3[lists[b, j]], g3) for j in range(KVB)], axis=0)
        )
    added = []
    for e, b in enumerate(blocks):
        delta = jnp.sum(grads[e] * mixed[b], axis=0, keepdims=True)
        g2 = jnp.concatenate(parts[e], axis=0)
        ph, pw = p_high[e], p_low[e]
        probs = ph.astype(F32) + pw.astype(F32)
        s_high, s_low = halves(probs * (probs_grads[e] - delta) * SCALE)
        keys = jnp.concatenate([k2[lists[b, j]] for j in range(KVB)], axis=1)
        both = mm(keys, s_high)
        out[e % 2][(GROUP // 2) * c + e // 2, 0:HD] = (
            both[:HD] + both[HD:] + mm(keys[:HD], s_low)
        )
        query = q2[b]
        both = mm_nt(query, s_high)
        grad_keys = both[:HD] + both[HD:] + mm_nt(query[:HD], s_low)
        both = mm_nt(g2, ph)
        grad_values = both[:HD] + both[HD:] + mm_nt(g2[:HD], pw)
        added.append(jnp.concatenate([grad_keys, grad_values], axis=0))
    for b, both in zip(blocks, added):
        for j in range(KVB):
            acc[lists[b, j]] += both[:, j * BLK : (j + 1) * BLK]

    @pl.when(c == NBLOCKS // GROUP - 1)
    def _():
        for b in range(NBLOCKS):
            out[b % 2][b // 2, HD : 3 * HD] = acc[b]


def norm_kernel(
    z_ref, parked_whole, parked_rows, u0, u1, u2, u3, pieces, out, direct_sum,
    upstream, mixed, w_high, w_low, rows, whole, arrived,
):
    copies = fetch((parked_rows, parked_whole), (rows, whole), arrived)
    n = 4
    quarter, width = direct_sum.shape
    feats = width // n
    for k, u in enumerate((u0, u1, u2, u3)):
        column = lax.rem(z_ref[0] - k + n, n) * feats
        upstream[:, pl.ds(pl.multiple_of(column, feats), feats)] = u[...]
    for group in range(n):
        for h in range(n):
            at = group * feats + h * HD
            mixed[at : at + HD, :] = unfold(pieces[2 * h * n + group], pieces[(2 * h + 1) * n + group])
    m_high, m_low = halves(mixed[...].T)
    for copy in copies:
        copy.wait()
    for group in range(n):
        at = slice(group * feats, (group + 1) * feats)
        w_high[at], w_low[at] = halves(whole[at])
    projected = mm_nt(m_high, w_high[...]) + mm_nt(m_low, w_high[...]) + mm_nt(m_high, w_low[...])
    summed = rows[...].reshape(2 * quarter, width) + projected
    mean = jnp.sum(summed, axis=-1, keepdims=True) / width
    second = jnp.sum(summed * summed, axis=-1, keepdims=True) / width
    inverse = lax.rsqrt(second - mean * mean + EPS)
    normed = (summed - mean) * inverse
    up = jnp.concatenate([upstream[...], upstream[...]], axis=0)
    up_mean = jnp.sum(up, axis=-1, keepdims=True) / width
    up_dot = jnp.sum(up * normed, axis=-1, keepdims=True) / width
    direct = inverse * (up - up_mean - normed * up_dot)
    direct_sum[...] = direct[:quarter] + direct[quarter:]
    d_high, d_low = halves(direct)
    grad = mm(d_high, w_high[...]) + mm(d_low, w_high[...]) + mm(d_high, w_low[...])
    grad = grad.T
    for group in range(n):
        for h in range(n):
            at = group * feats + h * HD
            out[2 * h * n + group], out[(2 * h + 1) * n + group] = fold(grad[at : at + HD])


def input_kernel(
    half, z_ref, parked_high, parked_low, parked_sum, grads, f0, f1, f2, f3,
    weight_high, weight_low, direct_sum, arrived,
):
    copies = fetch(
        (parked_high, parked_low, parked_sum), (weight_high, weight_low, direct_sum), arrived
    )
    z = z_ref[0]
    n = 4
    quarter, width = direct_sum.shape
    feats = width // n
    g = jnp.concatenate([grads[2 * h] + grads[2 * h + 1] for h in range(n)], axis=0).T
    g_high, g_low = halves(g)
    mine = pl.ds(pl.multiple_of(lax.rem(z, 2) * quarter, quarter), quarter)
    here = z // 2 == half
    for copy in copies:
        copy.wait()
    for k, f in enumerate((f0, f1, f2, f3)):
        column = lax.rem(z + k, n) * feats
        at = pl.ds(pl.multiple_of(column, feats), feats)
        w_high, w_low = weight_high[:, at], weight_low[:, at]
        f[...] = mm(g_high, w_high) + mm(g_low, w_high) + mm(g_high, w_low)
        f[mine, :] += jnp.where(here, direct_sum[:, at], 0.0)


HD = 64
NBLOCKS = 16
GROUP = 8
SCALE = 1.0 / math.sqrt(HD)


def shape(dims, kind=F32):
    return jax.ShapeDtypeStruct(dims, kind)


def in_hbm(dims, kind=F32):
    return pltpu.HBM(dims, kind)


def shards(packets, baseline, w_query, w_key, w_value, w_out, gain, probe, sessions, block_lists):
    tokens, feats = packets.shape
    width = w_query.shape[1]
    n = lax.axis_size("head")
    heads = feats // HD
    members = lax.axis_size("ctx")
    quarter = tokens // n
    z = lax.axis_index("head")
    z_ref = z.reshape(1)
    slab = feats // members
    part = 3 * HD

    travel = packets - baseline
    half = tokens // 2
    own = jnp.concatenate([baseline + alpha * travel for alpha in ALPHAS])
    ups, downs = [own], [own]
    high, low = call(
        weights_kernel, 16, (in_hbm((heads * part, width), BF16),) * 2, [], 0,
        w_query, w_key, w_value,
    )
    slab_rows = lax.dynamic_slice_in_dim(w_out, lax.axis_index("ctx") * slab, slab, 0)
    for step in range(1, n):
        ups.append(shift(ups[-1], 1, step - 1, n - 2))
        downs.append(shift(downs[-1], -1, 1, n - step))
        if step == 1:
            ups[-1], downs[-1], high, low = lax.optimization_barrier(
                (ups[-1], downs[-1], high, low)
            )
        if step == n - 2:
            ups[-1], downs[-1], slab_rows = lax.optimization_barrier(
                (ups[-1], downs[-1], slab_rows)
            )

    whole_out = lax.all_gather(slab_rows, ("head", "ctx"), axis=0, tiled=True)
    listed = block_lists.reshape(1, -1).astype(F32)
    listed = jnp.pad(listed, ((0, 7), (0, tokens - listed.shape[1])))
    first, first_rows = call(
        project_kernel, 20,
        (shape((members, part, tokens)), shape((2, quarter, width))),
        [pltpu.VMEM((2 * tokens, width), BF16)] * 2,
        1, z_ref, high, low, own, ups[1], ups[2], downs[1], downs[2],
    )
    qkv, rows = call(
        project_last_kernel, 20,
        (in_hbm((members, part + 8, tokens)), in_hbm((2, quarter, width))),
        [
            pltpu.VMEM((members, part + 8, tokens), F32),
            pltpu.VMEM((2, quarter, width), F32),
            pltpu.SemaphoreType.DMA((n + 1,)),
        ],
        1, z_ref, high, low, listed, ups[3], downs[3], first, first_rows, parked_out=True,
    )
    qkv, probe = lax.optimization_barrier((qkv, probe))
    qkv = lax.all_to_all(qkv, "ctx", 0, 0, tiled=True)
    upstream = probe * gain
    upstream = exchange(
        [
            lax.dynamic_slice_in_dim(upstream, lax.rem(z + k, n) * quarter, quarter, 0)
            for k in range(n)
        ]
    )
    qkv, upstream = lax.optimization_barrier((qkv, upstream))
    lists = qkv[:, part, : block_lists.size].astype(jnp.int32).reshape(-1, KVB)

    blocks = members * tokens // BLK
    everyone = members * n
    session_row = sessions.astype(F32).reshape(blocks, BLK)
    mixed, folded, p_high, p_low = call(
        attend_kernel, 20,
        (
            in_hbm((blocks, HD, BLK)),
            in_hbm((everyone, HD // 2, BLK)),
            in_hbm((blocks, KVB * BLK, BLK), BF16),
            in_hbm((blocks, KVB * BLK, BLK), BF16),
        ),
        [
            pltpu.VMEM((blocks, part, BLK), BF16),
            pltpu.VMEM((blocks, BLK, part), BF16),
            pltpu.VMEM((blocks, 2 * HD, BLK), BF16),
            pltpu.VMEM((blocks, BLK, 1), F32),
        ],
        1, lists, session_row, qkv, streamed_out=(2, 3),
    )
    folded = lax.all_to_all(folded, ("ctx", "head"), 0, 0, tiled=True)
    grad, direct_sum = call(
        norm_kernel, 24,
        (shape((everyone, HD // 2, BLK)), in_hbm((quarter, width))),
        [
            pltpu.VMEM((quarter, width), F32),
            pltpu.VMEM((width, 2 * quarter), F32),
            pltpu.VMEM((width, width), BF16),
            pltpu.VMEM((width, width), BF16),
            pltpu.VMEM((2, quarter, width), F32),
            pltpu.VMEM((width, width), F32),
            pltpu.SemaphoreType.DMA((2,)),
        ],
        1, z_ref, whole_out, rows, *upstream, folded, parked=(1, 2),
    )
    grad = lax.all_to_all(grad, ("ctx", "head"), 0, 0, tiled=True)
    grad_qkv = call(
        attend_back_kernel, 20,
        (shape((members, part, half)),) * 2,
        [
            pltpu.VMEM((blocks, 2 * HD, BLK), BF16),
            pltpu.VMEM((blocks, 2 * HD, BLK), BF16),
            pltpu.VMEM((blocks, BLK, part), BF16),
            pltpu.VMEM((blocks, 2 * HD, BLK), F32),
        ],
        1, lists, qkv, p_high, p_low, grad, mixed, streamed_in=(2, 3),
    )
    grad_qkv = [lax.all_to_all(g, "ctx", 0, 0, tiled=True) for g in grad_qkv]
    totals = []
    for e in range(2):
        parts = exchange(
            call(
                functools.partial(input_kernel, e), 16,
                (shape((half, feats)),) * n,
                [pltpu.VMEM((heads * part, width), BF16)] * 2
                + [pltpu.VMEM((quarter, width), F32), pltpu.SemaphoreType.DMA((3,))],
                1, z_ref, high, low, direct_sum, grad_qkv[e], parked=(1, 2, 3),
            )
        )
        totals.append(parts[0] + parts[1] + parts[2] + parts[3])
    return travel * jnp.concatenate(totals) / len(ALPHAS)


def pick_shards(mesh):
    members, n = mesh.shape["ctx"], mesh.shape["head"]
    return shards if n == 4 and members == 2 * HEADS // n else general_shards


def solution(mesh):
    return jax.shard_map(
        pick_shards(mesh),
        mesh=mesh,
        in_specs=(
            P("ctx", "head"),
            P("ctx", "head"),
            P("head", None),
            P("head", None),
            P("head", None),
            P("head", None),
            P("head"),
            P("ctx", "head"),
            P(),
            P("ctx", None),
        ),
        out_specs=P("ctx", "head"),
        check_vma=False,
    )
```
